128 devices in a mesh: dp: 4 (over z), index: 32 (over x, y, core).
Axes of the slice: x: 4, y: 4, z: 4, core: 2. Of those that a mesh axis runs over, the one named last changes fastest.
Arguments:
- query_codes: int32 [2048, 64], P(('dp', 'index')), may hold values from 0 to 65535, as said below
- positive_ids: int32 [2048], P(('dp', 'index')), may hold values from 0 to 65535
- negative_ids: int32 [2048, 16], P(('dp', 'index')), may hold values from 0 to 65535, as said below
- bank_codes: bfloat16 [65536, 1024], P('index'), may hold values from -1 to 1, as said below
- bank_emb: bfloat16 [65536, 1024], P('index'), may hold values from -0.1875 to 0.1875
- query_emb: bfloat16 [2048, 1024], P(('dp', 'index')), may hold values from -0.75 to 0.75
- positive_emb: bfloat16 [2048, 1024], P(('dp', 'index')), may hold values from -0.1875 to 0.1875
- head: bfloat16 [1024, 1024], replicated, may hold values from -0.1875 to 0.1875
Outputs:
- mined_ids: int32 [2048, 16], P(('dp', 'index'))
- mined_dist: int32 [2048, 16], P(('dp', 'index'))
- query_grad: bfloat16 [2048, 1024], P(('dp', 'index'))
- positive_grad: bfloat16 [2048, 1024], P(('dp', 'index'))
- head_grad: float32 [1024, 1024], P(('dp', 'index'))
The draws below stay inside these ranges and needn't reach their ends.
Inputs may be any that keep to these rules, and one draw needn't show every extreme that they name: `query_codes`: each word holds 16 independent code bits in its low 16 bits. `bank_codes`: every entry is +1 or -1. `negative_ids`: the owner of an id is id // 2048. Among the 256 ids of one device, one owner holds exactly 39 and every other owner exactly 7; that busiest owner is the same for all devices of one dp group.
All inputs are finite; a program needn't handle non-finite values.
Results may differ from the reference program's by a relative error of at most 0.015.
Values may be sent and summed in bfloat16 or wider, within the bound.
A program may use at most 128 MiB of HBM per device.

```python
import math
import jax
import jax.numpy as jnp
from jax import lax

D = 1024
BITS = 1024
WORDS = 64
TOPK = 16
NEG = 16
CANDS = 17
Q_DEV = 16
PASS_DEV = 2048
QUERIES = 2048
PASSAGES = 65536
N_INDEX = 32


def shared_codes(key):
    base = jax.random.fold_in(key, 7301)
    bit_key, plant_key, perm_key, rand_key, flip_key, order_key = jax.random.split(base, 6)
    query_bits = jax.random.randint(bit_key, (QUERIES, BITS), 0, 2, dtype=jnp.int32)
    planted = jax.random.randint(plant_key, (QUERIES,), 0, 4, dtype=jnp.int32) == 0
    picked_rows = jax.random.permutation(perm_key, PASSAGES)[:QUERIES].astype(jnp.int32)
    random_ids = jax.random.randint(rand_key, (QUERIES,), 0, PASSAGES, dtype=jnp.int32)
    query_index = jnp.arange(QUERIES, dtype=jnp.int32)
    random_ids = jnp.where(query_index == 1, 0, random_ids)
    random_ids = jnp.where(query_index == QUERIES - 1, PASSAGES - 1, random_ids)
    planted = jnp.logical_and(planted, jnp.logical_and(query_index != 1, query_index != QUERIES - 1))
    positive_ids = jnp.where(planted, picked_rows, random_ids)
    deviation = math.sqrt(BITS) / 2.0
    lowest = max(int(BITS // 2 - 6.0 * deviation), 0)
    highest = int(BITS // 2 - 3.0 * deviation)
    flip_counts = jax.random.randint(flip_key, (QUERIES,), lowest, highest + 1, dtype=jnp.int32)
    orders = jax.vmap(lambda subkey: jax.random.permutation(subkey, BITS))(jax.random.split(order_key, QUERIES))
    flipped = (orders.astype(jnp.int32) < flip_counts[:, None]).astype(jnp.int32)
    near_bits = jnp.bitwise_xor(query_bits, flipped)
    return (query_bits, planted, positive_ids, near_bits)


def draw_query_codes(key, part):
    query_bits, planted, positive_ids, near_bits = shared_codes(key)
    powers = jnp.left_shift(1, jnp.arange(16, dtype=jnp.int32))
    grouped = query_bits.reshape(QUERIES, WORDS, 16)
    return jnp.sum(grouped * powers[None, None, :], axis=2).astype(jnp.int32)


def draw_positive_ids(key, part):
    query_bits, planted, positive_ids, near_bits = shared_codes(key)
    return positive_ids


def draw_bank_codes(key, part):
    query_bits, planted, positive_ids, near_bits = shared_codes(key)
    flips = jax.random.bernoulli(jax.random.fold_in(key, 11), 0.5, (PASSAGES, BITS))
    signs = jnp.where(flips, 1.0, -1.0).astype(jnp.float32)
    targets = jnp.where(planted, positive_ids, PASSAGES)
    near_signs = (2 * near_bits - 1).astype(jnp.float32)
    signs = signs.at[targets].set(near_signs, mode='drop')
    return signs.astype(jnp.bfloat16)


def draw_negative_ids(key, part):
    block_slots = Q_DEV * NEG
    blocks = QUERIES // Q_DEV
    groups = blocks // N_INDEX
    hot_key, order_key, shuffle_key, offset_key = jax.random.split(key, 4)
    hottest = jax.random.randint(hot_key, (groups,), 0, N_INDEX, dtype=jnp.int32)
    orders = jax.vmap(lambda subkey: jax.random.permutation(subkey, N_INDEX))(jax.random.split(order_key, blocks))
    slot_index = jnp.arange(block_slots, dtype=jnp.int32)
    spread_owner = orders[:, slot_index % N_INDEX].astype(jnp.int32)
    hot_owner = jnp.repeat(hottest, N_INDEX)[:, None]
    owners = jnp.where(slot_index[None, :] < block_slots // 8, hot_owner, spread_owner)
    shuffles = jax.vmap(lambda subkey: jax.random.permutation(subkey, block_slots))(jax.random.split(shuffle_key, blocks))
    owners = jnp.take_along_axis(owners, shuffles, axis=1)
    offsets = jax.random.randint(offset_key, (blocks, block_slots), 0, PASS_DEV, dtype=jnp.int32)
    return (owners * PASS_DEV + offsets).reshape(QUERIES, NEG)


def strengthened(entries, rng, source, target, shards_of, factor):
    owner, partner = [(jnp.arange(entries.shape[position]) // (entries.shape[position] // shards_of)).reshape([-1 if axis == position else 1 for axis in range(entries.ndim)]) for position in (source, target)]
    chosen = jax.random.permutation(rng, shards_of)[partner]
    strong = (owner == chosen) | (owner == (partner + shards_of // 2) % shards_of)
    return jnp.where(strong, factor * entries, entries)


def level_of(key, extent, cuts, low, high):
    factor_of = 1.0
    for dim, blocks in cuts:
        steps = jax.random.uniform(jax.random.fold_in(jax.random.fold_in(key, 6), dim), (blocks,), jnp.float32, low / len(cuts), high / len(cuts))
        factor_of = factor_of * jnp.repeat(jnp.exp(steps), extent[dim] // blocks).reshape((-1,) + (1,) * (len(extent) - 1 - dim))
    return factor_of


def bell_draw(key, dims, width, limit, pieces=(), held_as=jnp.bfloat16):
    factor_of = level_of(key, dims, pieces, -0.22, 0.18) if pieces else 1.0
    array = jax.random.normal(key, dims, jnp.float32) * width * factor_of
    return jnp.minimum(jnp.maximum(array, -limit), limit).astype(held_as)


def bell_draw_with(rng, shape, width, most, cuts, heavy, kind=jnp.bfloat16):
    array = width * jax.random.normal(rng, shape, jnp.float32)
    if cuts:
        array = array * level_of(rng, shape, cuts, -0.22, 0.18)
    return jnp.clip(strengthened(array, jax.random.fold_in(rng, 3), *heavy), -most, most).astype(kind)


def setup_inputs(seed: int = 0) -> dict:
    seeds = jax.random.split(jax.random.key(seed), 9)
    query_codes = draw_query_codes(jax.random.fold_in(seeds[8], 71), 0)
    positive_ids = draw_positive_ids(jax.random.fold_in(seeds[8], 71), 0)
    negative_ids = draw_negative_ids(jax.random.fold_in(seeds[8], 71), 0)
    bank_codes = draw_bank_codes(jax.random.fold_in(seeds[8], 71), 0)
    bank_emb = bell_draw(seeds[4], (PASSAGES, D), D ** -0.5, 0.1875, ((0, 32),))
    query_emb = bell_draw_with(seeds[5], (QUERIES, D), D ** -0.5, 0.75, ((0, 128),), (0, 1, 128, 5.5))
    positive_emb = bell_draw(seeds[6], (QUERIES, D), D ** -0.5, 0.1875, ((0, 128),))
    head = bell_draw(seeds[7], (D, D), D ** -0.5, 0.1875)
    return {"query_codes": query_codes, "positive_ids": positive_ids, "negative_ids": negative_ids, "bank_codes": bank_codes, "bank_emb": bank_emb, "query_emb": query_emb, "positive_emb": positive_emb, "head": head}


INV_TEMP = 50.0
EPSILON = 1e-06

def unpack_signs(codes):
    shifts = jnp.arange(16, dtype=jnp.int32)
    bitset = jnp.bitwise_and(jnp.right_shift(codes[:, :, None], shifts[None, None, :]), 1)
    return (2 * bitset - 1).reshape(codes.shape[0], -1).astype(jnp.bfloat16)

def keep_best(first_keys, second_keys):
    joined = jnp.concatenate([first_keys, second_keys], axis=1)
    return -lax.top_k(-joined, CANDS)[0]

def drop_positive(best_keys, positive_ids, passages):
    is_positive = (best_keys % passages == positive_ids[:, None]).astype(jnp.int32)
    passed = jnp.cumsum(is_positive, axis=1) > 0
    return jnp.where(passed[:, :TOPK], best_keys[:, 1:TOPK + 1], best_keys[:, :TOPK])

def head_backward(query_emb, positive_emb, negative_rows, head):
    query_count, feature_count = query_emb.shape
    query_z = jnp.dot(query_emb, head, preferred_element_type=jnp.float32)
    positive_z = jnp.dot(positive_emb, head, preferred_element_type=jnp.float32)
    negative_z = jnp.dot(negative_rows.reshape(-1, feature_count), head, preferred_element_type=jnp.float32)
    negative_z = negative_z.reshape(query_count, NEG, feature_count)
    cand_z = jnp.concatenate([positive_z[:, None, :], negative_z], axis=1)
    query_norm = jnp.sqrt(lax.optimization_barrier(jnp.sum(query_z * query_z, axis=-1, keepdims=True)) + EPSILON)
    cand_norm = jnp.sqrt(lax.optimization_barrier(jnp.sum(cand_z * cand_z, axis=-1, keepdims=True)) + EPSILON)
    query_unit = query_z / query_norm
    cand_unit = cand_z / cand_norm
    logits = INV_TEMP * jnp.einsum('qd,qkd->qk', query_unit, cand_unit)
    weights = jnp.exp(logits)
    softmax_probs = weights / lax.optimization_barrier(jnp.sum(weights, axis=1, keepdims=True))
    first_mark = (jnp.arange(NEG + 1) == 0).astype(jnp.float32)
    slopes = softmax_probs - first_mark[None, :]
    query_du = INV_TEMP * jnp.einsum('qk,qkd->qd', slopes, cand_unit)
    cand_du = INV_TEMP * slopes[:, :, None] * query_unit[:, None, :]
    query_dz = (query_du - query_unit * lax.optimization_barrier(jnp.sum(query_unit * query_du, axis=-1, keepdims=True))) / query_norm
    cand_dz = (cand_du - cand_unit * lax.optimization_barrier(jnp.sum(cand_unit * cand_du, axis=-1, keepdims=True))) / cand_norm
    query_dz = query_dz.astype(jnp.bfloat16)
    cand_dz = cand_dz.astype(jnp.bfloat16)
    return (query_dz, cand_dz[:, 0, :], cand_dz[:, 1:, :])

def reference(query_codes, positive_ids, negative_ids, bank_codes, bank_emb, query_emb, positive_emb, head):
    passages = bank_codes.shape[0]
    sign_bits = unpack_signs(query_codes)

    def shard_step(carried, shard_number):
        first_id = shard_number * PASS_DEV
        bank_block = lax.dynamic_slice_in_dim(bank_codes, first_id, PASS_DEV, 0)
        products = lax.dot_general(sign_bits, bank_block, (((1,), (1,)), ((), ())), preferred_element_type=jnp.float32)
        hamming = ((BITS - products) * 0.5).astype(jnp.int32)
        keyed = hamming * passages + (first_id + jnp.arange(PASS_DEV, dtype=jnp.int32))[None, :]
        return (keep_best(carried, -lax.top_k(-keyed, CANDS)[0]), None)
    initial = jnp.full((QUERIES, CANDS), 2147483647, jnp.int32)
    best_keys, _ = lax.scan(shard_step, initial, jnp.arange(N_INDEX, dtype=jnp.int32))
    chosen = drop_positive(best_keys, positive_ids, passages)
    mined_ids = chosen % passages
    mined_dist = chosen // passages
    negative_rows = jnp.take(bank_emb, negative_ids.reshape(-1), axis=0).reshape(QUERIES, NEG, D)
    query_dz, positive_dz, negative_dz = head_backward(query_emb, positive_emb, negative_rows, head)
    contract_out = (((1,), (1,)), ((), ()))
    query_grad = lax.dot_general(query_dz, head, contract_out, preferred_element_type=jnp.float32).astype(jnp.bfloat16)
    positive_grad = lax.dot_general(positive_dz, head, contract_out, preferred_element_type=jnp.float32).astype(jnp.bfloat16)
    rows_all = jnp.concatenate([query_emb, positive_emb, negative_rows.reshape(-1, D)], axis=0)
    slopes_all = jnp.concatenate([query_dz, positive_dz, negative_dz.reshape(-1, D)], axis=0)
    head_grad = lax.dot_general(rows_all, slopes_all, (((0,), (0,)), ((), ())), preferred_element_type=jnp.float32)
    return (mined_ids, mined_dist, query_grad, positive_grad, head_grad)
```

```python
import functools

import jax
import jax.numpy as jnp
from jax import lax
from jax.experimental import pallas as pl
from jax.experimental.pallas import tpu as pltpu
from jax.sharding import PartitionSpec as P

F32 = jnp.float32
BF16 = jnp.bfloat16
MESH = pl.DeviceIdType.MESH
MIB = 1 << 20
GROUP = 32
SIDE = 4
BIG = float(1 << 23)
LAST = (((1,), (1,)), ((), ()))


def iota(shape, dim):
    return lax.broadcasted_iota(jnp.int32, shape, dim)


def dot(a, b, dims=(((1,), (0,)), ((), ()))):
    return lax.dot_general(a, b, dims, preferred_element_type=F32)


def copy_to(src, dst, send_sem, recv_sem, device):
    return pltpu.make_async_remote_copy(
        src_ref=src,
        dst_ref=dst,
        send_sem=send_sem,
        recv_sem=recv_sem,
        device_id=device,
        device_id_type=MESH,
    )


def coords():
    z = lax.axis_index("dp")
    me = lax.axis_index("index")
    x = lax.div(me, 8)
    y = lax.rem(lax.div(me, 2), 4)
    c = lax.rem(me, 2)
    return z, me, x, y, c


def at(x, y, c):
    return x * 8 + y * 2 + c


def group_barrier(z, me, with_z):
    barrier = pltpu.get_barrier_semaphore()

    def greet(k, carry):
        pl.semaphore_signal(
            barrier, inc=1, device_id=(z, lax.rem(me + k, GROUP)), device_id_type=MESH
        )
        return carry

    lax.fori_loop(1, GROUP, greet, 0)
    count = GROUP - 1
    if with_z:
        for k in range(1, SIDE):
            pl.semaphore_signal(
                barrier, inc=1, device_id=(lax.rem(z + k, SIDE), me), device_id_type=MESH
            )
        count += SIDE - 1
    pl.semaphore_wait(barrier, count)


def request_table(pay):
    hi = jnp.floor(pay * (1.0 / 256.0))
    lo = pay - 256.0 * hi
    halves = jnp.concatenate([hi, lo], axis=0).astype(BF16)
    lane_of = iota((128, 256), 0)
    item = iota((128, 256), 1)
    spread = jnp.where(lane_of == 65 + (item & 15), 1.0, 0.0).astype(BF16)
    got = dot(halves, spread)
    ids = 256.0 * got[0:16] + got[16:32]
    ids = jnp.where(iota((16, 256), 0) == (iota((16, 256), 1) >> 4), ids, 0.0)
    id_row = jnp.sum(ids, axis=0, keepdims=True)
    owner_row = jnp.floor(id_row * (1.0 / 2048.0))
    owner_b = jnp.broadcast_to(owner_row, (256, 256))
    owner_t = jnp.transpose(owner_b)
    earlier = iota((256, 256), 0) < iota((256, 256), 1)
    same = jnp.where(owner_b == owner_t, 1.0, 0.0)
    rank = jnp.sum(jnp.where(earlier, same, 0.0), axis=0, keepdims=True)
    slot_row = jnp.where(rank < 7.0, owner_row * 8.0 + rank, 249.0 + rank)
    slot_b = jnp.broadcast_to(slot_row, (288, 256))
    hit = iota((288, 256), 0).astype(F32) == slot_b
    id_col = jnp.sum(jnp.where(hit, jnp.broadcast_to(id_row, (288, 256)) + 1.0, 0.0), axis=1, keepdims=True) - 1.0
    which = jnp.where(iota((256, 128), 1) == (iota((256, 128), 0) >> 4), 1.0, 0.0).astype(BF16)
    owned_by = dot(jnp.where(hit, 1.0, 0.0).astype(BF16), which)
    lane32 = iota((32, 128), 1)
    sub32 = iota((32, 128), 0)
    ext_row = jnp.sum(
        jnp.where(lane32 == sub32 + 96, jnp.broadcast_to(id_col[256:288], (32, 128)), 0.0), axis=0, keepdims=True
    )
    lane16 = iota((16, 128), 1)
    common = jnp.where(
        lane16 < 65, pay, jnp.where(lane16 >= 96, jnp.broadcast_to(ext_row, (16, 128)), 0.0)
    )
    return id_col, owned_by, common


def onehot_rows(rel, count):
    return jnp.where(
        jnp.broadcast_to(rel, (count, 2048)) == iota((count, 2048), 1).astype(F32), 1.0, 0.0
    ).astype(BF16)


def fetch_kernel(
    pay_ref, bank_hbm,
    table_ref, owned_ref, base_ref, ext_ref,
    bank, out_buf, in_buf, bsend, brecv, esend, eown, ecore, s1, r2a, r2b, s2a, s2b, r3a, r3b,
    load_sem, p_send, p_recv, b_send, b_recv, c_sem, x_send, x_recv,
):
    z, me, x, y, c = coords()
    load = pltpu.make_async_copy(bank_hbm, bank, load_sem)
    load.start()
    id_col, owned_by, common = request_table(pay_ref[...])
    owned_ref[...] = owned_by
    lane = iota((32, 8, 128), 2)
    base_cols = jnp.broadcast_to(id_col[0:256], (256, 128)).reshape(32, 8, 128)
    out_buf[:, 0:8, :] = jnp.where(lane == 65, base_cols, jnp.broadcast_to(common[None, 0:8], (32, 8, 128)))
    out_buf[:, 8:16, :] = jnp.broadcast_to(common[None, 8:16], (32, 8, 128))
    group_barrier(z, me, False)

    def p_copy(k):
        peer = lax.rem(me + k, GROUP)
        return copy_to(out_buf.at[peer], in_buf.at[me], p_send.at[peer], p_recv.at[me], (z, peer))

    def p_take(k):
        source = lax.rem(me + GROUP - k, GROUP)
        return copy_to(out_buf.at[source], in_buf.at[source], p_send.at[source], p_recv.at[source], (z, source))

    def b_copy(k):
        peer = lax.rem(me + k, GROUP)
        return copy_to(bsend.at[peer], brecv.at[me], b_send.at[peer], b_recv.at[me], (z, peer))

    def b_take(k):
        source = lax.rem(me + GROUP - k, GROUP)
        return copy_to(bsend.at[source], brecv.at[source], b_send.at[source], b_recv.at[source], (z, source))

    def each(act):
        def step(k, carry):
            act(k)
            return carry

        lax.fori_loop(1, GROUP, step, 0)

    each(lambda k: p_copy(k).start())
    in_buf[me] = out_buf[me]
    each(lambda k: p_take(k).wait_recv())
    load.wait()

    first = (me * 2048).astype(F32)
    asked = in_buf[:, 0:8, :].reshape(256, 128)
    base_rel = jnp.sum(jnp.where(iota((256, 128), 1) == 65, asked, 0.0), axis=1, keepdims=True) - first
    hot = onehot_rows(base_rel, 256)
    for h in range(2):
        part = dot(hot, bank[:, h * 512 : (h + 1) * 512])
        bsend[:, 8 * h : 8 * h + 8, :] = part.reshape(32, 8, 512).astype(BF16)
    each(lambda k: b_copy(k).start())
    brecv[me] = bsend[me]

    def extras(core):
        rows = in_buf[:, 0:1, :].reshape(16, 2, 1, 128)
        mine = jnp.where(core == 0, rows[:, 0], rows[:, 1])
        wide = jnp.broadcast_to(mine, (16, 32, 128))
        keep = iota((16, 32, 128), 2) == iota((16, 32, 128), 1) + 96
        rel = jnp.sum(jnp.where(keep, wide, 0.0), axis=2, keepdims=True).reshape(512, 1) - first
        return dot(onehot_rows(rel, 512), bank[...])

    esend[...] = extras(1 - c).reshape(16, 32, 1024).astype(BF16)
    core_copy = copy_to(esend, ecore, c_sem.at[0], c_sem.at[1], (z, at(x, y, 1 - c)))
    core_copy.start()
    eown[...] = extras(c).reshape(16, 32, 1024).astype(BF16)
    core_copy.wait_recv()
    s1[...] = (eown[...].astype(F32) + ecore[...].astype(F32)).astype(BF16).reshape(4, 4, 32, 1024)

    left, right = pl.ds(0, 512), pl.ds(512, 512)

    def a2(k, into):
        to = lax.rem(x + k, SIDE)
        return copy_to(s1.at[to, :, :, left], r2a.at[into], x_send.at[0, into], x_recv.at[0, into], (z, at(to, y, c)))

    def b2(k, into):
        to = lax.rem(y + k, SIDE)
        return copy_to(s1.at[:, to, :, right], r2b.at[into], x_send.at[1, into], x_recv.at[1, into], (z, at(x, to, c)))

    def a3(k, into):
        to = lax.rem(y + k, SIDE)
        return copy_to(s2a.at[to], r3a.at[into], x_send.at[2, into], x_recv.at[2, into], (z, at(x, to, c)))

    def b3(k, into):
        to = lax.rem(x + k, SIDE)
        return copy_to(s2b.at[to], r3b.at[into], x_send.at[3, into], x_recv.at[3, into], (z, at(to, y, c)))

    for k in range(1, SIDE):
        a2(k, k - 1).start()
        b2(k, k - 1).start()
    for k in range(1, SIDE):
        a2(k, k - 1).wait_recv()
        b2(k, k - 1).wait_recv()

    def total(own, got):
        t = own.astype(F32)
        for k in range(SIDE - 1):
            t = t + got[k].astype(F32)
        return t.astype(BF16)

    s2a[...] = total(s1[x, :, :, 0:512], r2a)
    s2b[...] = total(s1[:, y, :, 512:1024], r2b)
    for k in range(1, SIDE):
        a3(k, k - 1).start()
        b3(k, k - 1).start()
    for k in range(1, SIDE):
        a3(k, k - 1).wait_recv()
        b3(k, k - 1).wait_recv()
    ext_ref[:, 0:512] = total(s2a[y], r3a)
    ext_ref[:, 512:1024] = total(s2b[x], r3b)

    each(lambda k: b_take(k).wait_recv())
    got = brecv[...].astype(F32)
    base_ref[:, 0:512] = got[:, 0:8].reshape(256, 512).astype(BF16)
    base_ref[:, 512:1024] = got[:, 8:16].reshape(256, 512).astype(BF16)
    table_ref[...] = in_buf[...].reshape(512, 128)
    each(lambda k: p_copy(k).wait_send())
    each(lambda k: b_copy(k).wait_send())
    core_copy.wait_send()
    for k in range(1, SIDE):
        for make in (a2, b2, a3, b3):
            make(k, k - 1).wait_send()


def fetch(pay, bank_emb):
    vm = pl.BlockSpec(memory_space=pltpu.VMEM)
    dma = pltpu.SemaphoreType.DMA
    return pl.pallas_call(
        fetch_kernel,
        out_shape=(
            jax.ShapeDtypeStruct((512, 128), F32),
            jax.ShapeDtypeStruct((288, 128), F32),
            jax.ShapeDtypeStruct((256, 1024), BF16),
            jax.ShapeDtypeStruct((32, 1024), BF16),
        ),
        in_specs=[vm, pl.BlockSpec(memory_space=pl.ANY)],
        out_specs=(vm,) * 4,
        scratch_shapes=[
            pltpu.VMEM((2048, 1024), BF16),
            pltpu.VMEM((32, 16, 128), F32),
            pltpu.VMEM((32, 16, 128), F32),
            pltpu.VMEM((32, 16, 512), BF16),
            pltpu.VMEM((32, 16, 512), BF16),
            pltpu.VMEM((16, 32, 1024), BF16),
            pltpu.VMEM((16, 32, 1024), BF16),
            pltpu.VMEM((16, 32, 1024), BF16),
            pltpu.VMEM((4, 4, 32, 1024), BF16),
            pltpu.VMEM((3, 4, 32, 512), BF16),
            pltpu.VMEM((3, 4, 32, 512), BF16),
            pltpu.VMEM((4, 32, 512), BF16),
            pltpu.VMEM((4, 32, 512), BF16),
            pltpu.VMEM((3, 32, 512), BF16),
            pltpu.VMEM((3, 32, 512), BF16),
            dma,
            dma((GROUP,)),
            dma((GROUP,)),
            dma((GROUP,)),
            dma((GROUP,)),
            dma((2,)),
            dma((4, 3)),
            dma((4, 3)),
        ],
        compiler_params=pltpu.CompilerParams(
            collective_id=0, has_side_effects=True, vmem_limit_bytes=56 * MIB
        ),
        name="fetch",
    )(pay, bank_emb)


def batcher(n):
    pairs = []
    p = 1
    while p < n:
        k = p
        while k >= 1:
            for j in range(k % p, n - k, 2 * k):
                for i in range(min(k, n - j - k)):
                    if (i + j) // (2 * p) == (i + j + k) // (2 * p):
                        pairs.append((i + j, i + j + k))
            k //= 2
        p *= 2
    return pairs


SORT16 = batcher(16)


def exchange(v, i, j):
    v[i], v[j] = jnp.minimum(v[i], v[j]), jnp.maximum(v[i], v[j])


def sort16(v):
    v = list(v)
    for i, j in SORT16:
        exchange(v, i, j)
    return v


def merge16(a, b):
    v = [jnp.minimum(a[i], b[15 - i]) for i in range(16)]
    for d in (8, 4, 2, 1):
        for i in range(16):
            if i & d == 0:
                exchange(v, i, i + d)
    return v


def sign_rows(table):
    hi = jnp.floor(table * (1.0 / 256.0))
    lo = table - 256.0 * hi
    both = jnp.concatenate([hi, lo], axis=1).astype(BF16)
    k = iota((1024, 256), 0)
    lane = iota((1024, 256), 1)
    source = (k >> 4) + jnp.where((k & 8) == 0, 128, 0)
    pick = jnp.where(lane == source, 1.0, 0.0).astype(BF16)
    byte = dot(pick, both, LAST).astype(jnp.int32)
    bit = byte & (1 << (iota((1024, 512), 0) & 7))
    signs = jnp.where(bit != 0, -1024.0, 1024.0).astype(BF16)
    lane16 = iota((16, 256), 1)
    weigh = jnp.where(lane16 == 64, 256.0, jnp.where(lane16 == 192, 1.0, 0.0)).astype(BF16)
    return signs, dot(weigh, both, LAST)


def search_kernel(table_ref, codes_hbm, best_ref, codes, signs, keys, pos, load_sem):
    me = lax.axis_index("index")
    load = pltpu.make_async_copy(codes_hbm, codes, load_sem)
    load.start()
    signs_v, pos_v = sign_rows(table_ref[...])
    signs[...] = signs_v
    pos[...] = pos_v[0:8] - (me * 2048).astype(F32)
    load.wait()

    def product(m, carry):
        at_row = pl.multiple_of(m * 256, 256)
        keys[pl.ds(at_row, 256), :] = dot(codes[pl.ds(at_row, 256), :], signs[...])
        return carry

    lax.fori_loop(0, 8, product, 0)
    sub = iota((8, 128), 0)
    for t in range(4):
        lanes = slice(t * 128, (t + 1) * 128)
        wanted = pos[:, lanes]

        def load16(g):
            out = []
            for i in range(16):
                row = pl.multiple_of(g * 128 + i * 8, 8)
                p = (sub + (g * 128 + i * 8)).astype(F32)
                key = keys[pl.ds(row, 8), lanes] + (p + float(1 << 20))
                out.append(jnp.where(p == wanted, BIG, key))
            return out

        def step(g, best):
            return tuple(merge16(best, sort16(load16(g))))

        best = lax.fori_loop(1, 16, step, tuple(sort16(load16(0))))
        for d in (4, 2, 1):
            best = merge16(best, [pltpu.roll(b, d, 0) for b in best])
        for i in range(16):
            best_ref[t, i : i + 1, :] = best[i][0:1, :]


def search(table, bank_codes):
    vm = pl.BlockSpec(memory_space=pltpu.VMEM)
    return pl.pallas_call(
        search_kernel,
        out_shape=jax.ShapeDtypeStruct((4, 16, 128), F32),
        in_specs=[vm, pl.BlockSpec(memory_space=pl.ANY)],
        out_specs=vm,
        scratch_shapes=[
            pltpu.VMEM((2048, 1024), BF16),
            pltpu.VMEM((1024, 512), BF16),
            pltpu.VMEM((2048, 512), F32),
            pltpu.VMEM((8, 512), F32),
            pltpu.SemaphoreType.DMA,
        ],
        compiler_params=pltpu.CompilerParams(vmem_limit_bytes=48 * MIB),
        name="search",
    )(table, bank_codes)


def split(v):
    high = v.astype(BF16)
    return high, (v - high.astype(F32)).astype(BF16)


def head_kernel(query_ref, positive_ref, base_ref, ext_ref, owned_ref, head_ref, qg_ref, pg_ref, send_ref, xs, dz):
    xs[0:16] = query_ref[...]
    xs[16:32] = positive_ref[...]
    xs[32:288] = base_ref[...]
    xs[288:320] = ext_ref[...]
    head = head_ref[...]
    zed = dot(xs[...], head)
    norm = jnp.sqrt(jnp.sum(zed * zed, axis=1, keepdims=True) + 1e-6)
    inv = 1.0 / norm
    unit = zed * inv
    q_hi, q_lo = split(unit[0:16])
    c_hi, c_lo = split(unit[16:320])
    cos = dot(c_hi, q_hi, LAST) + (dot(c_lo, q_hi, LAST) + dot(c_hi, q_lo, LAST))
    logits = 50.0 * cos
    own_pos = jnp.where(iota((16, 16), 0) == iota((16, 16), 1), 1.0, 0.0)
    mask = jnp.concatenate([own_pos, owned_ref[:, 0:16]], axis=0)
    weights = jnp.where(mask > 0.5, jnp.exp(jnp.where(mask > 0.5, logits, 0.0)), 0.0)
    probs = weights / jnp.sum(weights, axis=0, keepdims=True)
    slopes = probs - jnp.concatenate([own_pos, jnp.zeros((288, 16), F32)], axis=0)
    s_hi, s_lo = split(slopes)
    first_dims = (((0,), (0,)), ((), ()))
    du = 50.0 * (dot(s_hi, c_hi, first_dims) + (dot(s_lo, c_hi, first_dims) + dot(s_hi, c_lo, first_dims)))
    q_unit = unit[0:16]
    dz[0:16] = ((du - q_unit * jnp.sum(q_unit * du, axis=1, keepdims=True)) * inv[0:16]).astype(BF16)
    inv_c = inv[16:320]
    k1_hi, k1_lo = split(slopes * (50.0 * inv_c))
    k2 = jnp.sum(slopes * logits, axis=1, keepdims=True) * inv_c
    along = dot(k1_hi, q_hi) + (dot(k1_lo, q_hi) + dot(k1_hi, q_lo))
    dz[16:320] = (along - unit[16:320] * k2).astype(BF16)
    grads = dot(dz[0:32], head, LAST).astype(BF16)
    qg_ref[...] = grads[0:16]
    pg_ref[...] = grads[16:32]
    for m in range(8):
        part = dot(xs[:, m * 128 : (m + 1) * 128], dz[...], first_dims)
        part = part.reshape(16, 8, 1024)
        part = jnp.concatenate([part[:, :, 0:512], part[:, :, 512:1024]], axis=1).astype(BF16)
        part = part.reshape(2, 4, 2, 16, 512)
        x0 = (m % 2) * 2
        for core in range(2):
            send_ref[core, m // 2, x0 : x0 + 2] = part[:, :, core]


def head_backward(query_emb, positive_emb, base, ext, owned, head):
    vm = pl.BlockSpec(memory_space=pltpu.VMEM)
    return pl.pallas_call(
        head_kernel,
        out_shape=(
            jax.ShapeDtypeStruct((16, 1024), BF16),
            jax.ShapeDtypeStruct((16, 1024), BF16),
            jax.ShapeDtypeStruct((2, 4, 4, 4, 16, 512), BF16),
        ),
        in_specs=[vm] * 6,
        out_specs=(vm,) * 3,
        scratch_shapes=[pltpu.VMEM((320, 1024), BF16), pltpu.VMEM((320, 1024), BF16)],
        compiler_params=pltpu.CompilerParams(vmem_limit_bytes=48 * MIB),
        name="head",
    )(query_emb, positive_emb, base, ext, owned, head)


ORDERS = ((0, 1, 2), (1, 2, 0), (2, 0, 1), (0, 2, 1))


def finish_kernel(
    best_ref, send_ref, ids_ref, dist_ref, hg_ref,
    crecv, packed, square, core_in, parts, inbox, mids, inbox2, tail, inbox3,
    t_send, t_recv, c_sem, r_send, r_recv,
):
    z, me, x, y, c = coords()
    group_barrier(z, me, True)
    place = (z, x, y)

    def device(axis, to):
        where = [z, x, y]
        where[axis] = to
        return (where[0], at(where[1], where[2], c))

    core_copy = copy_to(send_ref.at[1 - c], core_in, c_sem.at[0], c_sem.at[1], (z, at(x, y, 1 - c)))
    core_copy.start()

    def t_copy(k):
        peer = lax.rem(me + k, GROUP)
        return copy_to(best_ref.at[lax.div(peer, 8)], crecv.at[me], t_send.at[peer], t_recv.at[me], (z, peer))

    def t_take(k):
        source = lax.rem(me + GROUP - k, GROUP)
        return copy_to(best_ref.at[0], crecv.at[source], t_send.at[source], t_recv.at[source], (z, source))

    def each(act):
        def step(k, carry):
            act(k)
            return carry

        lax.fori_loop(1, GROUP, step, 0)

    each(lambda k: t_copy(k).start())
    crecv[me] = best_ref[lax.div(me, 8)]

    core_copy.wait_recv()
    parts[...] = (send_ref[c].astype(F32) + core_in[...].astype(F32)).astype(BF16)

    def lanes(p):
        return pl.ds(p * 128, 128)

    def first(p, k):
        axis = ORDERS[p][0]
        to = lax.rem(place[axis] + k, SIDE)
        index = [slice(None)] * 3
        index[axis] = to
        return copy_to(
            parts.at[(*index, slice(None), lanes(p))], inbox.at[p, k - 1],
            r_send.at[0, p, k - 1], r_recv.at[0, p, k - 1], device(axis, to),
        )

    def second(p, k):
        axis = ORDERS[p][1]
        to = lax.rem(place[axis] + k, SIDE)
        rest = [a for a in range(3) if a != ORDERS[p][0]]
        index = [slice(None)] * 2
        index[rest.index(axis)] = to
        return copy_to(
            mids.at[(p, *index)], inbox2.at[p, k - 1],
            r_send.at[1, p, k - 1], r_recv.at[1, p, k - 1], device(axis, to),
        )

    def third(p, k):
        axis = ORDERS[p][2]
        to = lax.rem(place[axis] + k, SIDE)
        return copy_to(
            tail.at[p, to], inbox3.at[p, k - 1],
            r_send.at[2, p, k - 1], r_recv.at[2, p, k - 1], device(axis, to),
        )

    def total(own, got):
        t = own.astype(F32)
        for k in range(SIDE - 1):
            t = t + got[k].astype(F32)
        return t

    def start(make):
        for k in range(1, SIDE):
            for p in range(4):
                make(p, k).start()

    def arrive(make, p):
        for k in range(1, SIDE):
            make(p, k).wait_recv()

    start(first)

    each(lambda k: t_take(k).wait_recv())
    lane = iota((16, 128), 1)
    packed[...] = jnp.full((8, 16, 128), 2147483647, jnp.int32)
    mine = lax.rem(me, 8)
    for g in range(4):
        merged = jnp.zeros((16, 128), jnp.int32)
        for s in range(8):
            key = crecv[g * 8 + s].astype(jnp.int32)
            key = ((key >> 11) << 16) + (key & 2047) + (g * 8 + s) * 2048
            key = pltpu.roll(key, lax.rem((s - mine + 8) * 16, 128), 1)
            merged = jnp.where((lane >> 4) == s, key, merged)
        packed[g] = merged
    best = [packed[:, i, :] for i in range(16)]
    for d in (64, 32, 16):
        best = merge16(best, [pltpu.roll(b, d, 1) for b in best])
    for d in (6, 7):
        best = merge16(best, [pltpu.roll(b, d, 0) for b in best])
    for i in range(16):
        square[i : i + 1, :] = best[i][0:1, :]
    square[16:128, :] = jnp.zeros((112, 128), jnp.int32)
    flat = square[...]
    ids_ref[...] = jnp.transpose((flat & 65535).astype(F32))[0:16, 0:16].astype(jnp.int32)
    dist_ref[...] = jnp.transpose((flat >> 16).astype(F32))[0:16, 0:16].astype(jnp.int32)

    for p in range(4):
        arrive(first, p)
        index = [slice(None)] * 3
        index[ORDERS[p][0]] = place[ORDERS[p][0]]
        own = parts[(*index, slice(None), slice(p * 128, (p + 1) * 128))]
        mids[p] = total(own, inbox.at[p]).astype(BF16)
        for k in range(1, SIDE):
            second(p, k).start()
    for p in range(4):
        arrive(second, p)
        axis = ORDERS[p][1]
        rest = [a for a in range(3) if a != ORDERS[p][0]]
        index = [slice(None)] * 2
        index[rest.index(axis)] = place[axis]
        own = mids[(p, *index)]
        tail[p] = total(own, inbox2.at[p]).astype(BF16)
        for k in range(1, SIDE):
            third(p, k).start()
    for p in range(4):
        arrive(third, p)
        out = total(tail[p, place[ORDERS[p][2]]], inbox3.at[p])
        hg_ref[:, p * 128 : (p + 1) * 128] = out[0:8]
        hg_ref[:, 512 + p * 128 : 512 + (p + 1) * 128] = out[8:16]

    each(lambda k: t_copy(k).wait_send())
    core_copy.wait_send()
    for make in (first, second, third):
        for p in range(4):
            for k in range(1, SIDE):
                make(p, k).wait_send()


def finish(best, send):
    vm = pl.BlockSpec(memory_space=pltpu.VMEM)
    dma = pltpu.SemaphoreType.DMA
    return pl.pallas_call(
        finish_kernel,
        out_shape=(
            jax.ShapeDtypeStruct((16, 16), jnp.int32),
            jax.ShapeDtypeStruct((16, 16), jnp.int32),
            jax.ShapeDtypeStruct((8, 1024), F32),
        ),
        in_specs=[vm, vm],
        out_specs=(vm,) * 3,
        scratch_shapes=[
            pltpu.VMEM((32, 16, 128), F32),
            pltpu.VMEM((8, 16, 128), jnp.int32),
            pltpu.VMEM((128, 128), jnp.int32),
            pltpu.VMEM((4, 4, 4, 16, 512), BF16),
            pltpu.VMEM((4, 4, 4, 16, 512), BF16),
            pltpu.VMEM((4, 3, 4, 4, 16, 128), BF16),
            pltpu.VMEM((4, 4, 4, 16, 128), BF16),
            pltpu.VMEM((4, 3, 4, 16, 128), BF16),
            pltpu.VMEM((4, 4, 16, 128), BF16),
            pltpu.VMEM((4, 3, 16, 128), BF16),
            dma((GROUP,)),
            dma((GROUP,)),
            dma((2,)),
            dma((3, 4, 3)),
            dma((3, 4, 3)),
        ],
        compiler_params=pltpu.CompilerParams(
            collective_id=1, has_side_effects=True, vmem_limit_bytes=48 * MIB
        ),
        name="finish",
    )(best, send)


def local(
    query_codes, positive_ids, negative_ids, bank_codes, bank_emb, query_emb, positive_emb, head
):
    pay = jnp.concatenate([query_codes, positive_ids[:, None], negative_ids], axis=1).astype(F32)
    pay = jnp.pad(pay, ((0, 0), (0, 128 - pay.shape[1])))
    table, owned, base, ext = fetch(pay, bank_emb)
    best = search(table, bank_codes)
    query_grad, positive_grad, send = head_backward(query_emb, positive_emb, base, ext, owned, head)
    mined_ids, mined_dist, head_grad = finish(best, send)
    return (mined_ids, mined_dist, query_grad, positive_grad, head_grad)


def solution(mesh):
    both = ("dp", "index")
    rows = P(both, None)
    return jax.shard_map(
        local,
        mesh=mesh,
        in_specs=(rows, P(both), rows, P("index", None), P("index", None), rows, rows, P()),
        out_specs=(rows,) * 5,
        check_vma=False,
    )
```

```python
import functools

import jax
import jax.numpy as jnp
from jax import lax
from jax.experimental import pallas as pl
from jax.experimental.pallas import tpu as pltpu
from jax.sharding import PartitionSpec as P

F32 = jnp.float32
BF16 = jnp.bfloat16
MESH = pl.DeviceIdType.MESH
MIB = 1 << 20
GROUP = 32
SIDE = 4
BIG = float(1 << 23)
LAST = (((1,), (1,)), ((), ()))


def iota(shape, dim):
    return lax.broadcasted_iota(jnp.int32, shape, dim)


def dot(a, b, dims=(((1,), (0,)), ((), ()))):
    return lax.dot_general(a, b, dims, preferred_element_type=F32)


def copy_to(src, dst, send_sem, recv_sem, device):
    return pltpu.make_async_remote_copy(
        src_ref=src,
        dst_ref=dst,
        send_sem=send_sem,
        recv_sem=recv_sem,
        device_id=device,
        device_id_type=MESH,
    )


def coords():
    z = lax.axis_index("dp")
    me = lax.axis_index("index")
    x = lax.div(me, 8)
    y = lax.rem(lax.div(me, 2), 4)
    c = lax.rem(me, 2)
    return z, me, x, y, c


def at(x, y, c):
    return x * 8 + y * 2 + c


OFFSETS = sorted(
    ((dx, dy, dc) for dx in range(4) for dy in range(4) for dc in range(2) if dx or dy or dc),
    key=lambda o: -(min(o[0], 4 - o[0]) + min(o[1], 4 - o[1])),
)


def peers(x, y, c):
    return [at(lax.rem(x + dx, 4), lax.rem(y + dy, 4), lax.rem(c + dc, 2)) for dx, dy, dc in OFFSETS]


def take(ref, sem):
    pltpu.make_async_copy(ref, ref, sem).wait()


def request_table(codes, pos_row, negatives):
    hi = jnp.floor(negatives * (1.0 / 256.0))
    lo = negatives - 256.0 * hi
    halves = jnp.concatenate([hi, lo], axis=0).astype(BF16)
    spread = jnp.where(iota((16, 256), 0) == (iota((16, 256), 1) & 15), 1.0, 0.0).astype(BF16)
    got = dot(halves, spread)
    ids = 256.0 * got[0:16] + got[16:32]
    ids = jnp.where(iota((16, 256), 0) == (iota((16, 256), 1) >> 4), ids, 0.0)
    id_row = jnp.sum(ids, axis=0, keepdims=True)
    owner_row = jnp.floor(id_row * (1.0 / 2048.0))
    owner_b = jnp.broadcast_to(owner_row, (256, 256))
    owner_t = jnp.transpose(owner_b)
    earlier = iota((256, 256), 0) < iota((256, 256), 1)
    same = jnp.where(owner_b == owner_t, 1.0, 0.0)
    rank = jnp.sum(jnp.where(earlier, same, 0.0), axis=0, keepdims=True)
    slot_row = jnp.where(rank < 7.0, owner_row * 8.0 + rank, 249.0 + rank)
    slot_b = jnp.broadcast_to(slot_row, (288, 256))
    hit = iota((288, 256), 0).astype(F32) == slot_b
    id_col = jnp.sum(jnp.where(hit, jnp.broadcast_to(id_row, (288, 256)) + 1.0, 0.0), axis=1, keepdims=True) - 1.0
    which = jnp.where(iota((256, 128), 1) == (iota((256, 128), 0) >> 4), 1.0, 0.0).astype(BF16)
    owned_by = dot(jnp.where(hit, 1.0, 0.0).astype(BF16), which)
    lane32 = iota((32, 128), 1)
    sub32 = iota((32, 128), 0)
    ext_row = jnp.sum(
        jnp.where(lane32 == sub32 + 96, jnp.broadcast_to(id_col[256:288], (32, 128)), 0.0), axis=0, keepdims=True
    )
    diagonal = iota((16, 16), 0) == iota((16, 16), 1)
    pos_col = jnp.sum(jnp.where(diagonal, jnp.broadcast_to(pos_row, (16, 16)), 0.0), axis=1, keepdims=True)
    lane16 = iota((16, 128), 1)
    rest = jnp.where(lane16 >= 96, jnp.broadcast_to(ext_row, (16, 128)), 0.0)
    rest = jnp.where(lane16 == 64, jnp.broadcast_to(pos_col, (16, 128)), rest)
    return id_col, owned_by, jnp.where(lane16 < 64, codes, rest)


def onehot_rows(rel, count):
    return jnp.where(
        jnp.broadcast_to(rel, (count, 2048)) == iota((count, 2048), 1).astype(F32), 1.0, 0.0
    ).astype(BF16)


def batcher(n):
    pairs = []
    p = 1
    while p < n:
        k = p
        while k >= 1:
            for j in range(k % p, n - k, 2 * k):
                for i in range(min(k, n - j - k)):
                    if (i + j) // (2 * p) == (i + j + k) // (2 * p):
                        pairs.append((i + j, i + j + k))
            k //= 2
        p *= 2
    return pairs


SORT16 = batcher(16)


def exchange(v, i, j):
    v[i], v[j] = jnp.minimum(v[i], v[j]), jnp.maximum(v[i], v[j])


def sort16(v):
    v = list(v)
    for i, j in SORT16:
        exchange(v, i, j)
    return v


def merge16(a, b):
    v = [jnp.minimum(a[i], b[15 - i]) for i in range(16)]
    for d in (8, 4, 2, 1):
        for i in range(16):
            if i & d == 0:
                exchange(v, i, i + d)
    return v


def sign_rows(table):
    hi = jnp.floor(table * (1.0 / 256.0))
    lo = table - 256.0 * hi
    both = jnp.concatenate([hi, lo], axis=1).astype(BF16)
    k = iota((1024, 256), 0)
    lane = iota((1024, 256), 1)
    source = (k >> 4) + jnp.where((k & 8) == 0, 128, 0)
    pick = jnp.where(lane == source, 1.0, 0.0).astype(BF16)
    byte = dot(pick, both, LAST).astype(jnp.int32)
    bit = byte & (1 << (iota((1024, 512), 0) & 7))
    signs = jnp.where(bit != 0, -1024.0, 1024.0).astype(BF16)
    lane16 = iota((16, 256), 1)
    weigh = jnp.where(lane16 == 64, 256.0, jnp.where(lane16 == 192, 1.0, 0.0)).astype(BF16)
    return signs, dot(weigh, both, LAST)


PORTIONS = ((0, 0, 4, (0, 1, 2)), (1, 0, 4, (1, 2, 0)), (2, 0, 4, (2, 0, 1)), (3, 0, 2, (0, 1, 2)), (3, 2, 2, (1, 0, 2)))
TAIL = (0, 1, 2, 3, 3)


def extents(p, stage):
    _, _, ys, order = PORTIONS[p]
    return [(a, ys if a == 2 else SIDE) for a in range(3) if a not in order[:stage]]


def split(v):
    high = v.astype(BF16)
    return high, (v - high.astype(F32)).astype(BF16)


def whole_kernel(
    qcodes_ref, pos_ref, neg_ref, codes_hbm, bank_hbm, query_ref, positive_ref, head_hbm,
    best_ref, grads_ref, hg_ref,
    bank, codes, head, pay, owned, out_buf, in_buf, bsend, brecv, esend, eown, ecore, s1, r2a, r2b, s2a, s2b, r3a, r3b,
    signs, keys, pos, shard_best, crecv, packed, xs, dz, unit, inv, u_hi, u_lo,
    hs, core_in, parts, in1, mid, in2, tail, in3,
    load_sem, p_sem, b_sem, t_sem, c_sem, x_send, x_recv, h_send, h_recv, r_send, r_recv,
):
    z, me, x, y, c = coords()
    others = peers(x, y, c)
    partner = (z, at(x, y, 1 - c))
    load_bank = pltpu.make_async_copy(bank_hbm, bank, load_sem.at[0])
    load_codes = pltpu.make_async_copy(codes_hbm, codes, load_sem.at[1])
    load_head = pltpu.make_async_copy(head_hbm, head, load_sem.at[2])
    load_bank.start()
    barrier = pltpu.get_barrier_semaphore()
    for peer in others:
        pl.semaphore_signal(barrier, inc=1, device_id=(z, peer), device_id_type=MESH)
    for k in range(1, SIDE):
        pl.semaphore_signal(barrier, inc=1, device_id=(lax.rem(z + k, SIDE), me), device_id_type=MESH)
    load_codes.start()
    load_head.start()

    pay[...] = jnp.zeros((16, 128), F32)
    pay[:, 0:64] = qcodes_ref[...].astype(F32)
    id_col, owned_by, common = request_table(pay[...], pos_ref[...].astype(F32), neg_ref[...].astype(F32))
    owned[...] = owned_by
    lane = iota((32, 8, 128), 2)
    base_cols = jnp.broadcast_to(id_col[0:256], (256, 128)).reshape(32, 8, 128)
    out_buf[:, 0:8, :] = jnp.where(lane == 65, base_cols, jnp.broadcast_to(common[None, 0:8], (32, 8, 128)))
    out_buf[:, 8:16, :] = jnp.broadcast_to(common[None, 8:16], (32, 8, 128))
    pl.semaphore_wait(barrier, len(others) + SIDE - 1)
    for peer in others:
        copy_to(out_buf.at[peer], in_buf.at[me], p_sem.at[0], p_sem.at[1], (z, peer)).start()
    in_buf[me] = out_buf[me]

    xs[0:16] = query_ref[...]
    xs[16:32] = positive_ref[...]

    def project(start, count):
        rows = slice(start, start + count)
        zed = dot(xs[rows], head[...])
        scale = 1.0 / jnp.sqrt(jnp.sum(zed * zed, axis=1, keepdims=True) + 1e-6)
        u = zed * scale
        unit[rows] = u
        inv[rows] = jnp.broadcast_to(scale, (count, 128))
        high, low = split(u)
        u_hi[rows] = high
        u_lo[rows] = low

    load_head.wait()
    project(0, 32)
    load_bank.wait()
    take(in_buf.at[pl.ds(0, GROUP - 1)], p_sem.at[1])

    first = (me * 2048).astype(F32)
    asked = in_buf[:, 0:8, :].reshape(256, 128)
    base_rel = jnp.sum(jnp.where(iota((256, 128), 1) == 65, asked, 0.0), axis=1, keepdims=True) - first
    hot = onehot_rows(base_rel, 256)
    for h in range(2):
        part = dot(hot, bank[:, h * 512 : (h + 1) * 512])
        bsend[:, 8 * h : 8 * h + 8, :] = part.reshape(32, 8, 512).astype(BF16)
    for peer in others:
        copy_to(bsend.at[peer], brecv.at[me], b_sem.at[0], b_sem.at[1], (z, peer)).start()
    brecv[me] = bsend[me]

    def extras(core):
        rows = in_buf[:, 0:1, :].reshape(16, 2, 1, 128)
        mine = jnp.where(core == 0, rows[:, 0], rows[:, 1])
        wide = jnp.broadcast_to(mine, (16, 32, 128))
        keep = iota((16, 32, 128), 2) == iota((16, 32, 128), 1) + 96
        rel = jnp.sum(jnp.where(keep, wide, 0.0), axis=2, keepdims=True).reshape(512, 1) - first
        return dot(onehot_rows(rel, 512), bank[...])

    esend[...] = extras(1 - c).reshape(16, 32, 1024).astype(BF16)
    core_copy = copy_to(esend, ecore, c_sem.at[0], c_sem.at[1], partner)
    core_copy.start()
    eown[...] = extras(c).reshape(16, 32, 1024).astype(BF16)
    core_copy.wait_recv()
    s1[...] = (eown[...].astype(F32) + ecore[...].astype(F32)).astype(BF16).reshape(4, 4, 32, 1024)

    left, right = pl.ds(0, 512), pl.ds(512, 512)
    for k in (2, 1, 3):
        to = lax.rem(x + k, SIDE)
        copy_to(s1.at[to, :, :, left], r2a.at[k - 1], x_send.at[0], x_recv.at[0], (z, at(to, y, c))).start()
        to = lax.rem(y + k, SIDE)
        copy_to(s1.at[:, to, :, right], r2b.at[k - 1], x_send.at[1], x_recv.at[1], (z, at(x, to, c))).start()

    signs_v, pos_v = sign_rows(in_buf[...].reshape(512, 128))
    signs[...] = signs_v
    pos[...] = pos_v[0:8] - first
    load_codes.wait()

    def product(m, carry):
        at_row = pl.multiple_of(m * 256, 256)
        keys[pl.ds(at_row, 256), :] = dot(codes[pl.ds(at_row, 256), :], signs[...])
        return carry

    lax.fori_loop(0, 8, product, 0)
    sub = iota((8, 128), 0)

    def select(t):
        lanes = slice(t * 128, (t + 1) * 128)
        wanted = pos[:, lanes]

        def load16(g):
            out = []
            for i in range(16):
                row = pl.multiple_of(g * 128 + i * 8, 8)
                p = (sub + (g * 128 + i * 8)).astype(F32)
                key = keys[pl.ds(row, 8), lanes] + (p + float(1 << 20))
                out.append(jnp.where(p == wanted, BIG, key))
            return out

        def step(g, best):
            return tuple(merge16(best, sort16(load16(g))))

        best = lax.fori_loop(1, 16, step, tuple(sort16(load16(0))))
        for d in (4, 2, 1):
            best = merge16(best, [pltpu.roll(b, d, 0) for b in best])
        for i in range(16):
            shard_best[t, i : i + 1, :] = best[i][0:1, :]

    select(0)
    select(1)

    def total(own, got):
        t = own.astype(F32)
        for k in range(SIDE - 1):
            t = t + got[k].astype(F32)
        return t

    take(r2a, x_recv.at[0])
    take(r2b, x_recv.at[1])
    s2a[...] = total(s1[x, :, :, 0:512], r2a).astype(BF16)
    s2b[...] = total(s1[:, y, :, 512:1024], r2b).astype(BF16)
    for k in (2, 1, 3):
        to = lax.rem(y + k, SIDE)
        copy_to(s2a.at[to], r3a.at[k - 1], x_send.at[2], x_recv.at[2], (z, at(x, to, c))).start()
        to = lax.rem(x + k, SIDE)
        copy_to(s2b.at[to], r3b.at[k - 1], x_send.at[3], x_recv.at[3], (z, at(to, y, c))).start()

    select(2)
    select(3)
    for peer in others:
        copy_to(shard_best.at[lax.div(peer, 8)], crecv.at[me], t_sem.at[0], t_sem.at[1], (z, peer)).start()
    crecv[me] = shard_best[lax.div(me, 8)]

    take(brecv.at[pl.ds(0, GROUP - 1)], b_sem.at[1])
    got = brecv[...].astype(F32)
    xs[32:288, 0:512] = got[:, 0:8].reshape(256, 512).astype(BF16)
    xs[32:288, 512:1024] = got[:, 8:16].reshape(256, 512).astype(BF16)
    project(32, 256)
    take(r3a, x_recv.at[2])
    take(r3b, x_recv.at[3])
    xs[288:320, 0:512] = total(s2a[y], r3a).astype(BF16)
    xs[288:320, 512:1024] = total(s2b[x], r3b).astype(BF16)
    project(288, 32)

    q_hi, q_lo = u_hi[0:16], u_lo[0:16]
    c_hi, c_lo = u_hi[16:320], u_lo[16:320]
    logits = 50.0 * (dot(c_hi, q_hi, LAST) + (dot(c_lo, q_hi, LAST) + dot(c_hi, q_lo, LAST)))
    own_pos = jnp.where(iota((16, 16), 0) == iota((16, 16), 1), 1.0, 0.0)
    mask = jnp.concatenate([own_pos, owned[:, 0:16]], axis=0)
    weights = jnp.where(mask > 0.5, jnp.exp(jnp.where(mask > 0.5, logits, 0.0)), 0.0)
    probs = weights / jnp.sum(weights, axis=0, keepdims=True)
    slopes = probs - jnp.concatenate([own_pos, jnp.zeros((288, 16), F32)], axis=0)
    s_hi, s_lo = split(slopes)
    firsts = (((0,), (0,)), ((), ()))
    du = 50.0 * (dot(s_hi, c_hi, firsts) + (dot(s_lo, c_hi, firsts) + dot(s_hi, c_lo, firsts)))
    q_unit = unit[0:16]
    dz[0:16] = ((du - q_unit * jnp.sum(q_unit * du, axis=1, keepdims=True)) * inv[0:16, 0:1]).astype(BF16)
    inv_c = inv[16:320, 0:1]
    k1_hi, k1_lo = split(slopes * (50.0 * inv_c))
    k2 = jnp.sum(slopes * logits, axis=1, keepdims=True) * inv_c
    along = dot(k1_hi, q_hi) + (dot(k1_lo, q_hi) + dot(k1_hi, q_lo))
    dz[16:320] = (along - unit[16:320] * k2).astype(BF16)

    def piece(i):
        m = lax.rem(2 * (z + 1) + i, 8)
        return m, lax.div(m, 2), pl.ds(lax.rem(m, 2) * 2, 2)

    def h_copy(i):
        m, zz, xx = piece(i)
        return copy_to(hs.at[1 - c, zz, xx], core_in.at[zz, xx], h_send, h_recv.at[m], partner)

    def grow(i, carry):
        m, zz, xx = piece(i)
        part = dot(xs[:, pl.ds(pl.multiple_of(m * 128, 128), 128)], dz[...], firsts).reshape(16, 8, 1024)
        part = jnp.concatenate([part[:, :, 0:512], part[:, :, 512:1024]], axis=1).astype(BF16)
        part = part.reshape(2, 4, 2, 16, 512)
        for core in range(2):
            hs[core, zz, xx] = part[:, :, core]
        h_copy(i).start()
        return carry

    lax.fori_loop(0, 8, grow, 0)

    place = (z, x, y)

    def device(axis, to):
        where = [z, x, y]
        where[axis] = to
        return (where[0], at(where[1], where[2], c))

    def first_from(p, to):
        tile, y0, ys, order = PORTIONS[p]
        index = [slice(None), slice(None), pl.ds(y0, ys)]
        if order[0] == 2:
            index[2] = to
        else:
            index[order[0]] = to
        return (*index, slice(None), pl.ds(tile * 128, 128))

    def send_first(p, k):
        axis = PORTIONS[p][3][0]
        to = lax.rem(place[axis] + k, SIDE)
        copy_to(
            parts.at[first_from(p, to)], in1[p].at[k - 1], r_send.at[0, p], r_recv.at[0, p], device(axis, to)
        ).start()

    for i in range(8):
        m, zz, xx = piece(i)
        h_copy(i).wait_recv()
        parts[zz, xx] = (hs[c, zz, xx].astype(F32) + core_in[zz, xx].astype(F32)).astype(BF16)
        if i % 2 == 1 and i < 6:
            send_first(0, i // 2 + 1)
            send_first(3, i // 2 + 1)
    for k in (2, 1, 3):
        for p in (1, 4, 2):
            send_first(p, k)

    grads_ref[...] = dot(dz[0:32], head[...], LAST).astype(BF16)

    take(crecv.at[pl.ds(0, GROUP - 1)], t_sem.at[1])
    lane = iota((16, 128), 1)
    packed[...] = jnp.full((8, 16, 128), 2147483647, jnp.int32)
    mine = lax.rem(me, 8)
    for g in range(4):
        merged = jnp.zeros((16, 128), jnp.int32)
        for s in range(8):
            key = crecv[g * 8 + s].astype(jnp.int32)
            key = ((key >> 11) << 16) + (key & 2047) + (g * 8 + s) * 2048
            key = pltpu.roll(key, lax.rem((s - mine + 8) * 16, 128), 1)
            merged = jnp.where((lane >> 4) == s, key, merged)
        packed[g] = merged
    best = [packed[:, i, :] for i in range(16)]
    for d in (64, 32, 16):
        best = merge16(best, [pltpu.roll(b, d, 1) for b in best])
    for d in (6, 7):
        best = merge16(best, [pltpu.roll(b, d, 0) for b in best])
    for i in range(16):
        best_ref[i : i + 1, :] = best[i][0:1, :]

    def pick(p, stage, to):
        axis = PORTIONS[p][3][stage]
        return tuple(to if a == axis else slice(None) for a, _ in extents(p, stage))

    for p in (1, 2, 4, 0, 3):
        axis = PORTIONS[p][3][0]
        take(in1[p], r_recv.at[0, p])
        mid[p][...] = total(parts[first_from(p, place[axis])], in1[p]).astype(BF16)
        axis = PORTIONS[p][3][1]
        for k in (2, 1, 3):
            to = lax.rem(place[axis] + k, SIDE)
            copy_to(
                mid[p].at[pick(p, 1, to)], in2[p].at[k - 1], r_send.at[1, p], r_recv.at[1, p], device(axis, to)
            ).start()
    for p in (1, 2, 4, 0, 3):
        axis = PORTIONS[p][3][1]
        take(in2[p], r_recv.at[1, p])
        _, y0, ys, order = PORTIONS[p]
        sums = total(mid[p][pick(p, 1, place[axis])], in2[p]).astype(BF16)
        if TAIL[p] == 3:
            tail[3, y0 : y0 + ys] = sums
        else:
            tail[p] = sums
        if p == 4:
            continue
        q = TAIL[p]
        axis = order[2]
        for k in (2, 1, 3):
            to = lax.rem(place[axis] + k, SIDE)
            copy_to(
                tail.at[q, to], in3.at[q, k - 1], r_send.at[2, q], r_recv.at[2, q], device(axis, to)
            ).start()
    for q in range(4):
        take(in3.at[q], r_recv.at[2, q])
        out = total(tail[q, place[PORTIONS[q][3][2]]], in3.at[q])
        hg_ref[:, q * 128 : (q + 1) * 128] = out[0:8]
        hg_ref[:, 512 + q * 128 : 512 + (q + 1) * 128] = out[8:16]

    take(out_buf.at[pl.ds(0, GROUP - 1)], p_sem.at[0])
    take(bsend.at[pl.ds(0, GROUP - 1)], b_sem.at[0])
    take(crecv.at[pl.ds(0, GROUP - 1)], t_sem.at[0])
    core_copy.wait_send()
    take(r2a, x_send.at[0])
    take(r2b, x_send.at[1])
    take(r3a, x_send.at[2])
    take(r3b, x_send.at[3])
    take(core_in, h_send)
    for p in range(5):
        take(in1[p], r_send.at[0, p])
        take(in2[p], r_send.at[1, p])
    for q in range(4):
        take(in3.at[q], r_send.at[2, q])


def whole(codes, pos, neg, bank_codes, bank_emb, query_emb, positive_emb, head):
    vm = pl.BlockSpec(memory_space=pltpu.VMEM)
    anywhere = pl.BlockSpec(memory_space=pl.ANY)
    dma = pltpu.SemaphoreType.DMA
    block = (16, 128)

    def by_portion(stage, lead):
        return [pltpu.VMEM((*lead, *(n for _, n in extents(p, stage)), *block), BF16) for p in range(5)]

    return pl.pallas_call(
        whole_kernel,
        out_shape=(
            jax.ShapeDtypeStruct((16, 128), jnp.int32),
            jax.ShapeDtypeStruct((32, 1024), BF16),
            jax.ShapeDtypeStruct((8, 1024), F32),
        ),
        in_specs=[vm, vm, vm, anywhere, anywhere, vm, vm, anywhere],
        out_specs=(vm,) * 3,
        scratch_shapes=[
            pltpu.VMEM((2048, 1024), BF16),
            pltpu.VMEM((2048, 1024), BF16),
            pltpu.VMEM((1024, 1024), BF16),
            pltpu.VMEM((16, 128), F32),
            pltpu.VMEM((288, 128), F32),
            pltpu.VMEM((32, 16, 128), F32),
            pltpu.VMEM((32, 16, 128), F32),
            pltpu.VMEM((32, 16, 512), BF16),
            pltpu.VMEM((32, 16, 512), BF16),
            pltpu.VMEM((16, 32, 1024), BF16),
            pltpu.VMEM((16, 32, 1024), BF16),
            pltpu.VMEM((16, 32, 1024), BF16),
            pltpu.VMEM((4, 4, 32, 1024), BF16),
            pltpu.VMEM((3, 4, 32, 512), BF16),
            pltpu.VMEM((3, 4, 32, 512), BF16),
            pltpu.VMEM((4, 32, 512), BF16),
            pltpu.VMEM((4, 32, 512), BF16),
            pltpu.VMEM((3, 32, 512), BF16),
            pltpu.VMEM((3, 32, 512), BF16),
            pltpu.VMEM((1024, 512), BF16),
            pltpu.VMEM((2048, 512), F32),
            pltpu.VMEM((8, 512), F32),
            pltpu.VMEM((4, 16, 128), F32),
            pltpu.VMEM((32, 16, 128), F32),
            pltpu.VMEM((8, 16, 128), jnp.int32),
            pltpu.VMEM((320, 1024), BF16),
            pltpu.VMEM((320, 1024), BF16),
            pltpu.VMEM((320, 1024), F32),
            pltpu.VMEM((320, 128), F32),
            pltpu.VMEM((320, 1024), BF16),
            pltpu.VMEM((320, 1024), BF16),
            pltpu.VMEM((2, 4, 4, 4, 16, 512), BF16),
            pltpu.VMEM((4, 4, 4, 16, 512), BF16),
            pltpu.VMEM((4, 4, 4, 16, 512), BF16),
            by_portion(1, (3,)),
            by_portion(1, ()),
            by_portion(2, (3,)),
            pltpu.VMEM((4, 4, *block), BF16),
            pltpu.VMEM((4, 3, *block), BF16),
            dma((3,)),
            dma((2,)),
            dma((2,)),
            dma((2,)),
            dma((2,)),
            dma((4,)),
            dma((4,)),
            dma,
            dma((8,)),
            dma((3, 5)),
            dma((3, 5)),
        ],
        compiler_params=pltpu.CompilerParams(
            collective_id=0, has_side_effects=True, vmem_limit_bytes=60 * MIB
        ),
        name="whole",
    )(codes, pos, neg, bank_codes, bank_emb, query_emb, positive_emb, head)


def emit_kernel(best_ref, grads_ref, sums_ref, ids_ref, dist_ref, qg_ref, pg_ref, hg_ref, square):
    square[...] = jnp.zeros((128, 128), jnp.int32)
    square[0:16, :] = best_ref[...]
    flat = square[...]
    ids_ref[...] = jnp.transpose((flat & 65535).astype(F32))[0:16, 0:16].astype(jnp.int32)
    dist_ref[...] = jnp.transpose((flat >> 16).astype(F32))[0:16, 0:16].astype(jnp.int32)
    qg_ref[...] = grads_ref[0:16]
    pg_ref[...] = grads_ref[16:32]
    hg_ref[...] = sums_ref[...]


def emit(best, grads, sums):
    vm = pl.BlockSpec(memory_space=pltpu.VMEM)
    return pl.pallas_call(
        emit_kernel,
        out_shape=(
            jax.ShapeDtypeStruct((16, 16), jnp.int32),
            jax.ShapeDtypeStruct((16, 16), jnp.int32),
            jax.ShapeDtypeStruct((16, 1024), BF16),
            jax.ShapeDtypeStruct((16, 1024), BF16),
            jax.ShapeDtypeStruct((8, 1024), F32),
        ),
        in_specs=[vm] * 3,
        out_specs=(vm,) * 5,
        scratch_shapes=[pltpu.VMEM((128, 128), jnp.int32)],
        name="emit",
    )(best, grads, sums)


def local(
    query_codes, positive_ids, negative_ids, bank_codes, bank_emb, query_emb, positive_emb, head
):
    return emit(
        *whole(
            query_codes, positive_ids.reshape(1, -1), negative_ids, bank_codes, bank_emb, query_emb, positive_emb, head
        )
    )


def solution(mesh):
    both = ("dp", "index")
    rows = P(both, None)
    return jax.shard_map(
        local,
        mesh=mesh,
        in_specs=(rows, P(both), rows, P("index", None), P("index", None), rows, rows, P()),
        out_specs=(rows,) * 5,
        check_vma=False,
    )
```

```python
import functools

import jax
import jax.numpy as jnp
from jax import lax
from jax.experimental import pallas as pl
from jax.experimental.pallas import tpu as pltpu
from jax.sharding import PartitionSpec as P

F32 = jnp.float32
BF16 = jnp.bfloat16
MESH = pl.DeviceIdType.MESH
MIB = 1 << 20
GROUP = 32
SIDE = 4
BIG = float(1 << 23)
LAST = (((1,), (1,)), ((), ()))


def iota(shape, dim):
    return lax.broadcasted_iota(jnp.int32, shape, dim)


def dot(a, b, dims=(((1,), (0,)), ((), ()))):
    return lax.dot_general(a, b, dims, preferred_element_type=F32)


def copy_to(src, dst, send_sem, recv_sem, device):
    return pltpu.make_async_remote_copy(
        src_ref=src,
        dst_ref=dst,
        send_sem=send_sem,
        recv_sem=recv_sem,
        device_id=device,
        device_id_type=MESH,
    )


def coords():
    z = lax.axis_index("dp")
    me = lax.axis_index("index")
    x = lax.div(me, 8)
    y = lax.rem(lax.div(me, 2), 4)
    c = lax.rem(me, 2)
    return z, me, x, y, c


def at(x, y, c):
    return x * 8 + y * 2 + c


OFFSETS = sorted(
    ((dx, dy, dc) for dx in range(4) for dy in range(4) for dc in range(2) if dx or dy or dc),
    key=lambda o: -(min(o[0], 4 - o[0]) + min(o[1], 4 - o[1])),
)


def peers(x, y, c):
    return [at(lax.rem(x + dx, 4), lax.rem(y + dy, 4), lax.rem(c + dc, 2)) for dx, dy, dc in OFFSETS]


def take(ref, sem):
    pltpu.make_async_copy(ref, ref, sem).wait()


def request_table(codes, pos_row, negatives):
    hi = jnp.floor(negatives * (1.0 / 256.0))
    lo = negatives - 256.0 * hi
    halves = jnp.concatenate([hi, lo], axis=0).astype(BF16)
    spread = jnp.where(iota((16, 256), 0) == (iota((16, 256), 1) & 15), 1.0, 0.0).astype(BF16)
    got = dot(halves, spread)
    ids = 256.0 * got[0:16] + got[16:32]
    ids = jnp.where(iota((16, 256), 0) == (iota((16, 256), 1) >> 4), ids, 0.0)
    id_row = jnp.sum(ids, axis=0, keepdims=True)
    owner_row = jnp.floor(id_row * (1.0 / 2048.0))
    owner_b = jnp.broadcast_to(owner_row, (256, 256))
    owner_t = jnp.transpose(owner_b)
    earlier = iota((256, 256), 0) < iota((256, 256), 1)
    same = jnp.where(owner_b == owner_t, 1.0, 0.0)
    rank = jnp.sum(jnp.where(earlier, same, 0.0), axis=0, keepdims=True)
    slot_row = jnp.where(rank < 7.0, owner_row * 8.0 + rank, 249.0 + rank)
    slot_b = jnp.broadcast_to(slot_row, (288, 256))
    hit = iota((288, 256), 0).astype(F32) == slot_b
    id_col = jnp.sum(jnp.where(hit, jnp.broadcast_to(id_row, (288, 256)) + 1.0, 0.0), axis=1, keepdims=True) - 1.0
    which = jnp.where(iota((256, 128), 1) == (iota((256, 128), 0) >> 4), 1.0, 0.0).astype(BF16)
    owned_by = dot(jnp.where(hit, 1.0, 0.0).astype(BF16), which)
    lane32 = iota((32, 128), 1)
    sub32 = iota((32, 128), 0)
    ext_row = jnp.sum(
        jnp.where(lane32 == sub32 + 96, jnp.broadcast_to(id_col[256:288], (32, 128)), 0.0), axis=0, keepdims=True
    )
    diagonal = iota((16, 16), 0) == iota((16, 16), 1)
    pos_col = jnp.sum(jnp.where(diagonal, jnp.broadcast_to(pos_row, (16, 16)), 0.0), axis=1, keepdims=True)
    lane16 = iota((16, 128), 1)
    rest = jnp.where(lane16 >= 96, jnp.broadcast_to(ext_row, (16, 128)), 0.0)
    rest = jnp.where(lane16 == 64, jnp.broadcast_to(pos_col, (16, 128)), rest)
    return id_col, owned_by, jnp.where(lane16 < 64, codes, rest)


def onehot_rows(rel, count):
    return jnp.where(
        jnp.broadcast_to(rel, (count, 2048)) == iota((count, 2048), 1).astype(F32), 1.0, 0.0
    ).astype(BF16)


def batcher(n):
    pairs = []
    p = 1
    while p < n:
        k = p
        while k >= 1:
            for j in range(k % p, n - k, 2 * k):
                for i in range(min(k, n - j - k)):
                    if (i + j) // (2 * p) == (i + j + k) // (2 * p):
                        pairs.append((i + j, i + j + k))
            k //= 2
        p *= 2
    return pairs


SORT16 = batcher(16)


def exchange(v, i, j):
    v[i], v[j] = jnp.minimum(v[i], v[j]), jnp.maximum(v[i], v[j])


def sort16(v):
    v = list(v)
    for i, j in SORT16:
        exchange(v, i, j)
    return v


def merge16(a, b):
    v = [jnp.minimum(a[i], b[15 - i]) for i in range(16)]
    for d in (8, 4, 2, 1):
        for i in range(16):
            if i & d == 0:
                exchange(v, i, i + d)
    return v


def sign_rows(table):
    hi = jnp.floor(table * (1.0 / 256.0))
    lo = table - 256.0 * hi
    both = jnp.concatenate([hi, lo], axis=1).astype(BF16)
    k = iota((1024, 256), 0)
    lane = iota((1024, 256), 1)
    source = (k >> 4) + jnp.where((k & 8) == 0, 128, 0)
    pick = jnp.where(lane == source, 1.0, 0.0).astype(BF16)
    byte = dot(pick, both, LAST).astype(jnp.int32)
    bit = byte & (1 << (iota((1024, 512), 0) & 7))
    signs = jnp.where(bit != 0, -1024.0, 1024.0).astype(BF16)
    lane16 = iota((16, 256), 1)
    weigh = jnp.where(lane16 == 64, 256.0, jnp.where(lane16 == 192, 1.0, 0.0)).astype(BF16)
    return signs, dot(weigh, both, LAST)


PORTIONS = ((0, 0, 4, (0, 1, 2)), (1, 0, 4, (1, 2, 0)), (2, 0, 4, (2, 0, 1)), (3, 0, 2, (0, 1, 2)), (3, 2, 2, (1, 0, 2)))
TAIL = (0, 1, 2, 3, 3)
STEPS = (2, 1, 3, 0)


def extents(p, stage):
    _, _, ys, order = PORTIONS[p]
    return [(a, ys if a == 2 else SIDE) for a in range(3) if a not in order[:stage]]


def split(v):
    high = v.astype(BF16)
    return high, (v - high.astype(F32)).astype(BF16)


def whole_kernel(
    qcodes_hbm, pos_hbm, neg_hbm, codes_hbm, bank_hbm, query_hbm, positive_hbm, head_hbm,
    ids_ref, dist_ref, qg_ref, pg_ref, hg_ref,
    qcodes, pos_in, neg_in,
    bank, codes, head, pay, owned, out_buf, in_buf, bsend, brecv, esend, eown, ecore, s1, r2a, r2b, s2a, s2b, r3a, r3b,
    signs, keys, pos, shard_best, crecv, packed, square, xs, dz, unit, inv, u_hi, u_lo,
    hs, core_in, parts, in1, mid, in2, tail, in3,
    load_sem, small_sem, p_sem, b_sem, t_sem, c_sem, x_send, x_recv, h_send, h_recv, r_send, r_recv,
):
    z, me, x, y, c = coords()
    others = peers(x, y, c)
    partner = (z, at(x, y, 1 - c))
    load_bank = pltpu.make_async_copy(bank_hbm, bank, load_sem.at[0])
    load_codes = pltpu.make_async_copy(codes_hbm, codes, load_sem.at[1])
    load_head = pltpu.make_async_copy(head_hbm, head, load_sem.at[2])
    small = [
        pltpu.make_async_copy(source, target, small_sem.at[i])
        for i, (source, target) in enumerate(
            (
                (neg_hbm, neg_in),
                (pos_hbm, pos_in),
                (qcodes_hbm, qcodes),
                (query_hbm, xs.at[pl.ds(0, 16)]),
                (positive_hbm, xs.at[pl.ds(16, 16)]),
            )
        )
    ]
    for load in small:
        load.start()
    load_bank.start()
    barrier = pltpu.get_barrier_semaphore()
    for peer in others:
        pl.semaphore_signal(barrier, inc=1, device_id=(z, peer), device_id_type=MESH)
    for k in range(1, SIDE):
        pl.semaphore_signal(barrier, inc=1, device_id=(lax.rem(z + k, SIDE), me), device_id_type=MESH)
    load_codes.start()
    load_head.start()

    pay[...] = jnp.zeros((16, 128), F32)
    for load in small[:3]:
        load.wait()
    pay[:, 0:64] = qcodes[...].astype(F32)
    id_col, owned_by, common = request_table(pay[...], pos_in[...].astype(F32), neg_in[...].astype(F32))
    owned[...] = owned_by
    lane = iota((32, 8, 128), 2)
    base_cols = jnp.broadcast_to(id_col[0:256], (256, 128)).reshape(32, 8, 128)
    out_buf[:, 0:8, :] = jnp.where(lane == 65, base_cols, jnp.broadcast_to(common[None, 0:8], (32, 8, 128)))
    out_buf[:, 8:16, :] = jnp.broadcast_to(common[None, 8:16], (32, 8, 128))
    pl.semaphore_wait(barrier, len(others) + SIDE - 1)
    for peer in others:
        copy_to(out_buf.at[peer], in_buf.at[me], p_sem.at[0], p_sem.at[1], (z, peer)).start()
    in_buf[me] = out_buf[me]

    for load in small[3:]:
        load.wait()

    def project(start, count):
        rows = slice(start, start + count)
        zed = dot(xs[rows], head[...])
        scale = 1.0 / jnp.sqrt(jnp.sum(zed * zed, axis=1, keepdims=True) + 1e-6)
        u = zed * scale
        unit[rows] = u
        inv[rows] = jnp.broadcast_to(scale, (count, 128))
        high, low = split(u)
        u_hi[rows] = high
        u_lo[rows] = low

    load_head.wait()
    project(0, 32)
    load_bank.wait()
    take(in_buf.at[pl.ds(0, GROUP - 1)], p_sem.at[1])

    first = (me * 2048).astype(F32)
    asked = in_buf[:, 0:8, :].reshape(256, 128)
    base_rel = jnp.sum(jnp.where(iota((256, 128), 1) == 65, asked, 0.0), axis=1, keepdims=True) - first
    hot = onehot_rows(base_rel, 256)
    for h in range(2):
        part = dot(hot, bank[:, h * 512 : (h + 1) * 512])
        bsend[:, 8 * h : 8 * h + 8, :] = part.reshape(32, 8, 512).astype(BF16)
    for peer in others:
        copy_to(bsend.at[peer], brecv.at[me], b_sem.at[0], b_sem.at[1], (z, peer)).start()
    brecv[me] = bsend[me]

    def extras(core):
        rows = in_buf[:, 0:1, :].reshape(16, 2, 1, 128)
        mine = jnp.where(core == 0, rows[:, 0], rows[:, 1])
        wide = jnp.broadcast_to(mine, (16, 32, 128))
        keep = iota((16, 32, 128), 2) == iota((16, 32, 128), 1) + 96
        rel = jnp.sum(jnp.where(keep, wide, 0.0), axis=2, keepdims=True).reshape(512, 1) - first
        return dot(onehot_rows(rel, 512), bank[...])

    esend[...] = extras(1 - c).reshape(16, 32, 1024).astype(BF16)
    core_copy = copy_to(esend, ecore, c_sem.at[0], c_sem.at[1], partner)
    core_copy.start()
    eown[...] = extras(c).reshape(16, 32, 1024).astype(BF16)
    core_copy.wait_recv()
    s1[...] = (eown[...].astype(F32) + ecore[...].astype(F32)).astype(BF16).reshape(4, 4, 32, 1024)

    left, right = pl.ds(0, 512), pl.ds(512, 512)
    for j in (2, 1, 3, 0):
        xj, yj = lax.rem(x + j, SIDE), lax.rem(y + j, SIDE)
        for k in (2, 1, 3):
            xk, yk = lax.rem(x + k, SIDE), lax.rem(y + k, SIDE)
            copy_to(
                s1.at[xk, yj, :, left], r2a.at[j, k - 1], x_send.at[0, j], x_recv.at[0, j], (z, at(xk, y, c))
            ).start()
            copy_to(
                s1.at[xj, yk, :, right], r2b.at[j, k - 1], x_send.at[1, j], x_recv.at[1, j], (z, at(x, yk, c))
            ).start()

    signs_v, pos_v = sign_rows(in_buf[...].reshape(512, 128))
    signs[...] = signs_v
    pos[...] = pos_v[0:8] - first
    load_codes.wait()

    def product(m, carry):
        at_row = pl.multiple_of(m * 256, 256)
        keys[pl.ds(at_row, 256), :] = dot(codes[pl.ds(at_row, 256), :], signs[...])
        return carry

    lax.fori_loop(0, 8, product, 0)
    sub = iota((8, 128), 0)

    def select(t):
        lanes = slice(t * 128, (t + 1) * 128)
        wanted = pos[:, lanes]

        def load16(g):
            out = []
            for i in range(16):
                row = pl.multiple_of(g * 128 + i * 8, 8)
                p = (sub + (g * 128 + i * 8)).astype(F32)
                key = keys[pl.ds(row, 8), lanes] + (p + float(1 << 20))
                out.append(jnp.where(p == wanted, BIG, key))
            return out

        def step(g, best):
            return tuple(merge16(best, sort16(load16(g))))

        best = lax.fori_loop(1, 16, step, tuple(sort16(load16(0))))
        for d in (4, 2, 1):
            best = merge16(best, [pltpu.roll(b, d, 0) for b in best])
        for i in range(16):
            shard_best[t, i : i + 1, :] = best[i][0:1, :]

    def total(own, got):
        t = own.astype(F32)
        for k in range(SIDE - 1):
            t = t + got[k].astype(F32)
        return t

    def pass_on(j):
        xj, yj = lax.rem(x + j, SIDE), lax.rem(y + j, SIDE)
        take(r2a.at[j], x_recv.at[0, j])
        s2a[j] = total(s1[x, yj, :, 0:512], r2a.at[j]).astype(BF16)
        copy_to(s2a.at[j], r3a.at[j - 1], x_send.at[0, 4], x_recv.at[0, 4], (z, at(x, yj, c))).start()
        take(r2b.at[j], x_recv.at[1, j])
        s2b[j] = total(s1[xj, y, :, 512:1024], r2b.at[j]).astype(BF16)
        copy_to(s2b.at[j], r3b.at[j - 1], x_send.at[1, 4], x_recv.at[1, 4], (z, at(xj, y, c))).start()

    select(0)
    select(1)
    pass_on(2)
    select(2)
    pass_on(1)
    select(3)
    pass_on(3)
    for peer in others:
        copy_to(shard_best.at[lax.div(peer, 8)], crecv.at[me], t_sem.at[0], t_sem.at[1], (z, peer)).start()
    crecv[me] = shard_best[lax.div(me, 8)]

    take(brecv.at[pl.ds(0, GROUP - 1)], b_sem.at[1])
    got = brecv[...].astype(F32)
    xs[32:288, 0:512] = got[:, 0:8].reshape(256, 512).astype(BF16)
    xs[32:288, 512:1024] = got[:, 8:16].reshape(256, 512).astype(BF16)
    project(32, 256)
    take(r2a.at[0], x_recv.at[0, 0])
    own_left = total(s1[x, y, :, 0:512], r2a.at[0])
    take(r2b.at[0], x_recv.at[1, 0])
    own_right = total(s1[x, y, :, 512:1024], r2b.at[0])
    take(r3a, x_recv.at[0, 4])
    xs[288:320, 0:512] = total(own_left, r3a).astype(BF16)
    take(r3b, x_recv.at[1, 4])
    xs[288:320, 512:1024] = total(own_right, r3b).astype(BF16)
    project(288, 32)

    q_hi, q_lo = u_hi[0:16], u_lo[0:16]
    c_hi, c_lo = u_hi[16:320], u_lo[16:320]
    logits = 50.0 * (dot(c_hi, q_hi, LAST) + (dot(c_lo, q_hi, LAST) + dot(c_hi, q_lo, LAST)))
    own_pos = jnp.where(iota((16, 16), 0) == iota((16, 16), 1), 1.0, 0.0)
    mask = jnp.concatenate([own_pos, owned[:, 0:16]], axis=0)
    weights = jnp.where(mask > 0.5, jnp.exp(jnp.where(mask > 0.5, logits, 0.0)), 0.0)
    probs = weights / jnp.sum(weights, axis=0, keepdims=True)
    slopes = probs - jnp.concatenate([own_pos, jnp.zeros((288, 16), F32)], axis=0)
    s_hi, s_lo = split(slopes)
    firsts = (((0,), (0,)), ((), ()))
    du = 50.0 * (dot(s_hi, c_hi, firsts) + (dot(s_lo, c_hi, firsts) + dot(s_hi, c_lo, firsts)))
    q_unit = unit[0:16]
    dz[0:16] = ((du - q_unit * jnp.sum(q_unit * du, axis=1, keepdims=True)) * inv[0:16, 0:1]).astype(BF16)
    inv_c = inv[16:320, 0:1]
    k1_hi, k1_lo = split(slopes * (50.0 * inv_c))
    k2 = jnp.sum(slopes * logits, axis=1, keepdims=True) * inv_c
    along = dot(k1_hi, q_hi) + (dot(k1_lo, q_hi) + dot(k1_hi, q_lo))
    dz[16:320] = (along - unit[16:320] * k2).astype(BF16)

    def h_copy(i):
        zz = lax.rem(z + STEPS[i], SIDE)
        return copy_to(hs.at[1 - c, zz], core_in.at[zz], h_send, h_recv.at[i], partner)

    def grow(i):
        zz = lax.rem(z + STEPS[i], SIDE)
        part = dot(xs[:, pl.ds(pl.multiple_of(zz * 256, 256), 256)], dz[...], firsts).reshape(32, 8, 1024)
        part = jnp.concatenate([part[:, :, 0:512], part[:, :, 512:1024]], axis=1).astype(BF16)
        part = part.reshape(4, 4, 2, 16, 512)
        for core in range(2):
            hs[core, zz] = part[:, :, core]
        h_copy(i).start()

    place = (z, x, y)

    def device(axis, to):
        where = [z, x, y]
        where[axis] = to
        return (where[0], at(where[1], where[2], c))

    def first_from(p, to):
        tile, y0, ys, order = PORTIONS[p]
        index = [slice(None), slice(None), pl.ds(y0, ys)]
        if order[0] == 2:
            index[2] = to
        else:
            index[order[0]] = to
        return (*index, slice(None), pl.ds(tile * 128, 128))

    def gather_core(i):
        zz = lax.rem(z + STEPS[i], SIDE)
        h_copy(i).wait_recv()
        parts[zz] = (hs[c, zz].astype(F32) + core_in[zz].astype(F32)).astype(BF16)
        for p in (3, 4, 0, 1, 2):
            tile, y0, ys, order = PORTIONS[p]
            lanes = pl.ds(tile * 128, 128)
            if order[0] == 0:
                moves = [(zz, parts.at[zz, :, pl.ds(y0, ys), :, lanes], in1[p].at[STEPS[i] - 1])] if STEPS[i] else []
            else:
                moves = []
                for k in (2, 1, 3):
                    to = lax.rem(place[order[0]] + k, SIDE)
                    if order[0] == 1:
                        source = parts.at[zz, to, pl.ds(y0, ys), :, lanes]
                    else:
                        source = parts.at[zz, :, to, :, lanes]
                    moves.append((to, source, in1[p].at[k - 1, zz]))
            for to, source, target in moves:
                copy_to(source, target, r_send.at[0, p], r_recv.at[0, p], device(order[0], to)).start()

    grow(0)
    grow(1)
    gather_core(0)
    grow(2)
    gather_core(1)
    grow(3)
    gather_core(2)
    gather_core(3)

    grads = dot(dz[0:32], head[...], LAST).astype(BF16)
    qg_ref[...] = grads[0:16]
    pg_ref[...] = grads[16:32]

    take(crecv.at[pl.ds(0, GROUP - 1)], t_sem.at[1])
    lane = iota((16, 128), 1)
    packed[...] = jnp.full((8, 16, 128), 2147483647, jnp.int32)
    mine = lax.rem(me, 8)
    for g in range(4):
        merged = jnp.zeros((16, 128), jnp.int32)
        for s in range(8):
            key = crecv[g * 8 + s].astype(jnp.int32)
            key = ((key >> 11) << 16) + (key & 2047) + (g * 8 + s) * 2048
            key = pltpu.roll(key, lax.rem((s - mine + 8) * 16, 128), 1)
            merged = jnp.where((lane >> 4) == s, key, merged)
        packed[g] = merged
    best = [packed[:, i, :] for i in range(16)]
    for d in (64, 32, 16):
        best = merge16(best, [pltpu.roll(b, d, 1) for b in best])
    for d in (6, 7):
        best = merge16(best, [pltpu.roll(b, d, 0) for b in best])
    square[...] = jnp.zeros((128, 128), jnp.int32)
    for i in range(16):
        square[i : i + 1, :] = best[i][0:1, :]
    flat = square[...]
    ids_ref[...] = jnp.transpose((flat & 65535).astype(F32))[0:16, 0:16].astype(jnp.int32)
    dist_ref[...] = jnp.transpose((flat >> 16).astype(F32))[0:16, 0:16].astype(jnp.int32)

    def pick(p, stage, to):
        axis = PORTIONS[p][3][stage]
        return tuple(to if a == axis else slice(None) for a, _ in extents(p, stage))

    for p in (1, 2, 4, 0, 3):
        axis = PORTIONS[p][3][0]
        take(in1[p], r_recv.at[0, p])
        mid[p][...] = total(parts[first_from(p, place[axis])], in1[p]).astype(BF16)
        axis = PORTIONS[p][3][1]
        for k in (2, 1, 3):
            to = lax.rem(place[axis] + k, SIDE)
            copy_to(
                mid[p].at[pick(p, 1, to)], in2[p].at[k - 1], r_send.at[1, p], r_recv.at[1, p], device(axis, to)
            ).start()
    for p in (1, 2, 4, 0, 3):
        axis = PORTIONS[p][3][1]
        take(in2[p], r_recv.at[1, p])
        _, y0, ys, order = PORTIONS[p]
        sums = total(mid[p][pick(p, 1, place[axis])], in2[p]).astype(BF16)
        if TAIL[p] == 3:
            tail[3, y0 : y0 + ys] = sums
        else:
            tail[p] = sums
        if p == 4:
            continue
        q = TAIL[p]
        axis = order[2]
        for k in (2, 1, 3):
            to = lax.rem(place[axis] + k, SIDE)
            copy_to(
                tail.at[q, to], in3.at[q, k - 1], r_send.at[2, q], r_recv.at[2, q], device(axis, to)
            ).start()
    for q in range(4):
        take(in3.at[q], r_recv.at[2, q])
        out = total(tail[q, place[PORTIONS[q][3][2]]], in3.at[q])
        hg_ref[:, q * 128 : (q + 1) * 128] = out[0:8]
        hg_ref[:, 512 + q * 128 : 512 + (q + 1) * 128] = out[8:16]

    take(out_buf.at[pl.ds(0, GROUP - 1)], p_sem.at[0])
    take(bsend.at[pl.ds(0, GROUP - 1)], b_sem.at[0])
    take(crecv.at[pl.ds(0, GROUP - 1)], t_sem.at[0])
    core_copy.wait_send()
    for j in range(SIDE):
        take(r2a.at[j], x_send.at[0, j])
        take(r2b.at[j], x_send.at[1, j])
    take(r3a, x_send.at[0, 4])
    take(r3b, x_send.at[1, 4])
    take(core_in, h_send)
    for p in range(5):
        take(in1[p], r_send.at[0, p])
        take(in2[p], r_send.at[1, p])
    for q in range(4):
        take(in3.at[q], r_send.at[2, q])


def whole(codes, pos, neg, bank_codes, bank_emb, query_emb, positive_emb, head):
    vm = pl.BlockSpec(memory_space=pltpu.VMEM)
    anywhere = pl.BlockSpec(memory_space=pl.ANY)
    dma = pltpu.SemaphoreType.DMA
    block = (16, 128)

    def by_portion(stage, lead):
        return [pltpu.VMEM((*lead, *(n for _, n in extents(p, stage)), *block), BF16) for p in range(5)]

    return pl.pallas_call(
        whole_kernel,
        out_shape=(
            jax.ShapeDtypeStruct((16, 16), jnp.int32),
            jax.ShapeDtypeStruct((16, 16), jnp.int32),
            jax.ShapeDtypeStruct((16, 1024), BF16),
            jax.ShapeDtypeStruct((16, 1024), BF16),
            jax.ShapeDtypeStruct((8, 1024), F32),
        ),
        in_specs=[anywhere] * 8,
        out_specs=(vm,) * 5,
        scratch_shapes=[
            pltpu.VMEM((16, 64), jnp.int32),
            pltpu.VMEM((1, 16), jnp.int32),
            pltpu.VMEM((16, 16), jnp.int32),
            pltpu.VMEM((2048, 1024), BF16),
            pltpu.VMEM((2048, 1024), BF16),
            pltpu.VMEM((1024, 1024), BF16),
            pltpu.VMEM((16, 128), F32),
            pltpu.VMEM((288, 128), F32),
            pltpu.VMEM((32, 16, 128), F32),
            pltpu.VMEM((32, 16, 128), F32),
            pltpu.VMEM((32, 16, 512), BF16),
            pltpu.VMEM((32, 16, 512), BF16),
            pltpu.VMEM((16, 32, 1024), BF16),
            pltpu.VMEM((16, 32, 1024), BF16),
            pltpu.VMEM((16, 32, 1024), BF16),
            pltpu.VMEM((4, 4, 32, 1024), BF16),
            pltpu.VMEM((4, 3, 32, 512), BF16),
            pltpu.VMEM((4, 3, 32, 512), BF16),
            pltpu.VMEM((4, 32, 512), BF16),
            pltpu.VMEM((4, 32, 512), BF16),
            pltpu.VMEM((3, 32, 512), BF16),
            pltpu.VMEM((3, 32, 512), BF16),
            pltpu.VMEM((1024, 512), BF16),
            pltpu.VMEM((2048, 512), F32),
            pltpu.VMEM((8, 512), F32),
            pltpu.VMEM((4, 16, 128), F32),
            pltpu.VMEM((32, 16, 128), F32),
            pltpu.VMEM((8, 16, 128), jnp.int32),
            pltpu.VMEM((128, 128), jnp.int32),
            pltpu.VMEM((320, 1024), BF16),
            pltpu.VMEM((320, 1024), BF16),
            pltpu.VMEM((320, 1024), F32),
            pltpu.VMEM((320, 128), F32),
            pltpu.VMEM((320, 1024), BF16),
            pltpu.VMEM((320, 1024), BF16),
            pltpu.VMEM((2, 4, 4, 4, 16, 512), BF16),
            pltpu.VMEM((4, 4, 4, 16, 512), BF16),
            pltpu.VMEM((4, 4, 4, 16, 512), BF16),
            by_portion(1, (3,)),
            by_portion(1, ()),
            by_portion(2, (3,)),
            pltpu.VMEM((4, 4, *block), BF16),
            pltpu.VMEM((4, 3, *block), BF16),
            dma((3,)),
            dma((5,)),
            dma((2,)),
            dma((2,)),
            dma((2,)),
            dma((2,)),
            dma((2, 5)),
            dma((2, 5)),
            dma,
            dma((4,)),
            dma((3, 5)),
            dma((3, 5)),
        ],
        compiler_params=pltpu.CompilerParams(
            collective_id=0, has_side_effects=True, vmem_limit_bytes=60 * MIB
        ),
        name="whole",
    )(codes, pos, neg, bank_codes, bank_emb, query_emb, positive_emb, head)


def emit_kernel(*refs):
    sources, targets, sem = refs[0:5], refs[5:10], refs[10]
    copies = [pltpu.make_async_copy(a, b, sem.at[i]) for i, (a, b) in enumerate(zip(sources, targets))]
    for copy in copies:
        copy.start()
    for copy in copies:
        copy.wait()


def emit(*arrays):
    anywhere = pl.BlockSpec(memory_space=pl.ANY)
    return pl.pallas_call(
        emit_kernel,
        out_shape=tuple(jax.ShapeDtypeStruct(a.shape, a.dtype) for a in arrays),
        in_specs=[anywhere] * 5,
        out_specs=(anywhere,) * 5,
        scratch_shapes=[pltpu.SemaphoreType.DMA((5,))],
        name="emit",
    )(*arrays)


def local(
    query_codes, positive_ids, negative_ids, bank_codes, bank_emb, query_emb, positive_emb, head
):
    return emit(
        *whole(
            query_codes, positive_ids.reshape(1, -1), negative_ids, bank_codes, bank_emb, query_emb, positive_emb, head
        )
    )


def solution(mesh):
    both = ("dp", "index")
    rows = P(both, None)
    return jax.shard_map(
        local,
        mesh=mesh,
        in_specs=(rows, P(both), rows, P("index", None), P("index", None), rows, rows, P()),
        out_specs=(rows,) * 5,
        check_vma=False,
    )
```

```python
import functools

import jax
import jax.numpy as jnp
from jax import lax
from jax.experimental import pallas as pl
from jax.experimental.pallas import tpu as pltpu
from jax.sharding import PartitionSpec as P

F32 = jnp.float32
BF16 = jnp.bfloat16
MESH = pl.DeviceIdType.MESH
MIB = 1 << 20
GROUP = 32
SIDE = 4
BIG = float(1 << 23)
LAST = (((1,), (1,)), ((), ()))


def iota(shape, dim):
    return lax.broadcasted_iota(jnp.int32, shape, dim)


def dot(a, b, dims=(((1,), (0,)), ((), ()))):
    return lax.dot_general(a, b, dims, preferred_element_type=F32)


def copy_to(src, dst, send_sem, recv_sem, device):
    return pltpu.make_async_remote_copy(
        src_ref=src,
        dst_ref=dst,
        send_sem=send_sem,
        recv_sem=recv_sem,
        device_id=device,
        device_id_type=MESH,
    )


def coords():
    z = lax.axis_index("dp")
    me = lax.axis_index("index")
    x = lax.div(me, 8)
    y = lax.rem(lax.div(me, 2), 4)
    c = lax.rem(me, 2)
    return z, me, x, y, c


def at(x, y, c):
    return x * 8 + y * 2 + c


OFFSETS = sorted(
    ((dx, dy, dc) for dx in range(4) for dy in range(4) for dc in range(2) if dx or dy or dc),
    key=lambda o: -(min(o[0], 4 - o[0]) + min(o[1], 4 - o[1])),
)


def peers(x, y, c):
    return [at(lax.rem(x + dx, 4), lax.rem(y + dy, 4), lax.rem(c + dc, 2)) for dx, dy, dc in OFFSETS]


def take(ref, sem):
    pltpu.make_async_copy(ref, ref, sem).wait()


def request_table(pos_row, negatives):
    hi = jnp.floor(negatives * (1.0 / 256.0))
    lo = negatives - 256.0 * hi
    halves = jnp.concatenate([hi, lo], axis=0).astype(BF16)
    spread = jnp.where(iota((16, 256), 0) == (iota((16, 256), 1) & 15), 1.0, 0.0).astype(BF16)
    got = dot(halves, spread)
    ids = 256.0 * got[0:16] + got[16:32]
    ids = jnp.where(iota((16, 256), 0) == (iota((16, 256), 1) >> 4), ids, 0.0)
    id_row = jnp.sum(ids, axis=0, keepdims=True)
    owner_row = jnp.floor(id_row * (1.0 / 2048.0))
    owner_b = jnp.broadcast_to(owner_row, (256, 256))
    owner_t = jnp.transpose(owner_b)
    earlier = iota((256, 256), 0) < iota((256, 256), 1)
    same = jnp.where(owner_b == owner_t, 1.0, 0.0)
    rank = jnp.sum(jnp.where(earlier, same, 0.0), axis=0, keepdims=True)
    slot_row = jnp.where(rank < 7.0, owner_row * 8.0 + rank, 249.0 + rank)
    slot_b = jnp.broadcast_to(slot_row, (288, 256))
    hit = iota((288, 256), 0).astype(F32) == slot_b
    id_col = jnp.sum(jnp.where(hit, jnp.broadcast_to(id_row, (288, 256)) + 1.0, 0.0), axis=1, keepdims=True) - 1.0
    which = jnp.where(iota((256, 128), 1) == (iota((256, 128), 0) >> 4), 1.0, 0.0).astype(BF16)
    owned_by = dot(jnp.where(hit, 1.0, 0.0).astype(BF16), which)
    lane32 = iota((32, 128), 1)
    sub32 = iota((32, 128), 0)
    ext_row = jnp.sum(
        jnp.where(lane32 == sub32 + 96, jnp.broadcast_to(id_col[256:288], (32, 128)), 0.0), axis=0, keepdims=True
    )
    return id_col, owned_by, ext_row


def onehot_rows(rel, count):
    return jnp.where(
        jnp.broadcast_to(rel, (count, 2048)) == iota((count, 2048), 1).astype(F32), 1.0, 0.0
    ).astype(BF16)


def batcher(n):
    pairs = []
    p = 1
    while p < n:
        k = p
        while k >= 1:
            for j in range(k % p, n - k, 2 * k):
                for i in range(min(k, n - j - k)):
                    if (i + j) // (2 * p) == (i + j + k) // (2 * p):
                        pairs.append((i + j, i + j + k))
            k //= 2
        p *= 2
    return pairs


SORT16 = batcher(16)


def exchange(v, i, j):
    v[i], v[j] = jnp.minimum(v[i], v[j]), jnp.maximum(v[i], v[j])


def sort16(v):
    v = list(v)
    for i, j in SORT16:
        exchange(v, i, j)
    return v


def merge16(a, b):
    v = [jnp.minimum(a[i], b[15 - i]) for i in range(16)]
    for d in (8, 4, 2, 1):
        for i in range(16):
            if i & d == 0:
                exchange(v, i, i + d)
    return v


def sign_rows(table):
    hi = jnp.floor(table * (1.0 / 256.0))
    lo = table - 256.0 * hi
    both = jnp.concatenate([hi, lo], axis=1).astype(BF16)
    k = iota((1024, 256), 0)
    lane = iota((1024, 256), 1)
    source = (k >> 4) + jnp.where((k & 8) == 0, 128, 0)
    pick = jnp.where(lane == source, 1.0, 0.0).astype(BF16)
    byte = dot(pick, both, LAST).astype(jnp.int32)
    bit = byte & (1 << (iota((1024, 512), 0) & 7))
    return jnp.where(bit != 0, -1024.0, 1024.0).astype(BF16)


PORTIONS = ((0, 0, 4, (0, 1, 2)), (1, 0, 4, (1, 2, 0)), (2, 0, 4, (2, 0, 1)), (3, 0, 2, (0, 1, 2)), (3, 2, 2, (1, 0, 2)))
TAIL = (0, 1, 2, 3, 3)
STEPS = (2, 1, 3, 0)


def extents(p, stage):
    _, _, ys, order = PORTIONS[p]
    return [(a, ys if a == 2 else SIDE) for a in range(3) if a not in order[:stage]]


def split(v):
    high = v.astype(BF16)
    return high, (v - high.astype(F32)).astype(BF16)


def whole_kernel(
    qcodes_hbm, pos_hbm, neg_hbm, codes_hbm, bank_hbm, query_hbm, positive_hbm, head_hbm,
    out_hbm,
    qcodes, pos_in, neg_in, out_v,
    bank, codes, head, pay, owned, out_buf, in_buf, code_out, code_in, bsend, brecv, esend, eown, ecore, s1, r2a, r2b, s2a, s2b, r3a, r3b,
    signs, keys, pos, shard_best, crecv, packed, square, xs, dz, raw, unit, inv, u_hi, u_lo,
    hs, core_in, parts, in1, mid, in2, tail, in3,
    load_sem, small_sem, p_sem, q_sem, b_sem, t_sem, c_sem, x_send, x_recv, h_send, h_recv, r_send, r_recv,
):
    z, me, x, y, c = coords()
    others = peers(x, y, c)
    partner = (z, at(x, y, 1 - c))
    load_bank = pltpu.make_async_copy(bank_hbm, bank, load_sem.at[0])
    load_codes = pltpu.make_async_copy(codes_hbm, codes, load_sem.at[1])
    load_head = pltpu.make_async_copy(head_hbm, head, load_sem.at[2])
    small = [
        pltpu.make_async_copy(source, target, small_sem.at[i])
        for i, (source, target) in enumerate(
            (
                (neg_hbm, neg_in),
                (pos_hbm, pos_in),
                (qcodes_hbm, qcodes),
                (query_hbm, xs.at[pl.ds(0, 16)]),
                (positive_hbm, xs.at[pl.ds(16, 16)]),
            )
        )
    ]
    for load in small:
        load.start()
    load_bank.start()
    barrier = pltpu.get_barrier_semaphore()
    for peer in others:
        pl.semaphore_signal(barrier, inc=1, device_id=(z, peer), device_id_type=MESH)
    for k in range(1, SIDE):
        pl.semaphore_signal(barrier, inc=1, device_id=(lax.rem(z + k, SIDE), me), device_id_type=MESH)
    load_codes.start()
    load_head.start()

    for load in small[:3]:
        load.wait()
    pay[...] = jnp.zeros((8, 128), F32)
    pay[:, 64:80] = jnp.broadcast_to(pos_in[...].astype(F32), (8, 16))
    code_out[...] = jnp.zeros((16, 128), F32)
    code_out[:, 0:64] = qcodes[...].astype(F32)
    id_col, owned_by, ext_row = request_table(pos_in[...].astype(F32), neg_in[...].astype(F32))
    owned[...] = owned_by
    lane8 = iota((8, 128), 1)
    common = jnp.where(lane8 >= 96, jnp.broadcast_to(ext_row, (8, 128)), pay[...])
    base_cols = jnp.broadcast_to(id_col[0:256], (256, 128)).reshape(32, 8, 128)
    out_buf[...] = jnp.where(iota((32, 8, 128), 2) == 0, base_cols, jnp.broadcast_to(common[None], (32, 8, 128)))
    pl.semaphore_wait(barrier, len(others) + SIDE - 1)
    for peer in others:
        copy_to(out_buf.at[peer], in_buf.at[me], p_sem.at[0], p_sem.at[1], (z, peer)).start()
    for peer in others:
        copy_to(code_out, code_in.at[me], q_sem.at[0], q_sem.at[1], (z, peer)).start()
    in_buf[me] = out_buf[me]
    code_in[me] = code_out[...]

    for load in small[3:]:
        load.wait()

    def project(start, count):
        rows = slice(start, start + count)
        zed = dot(xs[rows], head[...])
        scale = 1.0 / jnp.sqrt(jnp.sum(zed * zed, axis=1, keepdims=True) + 1e-6)
        u = zed * scale
        unit[rows] = u
        inv[rows] = jnp.broadcast_to(scale, (count, 128))
        high, low = split(u)
        u_hi[rows] = high
        u_lo[rows] = low

    load_head.wait()
    project(0, 32)
    load_bank.wait()
    take(in_buf.at[pl.ds(0, GROUP - 1)], p_sem.at[1])

    first = (me * 2048).astype(F32)
    asked = in_buf[...].reshape(256, 128)
    base_rel = jnp.sum(jnp.where(iota((256, 128), 1) == 0, asked, 0.0), axis=1, keepdims=True) - first
    hot = onehot_rows(base_rel, 256)
    for h in range(2):
        part = dot(hot, bank[:, h * 512 : (h + 1) * 512])
        bsend[:, 8 * h : 8 * h + 8, :] = part.reshape(32, 8, 512).astype(BF16)
    for peer in others:
        copy_to(bsend.at[peer], brecv.at[me], b_sem.at[0], b_sem.at[1], (z, peer)).start()
    brecv[me] = bsend[me]

    def extras(core):
        rows = in_buf[:, 0:1, :].reshape(16, 2, 1, 128)
        mine = jnp.where(core == 0, rows[:, 0], rows[:, 1])
        wide = jnp.broadcast_to(mine, (16, 32, 128))
        keep = iota((16, 32, 128), 2) == iota((16, 32, 128), 1) + 96
        rel = jnp.sum(jnp.where(keep, wide, 0.0), axis=2, keepdims=True).reshape(512, 1) - first
        return dot(onehot_rows(rel, 512), bank[...])

    esend[...] = extras(1 - c).reshape(16, 32, 1024).astype(BF16)
    core_copy = copy_to(esend, ecore, c_sem.at[0], c_sem.at[1], partner)
    core_copy.start()
    eown[...] = extras(c).reshape(16, 32, 1024).astype(BF16)
    core_copy.wait_recv()
    s1[...] = (eown[...].astype(F32) + ecore[...].astype(F32)).astype(BF16).reshape(4, 4, 32, 1024)

    left, right = pl.ds(0, 512), pl.ds(512, 512)
    for j in (2, 1, 3, 0):
        xj, yj = lax.rem(x + j, SIDE), lax.rem(y + j, SIDE)
        for k in (2, 1, 3):
            xk, yk = lax.rem(x + k, SIDE), lax.rem(y + k, SIDE)
            copy_to(
                s1.at[xk, yj, :, left], r2a.at[j, k - 1], x_send.at[0, j], x_recv.at[0, j], (z, at(xk, y, c))
            ).start()
            copy_to(
                s1.at[xj, yk, :, right], r2b.at[j, k - 1], x_send.at[1, j], x_recv.at[1, j], (z, at(x, yk, c))
            ).start()

    take(code_in.at[pl.ds(0, GROUP - 1)], q_sem.at[1])
    signs[...] = sign_rows(code_in[...].reshape(512, 128))
    lane8 = iota((8, 128), 1)
    for t in range(4):
        row = jnp.zeros((8, 128), F32)
        for i in range(8):
            ids = pltpu.roll(in_buf[8 * t + i], (16 * i + 64) % 128, 1)
            row = jnp.where((lane8 >> 4) == i, ids, row)
        pos[:, t * 128 : (t + 1) * 128] = row - first
    load_codes.wait()

    def product(m, carry):
        at_row = pl.multiple_of(m * 256, 256)
        keys[pl.ds(at_row, 256), :] = dot(codes[pl.ds(at_row, 256), :], signs[...])
        return carry

    lax.fori_loop(0, 8, product, 0)
    sub = iota((8, 128), 0)

    def select(t):
        lanes = slice(t * 128, (t + 1) * 128)
        wanted = pos[:, lanes]

        def load16(g):
            out = []
            for i in range(16):
                row = pl.multiple_of(g * 128 + i * 8, 8)
                p = (sub + (g * 128 + i * 8)).astype(F32)
                key = keys[pl.ds(row, 8), lanes] + (p + float(1 << 20))
                out.append(jnp.where(p == wanted, BIG, key))
            return out

        def step(g, best):
            return tuple(merge16(best, sort16(load16(g))))

        best = lax.fori_loop(1, 16, step, tuple(sort16(load16(0))))
        for d in (4, 2, 1):
            best = merge16(best, [pltpu.roll(b, d, 0) for b in best])
        for i in range(16):
            shard_best[t, i : i + 1, :] = best[i][0:1, :]

    def total(own, got):
        t = own.astype(F32)
        for k in range(SIDE - 1):
            t = t + got[k].astype(F32)
        return t

    def pass_on(j):
        xj, yj = lax.rem(x + j, SIDE), lax.rem(y + j, SIDE)
        take(r2a.at[j], x_recv.at[0, j])
        s2a[j] = total(s1[x, yj, :, 0:512], r2a.at[j]).astype(BF16)
        copy_to(s2a.at[j], r3a.at[j - 1], x_send.at[0, 4], x_recv.at[0, 4], (z, at(x, yj, c))).start()
        take(r2b.at[j], x_recv.at[1, j])
        s2b[j] = total(s1[xj, y, :, 512:1024], r2b.at[j]).astype(BF16)
        copy_to(s2b.at[j], r3b.at[j - 1], x_send.at[1, 4], x_recv.at[1, 4], (z, at(xj, y, c))).start()

    firsts = (((0,), (0,)), ((), ()))
    own_pos = jnp.where(iota((16, 16), 0) == iota((16, 16), 1), 1.0, 0.0)
    q_unit, q_hi, q_lo = unit[0:16], u_hi[0:16], u_lo[0:16]

    def column(row):
        return jnp.sum(own_pos * jnp.broadcast_to(row, (16, 16)), axis=1, keepdims=True)

    def scores(start, count, mask):
        rows = slice(start, start + count)
        high, low = u_hi[rows], u_lo[rows]
        logits = 50.0 * (dot(high, q_hi, LAST) + (dot(low, q_hi, LAST) + dot(high, q_lo, LAST)))
        logits = jnp.where(mask > 0.5, logits, 0.0)
        return logits, jnp.where(mask > 0.5, jnp.exp(logits), 0.0)

    def negatives(start, count):
        rows = slice(start, start + count)
        logits, w = scores(start, count, owned[start - 32 : start - 32 + count, 0:16])
        w_hi, w_lo = split(w)
        high, low = u_hi[rows], u_lo[rows]
        along = dot(w_hi, high, firsts) + (dot(w_lo, high, firsts) + dot(w_hi, low, firsts))
        scale = inv[rows, 0:1]
        k_hi, k_lo = split(w * (50.0 * scale))
        pull = dot(k_hi, q_hi) + (dot(k_lo, q_hi) + dot(k_hi, q_lo))
        k2 = jnp.sum(w * logits, axis=1, keepdims=True) * scale
        raw[start - 32 : start - 32 + count] = pull - unit[rows] * k2
        return jnp.sum(w, axis=0, keepdims=True), along

    select(0)
    select(1)
    take(brecv.at[pl.ds(0, GROUP - 1)], b_sem.at[1])
    got = brecv[...].astype(F32)
    xs[32:288, 0:512] = got[:, 0:8].reshape(256, 512).astype(BF16)
    xs[32:288, 512:1024] = got[:, 8:16].reshape(256, 512).astype(BF16)
    project(32, 256)
    pass_on(2)
    select(2)
    pass_on(1)
    select(3)
    pass_on(3)
    for peer in others:
        copy_to(shard_best.at[lax.div(peer, 8)], crecv.at[me], t_sem.at[0], t_sem.at[1], (z, peer)).start()
    crecv[me] = shard_best[lax.div(me, 8)]
    pos_logits, pos_w = scores(16, 16, own_pos)
    base_sum, base_along = negatives(32, 256)

    take(r2a.at[0], x_recv.at[0, 0])
    own_left = total(s1[x, y, :, 0:512], r2a.at[0])
    take(r2b.at[0], x_recv.at[1, 0])
    own_right = total(s1[x, y, :, 512:1024], r2b.at[0])
    take(r3a, x_recv.at[0, 4])
    xs[288:320, 0:512] = total(own_left, r3a).astype(BF16)
    take(r3b, x_recv.at[1, 4])
    xs[288:320, 512:1024] = total(own_right, r3b).astype(BF16)
    project(288, 32)
    ext_sum, ext_along = negatives(288, 32)

    share = 1.0 / (base_sum + ext_sum + jnp.sum(pos_w, axis=0, keepdims=True))
    slot_share = jnp.sum(owned[:, 0:16] * share, axis=1, keepdims=True)
    dz[32:320] = (raw[...] * slot_share).astype(BF16)
    pos_slope = column(jnp.sum(pos_w, axis=0, keepdims=True) * share - 1.0)
    pos_unit = unit[16:32]
    du = 50.0 * (column(share) * (base_along + ext_along) + pos_slope * pos_unit)
    dz[0:16] = ((du - q_unit * jnp.sum(q_unit * du, axis=1, keepdims=True)) * inv[0:16, 0:1]).astype(BF16)
    pos_logit = jnp.sum(pos_logits, axis=1, keepdims=True)
    dz[16:32] = (pos_slope * (50.0 * q_unit - pos_unit * pos_logit) * inv[16:32, 0:1]).astype(BF16)

    def h_copy(i):
        zz = lax.rem(z + STEPS[i], SIDE)
        return copy_to(hs.at[1 - c, zz], core_in.at[zz], h_send, h_recv.at[i], partner)

    def grow(i):
        zz = lax.rem(z + STEPS[i], SIDE)
        part = dot(xs[:, pl.ds(pl.multiple_of(zz * 256, 256), 256)], dz[...], firsts).reshape(32, 8, 1024)
        part = jnp.concatenate([part[:, :, 0:512], part[:, :, 512:1024]], axis=1).astype(BF16)
        part = part.reshape(4, 4, 2, 16, 512)
        for core in range(2):
            hs[core, zz] = part[:, :, core]
        h_copy(i).start()

    place = (z, x, y)

    def device(axis, to):
        where = [z, x, y]
        where[axis] = to
        return (where[0], at(where[1], where[2], c))

    def first_from(p, to):
        tile, y0, ys, order = PORTIONS[p]
        index = [slice(None), slice(None), pl.ds(y0, ys)]
        if order[0] == 2:
            index[2] = to
        else:
            index[order[0]] = to
        return (*index, slice(None), pl.ds(tile * 128, 128))

    def gather_core(i):
        zz = lax.rem(z + STEPS[i], SIDE)
        h_copy(i).wait_recv()
        parts[zz] = (hs[c, zz].astype(F32) + core_in[zz].astype(F32)).astype(BF16)
        for p in (3, 4, 0, 1, 2):
            tile, y0, ys, order = PORTIONS[p]
            lanes = pl.ds(tile * 128, 128)
            if order[0] == 0:
                moves = [(zz, parts.at[zz, :, pl.ds(y0, ys), :, lanes], in1[p].at[STEPS[i] - 1])] if STEPS[i] else []
            else:
                moves = []
                for k in (2, 1, 3):
                    to = lax.rem(place[order[0]] + k, SIDE)
                    if order[0] == 1:
                        source = parts.at[zz, to, pl.ds(y0, ys), :, lanes]
                    else:
                        source = parts.at[zz, :, to, :, lanes]
                    moves.append((to, source, in1[p].at[k - 1, zz]))
            for to, source, target in moves:
                copy_to(source, target, r_send.at[0, p], r_recv.at[0, p], device(order[0], to)).start()

    grow(0)
    grow(1)
    gather_core(0)
    grow(2)
    gather_core(1)
    grow(3)
    gather_core(2)
    gather_core(3)

    out_v[8:40] = dot(dz[0:32], head[...], LAST)

    take(crecv.at[pl.ds(0, GROUP - 1)], t_sem.at[1])
    lane = iota((16, 128), 1)
    packed[...] = jnp.full((8, 16, 128), 2147483647, jnp.int32)
    mine = lax.rem(me, 8)
    for g in range(4):
        merged = jnp.zeros((16, 128), jnp.int32)
        for s in range(8):
            key = crecv[g * 8 + s].astype(jnp.int32)
            key = ((key >> 11) << 16) + (key & 2047) + (g * 8 + s) * 2048
            key = pltpu.roll(key, lax.rem((s - mine + 8) * 16, 128), 1)
            merged = jnp.where((lane >> 4) == s, key, merged)
        packed[g] = merged
    best = [packed[:, i, :] for i in range(16)]
    for d in (64, 32, 16):
        best = merge16(best, [pltpu.roll(b, d, 1) for b in best])
    for d in (6, 7):
        best = merge16(best, [pltpu.roll(b, d, 0) for b in best])
    square[...] = jnp.zeros((128, 128), jnp.int32)
    for i in range(16):
        square[i : i + 1, :] = best[i][0:1, :]
    flat = square[...]
    out_v[40:56, 0:128] = jnp.transpose((flat & 65535).astype(F32))[0:16]
    out_v[40:56, 128:256] = jnp.transpose((flat >> 16).astype(F32))[0:16]
    early = pltpu.make_async_copy(out_v.at[pl.ds(8, 48)], out_hbm.at[pl.ds(8, 48)], small_sem.at[0])
    early.start()

    def pick(p, stage, to):
        axis = PORTIONS[p][3][stage]
        return tuple(to if a == axis else slice(None) for a, _ in extents(p, stage))

    for p in (1, 2, 4, 0, 3):
        axis = PORTIONS[p][3][0]
        take(in1[p], r_recv.at[0, p])
        mid[p][...] = total(parts[first_from(p, place[axis])], in1[p]).astype(BF16)
        axis = PORTIONS[p][3][1]
        for k in (2, 1, 3):
            to = lax.rem(place[axis] + k, SIDE)
            copy_to(
                mid[p].at[pick(p, 1, to)], in2[p].at[k - 1], r_send.at[1, p], r_recv.at[1, p], device(axis, to)
            ).start()
    for p in (1, 2, 4, 0, 3):
        axis = PORTIONS[p][3][1]
        take(in2[p], r_recv.at[1, p])
        _, y0, ys, order = PORTIONS[p]
        sums = total(mid[p][pick(p, 1, place[axis])], in2[p]).astype(BF16)
        if TAIL[p] == 3:
            tail[3, y0 : y0 + ys] = sums
        else:
            tail[p] = sums
        if p == 4:
            continue
        q = TAIL[p]
        axis = order[2]
        for k in (2, 1, 3):
            to = lax.rem(place[axis] + k, SIDE)
            copy_to(
                tail.at[q, to], in3.at[q, k - 1], r_send.at[2, q], r_recv.at[2, q], device(axis, to)
            ).start()
    for q in range(4):
        take(in3.at[q], r_recv.at[2, q])
        out = total(tail[q, place[PORTIONS[q][3][2]]], in3.at[q])
        out_v[0:8, q * 128 : (q + 1) * 128] = out[0:8]
        out_v[0:8, 512 + q * 128 : 512 + (q + 1) * 128] = out[8:16]
    late = pltpu.make_async_copy(out_v.at[pl.ds(0, 8)], out_hbm.at[pl.ds(0, 8)], small_sem.at[1])
    late.start()

    take(out_buf.at[pl.ds(0, GROUP - 1)], p_sem.at[0])
    take(code_in.at[pl.ds(0, GROUP - 1)], q_sem.at[0])
    take(bsend.at[pl.ds(0, GROUP - 1)], b_sem.at[0])
    take(crecv.at[pl.ds(0, GROUP - 1)], t_sem.at[0])
    core_copy.wait_send()
    for j in range(SIDE):
        take(r2a.at[j], x_send.at[0, j])
        take(r2b.at[j], x_send.at[1, j])
    take(r3a, x_send.at[0, 4])
    take(r3b, x_send.at[1, 4])
    take(core_in, h_send)
    for p in range(5):
        take(in1[p], r_send.at[0, p])
        take(in2[p], r_send.at[1, p])
    for q in range(4):
        take(in3.at[q], r_send.at[2, q])
    early.wait()
    late.wait()


def whole(codes, pos, neg, bank_codes, bank_emb, query_emb, positive_emb, head):
    anywhere = pl.BlockSpec(memory_space=pl.ANY)
    dma = pltpu.SemaphoreType.DMA
    block = (16, 128)

    def by_portion(stage, lead):
        return [pltpu.VMEM((*lead, *(n for _, n in extents(p, stage)), *block), BF16) for p in range(5)]

    return pl.pallas_call(
        whole_kernel,
        out_shape=jax.ShapeDtypeStruct((56, 1024), F32),
        in_specs=[anywhere] * 8,
        out_specs=anywhere,
        scratch_shapes=[
            pltpu.VMEM((16, 64), jnp.int32),
            pltpu.VMEM((1, 16), jnp.int32),
            pltpu.VMEM((16, 16), jnp.int32),
            pltpu.VMEM((56, 1024), F32),
            pltpu.VMEM((2048, 1024), BF16),
            pltpu.VMEM((2048, 1024), BF16),
            pltpu.VMEM((1024, 1024), BF16),
            pltpu.VMEM((8, 128), F32),
            pltpu.VMEM((288, 128), F32),
            pltpu.VMEM((32, 8, 128), F32),
            pltpu.VMEM((32, 8, 128), F32),
            pltpu.VMEM((16, 128), F32),
            pltpu.VMEM((32, 16, 128), F32),
            pltpu.VMEM((32, 16, 512), BF16),
            pltpu.VMEM((32, 16, 512), BF16),
            pltpu.VMEM((16, 32, 1024), BF16),
            pltpu.VMEM((16, 32, 1024), BF16),
            pltpu.VMEM((16, 32, 1024), BF16),
            pltpu.VMEM((4, 4, 32, 1024), BF16),
            pltpu.VMEM((4, 3, 32, 512), BF16),
            pltpu.VMEM((4, 3, 32, 512), BF16),
            pltpu.VMEM((4, 32, 512), BF16),
            pltpu.VMEM((4, 32, 512), BF16),
            pltpu.VMEM((3, 32, 512), BF16),
            pltpu.VMEM((3, 32, 512), BF16),
            pltpu.VMEM((1024, 512), BF16),
            pltpu.VMEM((2048, 512), F32),
            pltpu.VMEM((8, 512), F32),
            pltpu.VMEM((4, 16, 128), F32),
            pltpu.VMEM((32, 16, 128), F32),
            pltpu.VMEM((8, 16, 128), jnp.int32),
            pltpu.VMEM((128, 128), jnp.int32),
            pltpu.VMEM((320, 1024), BF16),
            pltpu.VMEM((320, 1024), BF16),
            pltpu.VMEM((288, 1024), F32),
            pltpu.VMEM((320, 1024), F32),
            pltpu.VMEM((320, 128), F32),
            pltpu.VMEM((320, 1024), BF16),
            pltpu.VMEM((320, 1024), BF16),
            pltpu.VMEM((2, 4, 4, 4, 16, 512), BF16),
            pltpu.VMEM((4, 4, 4, 16, 512), BF16),
            pltpu.VMEM((4, 4, 4, 16, 512), BF16),
            by_portion(1, (3,)),
            by_portion(1, ()),
            by_portion(2, (3,)),
            pltpu.VMEM((4, 4, *block), BF16),
            pltpu.VMEM((4, 3, *block), BF16),
            dma((3,)),
            dma((5,)),
            dma((2,)),
            dma((2,)),
            dma((2,)),
            dma((2,)),
            dma((2,)),
            dma((2, 5)),
            dma((2, 5)),
            dma,
            dma((4,)),
            dma((3, 5)),
            dma((3, 5)),
        ],
        compiler_params=pltpu.CompilerParams(
            collective_id=0, has_side_effects=True, vmem_limit_bytes=60 * MIB
        ),
        name="whole",
    )(codes, pos, neg, bank_codes, bank_emb, query_emb, positive_emb, head)


OUT = (((16, 16), jnp.int32), ((16, 16), jnp.int32), ((16, 1024), BF16), ((16, 1024), BF16), ((8, 1024), F32))


def emit_kernel(packed_ref, *refs):
    targets, held, sem = refs[0:5], refs[5:9], refs[9]
    held[0][...] = packed_ref[40:56, 0:16].astype(jnp.int32)
    held[1][...] = packed_ref[40:56, 128:144].astype(jnp.int32)
    held[2][...] = packed_ref[8:24].astype(BF16)
    held[3][...] = packed_ref[24:40].astype(BF16)
    sources = (*held, packed_ref.at[pl.ds(0, 8)])
    copies = [pltpu.make_async_copy(a, b, sem.at[i]) for i, (a, b) in enumerate(zip(sources, targets))]
    for copy in copies:
        copy.start()
    for copy in copies:
        copy.wait()


def emit(packed):
    return pl.pallas_call(
        emit_kernel,
        out_shape=tuple(jax.ShapeDtypeStruct(*o) for o in OUT),
        in_specs=[pl.BlockSpec(memory_space=pltpu.VMEM)],
        out_specs=(pl.BlockSpec(memory_space=pl.ANY),) * 5,
        scratch_shapes=[*(pltpu.VMEM(*o) for o in OUT[:4]), pltpu.SemaphoreType.DMA((5,))],
        name="emit",
    )(packed)


def local(
    query_codes, positive_ids, negative_ids, bank_codes, bank_emb, query_emb, positive_emb, head
):
    return emit(
        whole(query_codes, positive_ids.reshape(1, -1), negative_ids, bank_codes, bank_emb, query_emb, positive_emb, head)
    )


def solution(mesh):
    both = ("dp", "index")
    rows = P(both, None)
    return jax.shard_map(
        local,
        mesh=mesh,
        in_specs=(rows, P(both), rows, P("index", None), P("index", None), rows, rows, P()),
        out_specs=(rows,) * 5,
        check_vma=False,
    )
```

```python
import functools

import jax
import jax.numpy as jnp
from jax import lax
from jax.experimental import pallas as pl
from jax.experimental.pallas import tpu as pltpu
from jax.sharding import PartitionSpec as P

F32 = jnp.float32
BF16 = jnp.bfloat16
MESH = pl.DeviceIdType.MESH
MIB = 1 << 20
GROUP = 32
SIDE = 4
BIG = float(1 << 23)
LAST = (((1,), (1,)), ((), ()))


def iota(shape, dim):
    return lax.broadcasted_iota(jnp.int32, shape, dim)


def dot(a, b, dims=(((1,), (0,)), ((), ()))):
    return lax.dot_general(a, b, dims, preferred_element_type=F32)


def copy_to(src, dst, send_sem, recv_sem, device):
    return pltpu.make_async_remote_copy(
        src_ref=src,
        dst_ref=dst,
        send_sem=send_sem,
        recv_sem=recv_sem,
        device_id=device,
        device_id_type=MESH,
    )


def coords():
    z = lax.axis_index("dp")
    me = lax.axis_index("index")
    x = lax.div(me, 8)
    y = lax.rem(lax.div(me, 2), 4)
    c = lax.rem(me, 2)
    return z, me, x, y, c


def at(x, y, c):
    return x * 8 + y * 2 + c


OFFSETS = sorted(
    ((dx, dy, dc) for dx in range(4) for dy in range(4) for dc in range(2) if dx or dy or dc),
    key=lambda o: -(min(o[0], 4 - o[0]) + min(o[1], 4 - o[1])),
)


def peers(x, y, c):
    return [at(lax.rem(x + dx, 4), lax.rem(y + dy, 4), lax.rem(c + dc, 2)) for dx, dy, dc in OFFSETS]


def take(ref, sem):
    pltpu.make_async_copy(ref, ref, sem).wait()


def request_table(pos_row, negatives):
    hi = jnp.floor(negatives * (1.0 / 256.0))
    lo = negatives - 256.0 * hi
    halves = jnp.concatenate([hi, lo], axis=0).astype(BF16)
    spread = jnp.where(iota((16, 256), 0) == (iota((16, 256), 1) & 15), 1.0, 0.0).astype(BF16)
    got = dot(halves, spread)
    ids = 256.0 * got[0:16] + got[16:32]
    ids = jnp.where(iota((16, 256), 0) == (iota((16, 256), 1) >> 4), ids, 0.0)
    id_row = jnp.sum(ids, axis=0, keepdims=True)
    owner_row = jnp.floor(id_row * (1.0 / 2048.0))
    owner_b = jnp.broadcast_to(owner_row, (256, 256))
    owner_t = jnp.transpose(owner_b)
    earlier = iota((256, 256), 0) < iota((256, 256), 1)
    same = jnp.where(owner_b == owner_t, 1.0, 0.0)
    rank = jnp.sum(jnp.where(earlier, same, 0.0), axis=0, keepdims=True)
    slot_row = jnp.where(rank < 7.0, owner_row * 8.0 + rank, 249.0 + rank)
    slot_b = jnp.broadcast_to(slot_row, (288, 256))
    hit = iota((288, 256), 0).astype(F32) == slot_b
    id_col = jnp.sum(jnp.where(hit, jnp.broadcast_to(id_row, (288, 256)) + 1.0, 0.0), axis=1, keepdims=True) - 1.0
    which = jnp.where(iota((256, 128), 1) == (iota((256, 128), 0) >> 4), 1.0, 0.0).astype(BF16)
    owned_by = dot(jnp.where(hit, 1.0, 0.0).astype(BF16), which)
    lane32 = iota((32, 128), 1)
    sub32 = iota((32, 128), 0)
    ext_row = jnp.sum(
        jnp.where(lane32 == sub32 + 96, jnp.broadcast_to(id_col[256:288], (32, 128)), 0.0), axis=0, keepdims=True
    )
    return id_col, owned_by, ext_row


def onehot_rows(rel, count):
    return jnp.where(
        jnp.broadcast_to(rel, (count, 2048)) == iota((count, 2048), 1).astype(F32), 1.0, 0.0
    ).astype(BF16)


def batcher(n):
    pairs = []
    p = 1
    while p < n:
        k = p
        while k >= 1:
            for j in range(k % p, n - k, 2 * k):
                for i in range(min(k, n - j - k)):
                    if (i + j) // (2 * p) == (i + j + k) // (2 * p):
                        pairs.append((i + j, i + j + k))
            k //= 2
        p *= 2
    return pairs


SORT16 = batcher(16)


def exchange(v, i, j):
    v[i], v[j] = jnp.minimum(v[i], v[j]), jnp.maximum(v[i], v[j])


def sort16(v):
    v = list(v)
    for i, j in SORT16:
        exchange(v, i, j)
    return v


def merge16(a, b):
    v = [jnp.minimum(a[i], b[15 - i]) for i in range(16)]
    for d in (8, 4, 2, 1):
        for i in range(16):
            if i & d == 0:
                exchange(v, i, i + d)
    return v


def sign_rows(table):
    hi = jnp.floor(table * (1.0 / 256.0))
    lo = table - 256.0 * hi
    both = jnp.concatenate([hi, lo], axis=1).astype(BF16)
    k = iota((1024, 256), 0)
    lane = iota((1024, 256), 1)
    source = (k >> 4) + jnp.where((k & 8) == 0, 128, 0)
    pick = jnp.where(lane == source, 1.0, 0.0).astype(BF16)
    byte = dot(pick, both, LAST).astype(jnp.int32)
    bit = byte & (1 << (iota((1024, 512), 0) & 7))
    return jnp.where(bit != 0, -1024.0, 1024.0).astype(BF16)


PORTIONS = ((0, 0, 4, (0, 1, 2)), (1, 0, 4, (1, 2, 0)), (2, 0, 4, (2, 0, 1)), (3, 0, 2, (0, 1, 2)), (3, 2, 2, (1, 0, 2)))
TAIL = (0, 1, 2, 3, 3)
STEPS = (2, 1, 3, 0)


def extents(p, stage):
    _, _, ys, order = PORTIONS[p]
    return [(a, ys if a == 2 else SIDE) for a in range(3) if a not in order[:stage]]


def split(v):
    high = v.astype(BF16)
    return high, (v - high.astype(F32)).astype(BF16)


def whole_kernel(
    qcodes_hbm, pos_hbm, neg_hbm, codes_hbm, bank_hbm, query_hbm, positive_hbm, head_hbm,
    out_hbm,
    qcodes, pos_in, neg_in, out_v,
    bank, codes, head, pay, owned, out_buf, in_buf, bsend, brecv, esend, eown, ecore, s1, r2a, r2b, s2a, s2b, r3a, r3b,
    signs, keys, pos, shard_best, crecv, packed, square, xs, dz, raw, unit, inv, u_hi, u_lo,
    hs, core_in, parts, in1, mid, in2, tail, in3,
    load_sem, small_sem, p_sem, b_sem, t_sem, c_sem, x_send, x_recv, h_send, h_recv, r_send, r_recv,
):
    z, me, x, y, c = coords()
    others = peers(x, y, c)
    partner = (z, at(x, y, 1 - c))
    load_bank = pltpu.make_async_copy(bank_hbm, bank, load_sem.at[0])
    load_codes = pltpu.make_async_copy(codes_hbm, codes, load_sem.at[1])
    load_head = pltpu.make_async_copy(head_hbm, head, load_sem.at[2])
    small = [
        pltpu.make_async_copy(source, target, small_sem.at[i])
        for i, (source, target) in enumerate(
            (
                (neg_hbm, neg_in),
                (pos_hbm, pos_in),
                (qcodes_hbm, qcodes),
                (query_hbm, xs.at[pl.ds(0, 16)]),
                (positive_hbm, xs.at[pl.ds(16, 16)]),
            )
        )
    ]
    for load in small:
        load.start()
    load_bank.start()
    barrier = pltpu.get_barrier_semaphore()
    for peer in others:
        pl.semaphore_signal(barrier, inc=1, device_id=(z, peer), device_id_type=MESH)
    for k in range(1, SIDE):
        pl.semaphore_signal(barrier, inc=1, device_id=(lax.rem(z + k, SIDE), me), device_id_type=MESH)
    load_codes.start()
    load_head.start()

    for load in small[:3]:
        load.wait()
    pay[...] = jnp.zeros((8, 128), F32)
    pay[:, 64:80] = jnp.broadcast_to(pos_in[...].astype(F32), (8, 16))
    out_buf[:, 8:16, :] = jnp.broadcast_to(
        jnp.concatenate([qcodes[0:8], qcodes[8:16]], axis=1).astype(F32)[None], (32, 8, 128)
    )
    id_col, owned_by, ext_row = request_table(pos_in[...].astype(F32), neg_in[...].astype(F32))
    owned[...] = owned_by
    lane8 = iota((8, 128), 1)
    common = jnp.where(lane8 >= 96, jnp.broadcast_to(ext_row, (8, 128)), pay[...])
    base_cols = jnp.broadcast_to(id_col[0:256], (256, 128)).reshape(32, 8, 128)
    out_buf[:, 0:8, :] = jnp.where(
        iota((32, 8, 128), 2) == 0, base_cols, jnp.broadcast_to(common[None], (32, 8, 128))
    )
    pl.semaphore_wait(barrier, len(others) + SIDE - 1)
    for peer in others:
        copy_to(out_buf.at[peer], in_buf.at[me], p_sem.at[0], p_sem.at[1], (z, peer)).start()
    in_buf[me] = out_buf[me]

    for load in small[3:]:
        load.wait()

    def project(start, count):
        rows = slice(start, start + count)
        zed = dot(xs[rows], head[...])
        scale = 1.0 / jnp.sqrt(jnp.sum(zed * zed, axis=1, keepdims=True) + 1e-6)
        u = zed * scale
        unit[rows] = u
        inv[rows] = jnp.broadcast_to(scale, (count, 128))
        high, low = split(u)
        u_hi[rows] = high
        u_lo[rows] = low

    load_head.wait()
    project(0, 32)
    load_bank.wait()
    take(in_buf.at[pl.ds(0, GROUP - 1)], p_sem.at[1])

    first = (me * 2048).astype(F32)
    asked = in_buf[:, 0:8, :].reshape(256, 128)
    base_rel = jnp.sum(jnp.where(iota((256, 128), 1) == 0, asked, 0.0), axis=1, keepdims=True) - first
    hot = onehot_rows(base_rel, 256)
    for h in range(2):
        part = dot(hot, bank[:, h * 512 : (h + 1) * 512])
        bsend[:, 8 * h : 8 * h + 8, :] = part.reshape(32, 8, 512).astype(BF16)
    for peer in others:
        copy_to(bsend.at[peer], brecv.at[me], b_sem.at[0], b_sem.at[1], (z, peer)).start()
    brecv[me] = bsend[me]

    def extras(core):
        rows = in_buf[:, 0:1, :].reshape(16, 2, 1, 128)
        mine = jnp.where(core == 0, rows[:, 0], rows[:, 1])
        wide = jnp.broadcast_to(mine, (16, 32, 128))
        keep = iota((16, 32, 128), 2) == iota((16, 32, 128), 1) + 96
        rel = jnp.sum(jnp.where(keep, wide, 0.0), axis=2, keepdims=True).reshape(512, 1) - first
        return dot(onehot_rows(rel, 512), bank[...])

    esend[...] = extras(1 - c).reshape(16, 32, 1024).astype(BF16)
    core_copy = copy_to(esend, ecore, c_sem.at[0], c_sem.at[1], partner)
    core_copy.start()
    eown[...] = extras(c).reshape(16, 32, 1024).astype(BF16)
    core_copy.wait_recv()
    s1[...] = (eown[...].astype(F32) + ecore[...].astype(F32)).astype(BF16).reshape(4, 4, 32, 1024)

    left, right = pl.ds(0, 512), pl.ds(512, 512)
    for j in (2, 1, 3, 0):
        xj, yj = lax.rem(x + j, SIDE), lax.rem(y + j, SIDE)
        for k in (2, 1, 3):
            xk, yk = lax.rem(x + k, SIDE), lax.rem(y + k, SIDE)
            copy_to(
                s1.at[xk, yj, :, left], r2a.at[j, k - 1], x_send.at[0, j], x_recv.at[0, j], (z, at(xk, y, c))
            ).start()
            copy_to(
                s1.at[xj, yk, :, right], r2b.at[j, k - 1], x_send.at[1, j], x_recv.at[1, j], (z, at(x, yk, c))
            ).start()

    pairs = in_buf[:, 8:16, :]
    signs[...] = sign_rows(
        jnp.concatenate([pairs, pltpu.roll(pairs.reshape(256, 128), 64, 1).reshape(32, 8, 128)], axis=1).reshape(512, 128)
    )
    lane8 = iota((8, 128), 1)
    for t in range(4):
        row = jnp.zeros((8, 128), F32)
        for i in range(8):
            ids = pltpu.roll(in_buf[8 * t + i, 0:8], (16 * i + 64) % 128, 1)
            row = jnp.where((lane8 >> 4) == i, ids, row)
        pos[:, t * 128 : (t + 1) * 128] = row - first
    load_codes.wait()

    def product(m, carry):
        at_row = pl.multiple_of(m * 256, 256)
        keys[pl.ds(at_row, 256), :] = dot(codes[pl.ds(at_row, 256), :], signs[...])
        return carry

    lax.fori_loop(0, 8, product, 0)
    sub = iota((8, 128), 0)

    def select(t):
        lanes = slice(t * 128, (t + 1) * 128)
        wanted = pos[:, lanes]

        def load16(g):
            out = []
            for i in range(16):
                row = pl.multiple_of(g * 128 + i * 8, 8)
                p = (sub + (g * 128 + i * 8)).astype(F32)
                key = keys[pl.ds(row, 8), lanes] + (p + float(1 << 20))
                out.append(jnp.where(p == wanted, BIG, key))
            return out

        def step(g, best):
            return tuple(merge16(best, sort16(load16(g))))

        best = lax.fori_loop(1, 16, step, tuple(sort16(load16(0))))
        for d in (4, 2, 1):
            best = merge16(best, [pltpu.roll(b, d, 0) for b in best])
        for i in range(16):
            shard_best[t, i : i + 1, :] = best[i][0:1, :]

    def total(own, got):
        t = own.astype(F32)
        for k in range(SIDE - 1):
            t = t + got[k].astype(F32)
        return t

    def pass_on(j):
        xj, yj = lax.rem(x + j, SIDE), lax.rem(y + j, SIDE)
        take(r2a.at[j], x_recv.at[0, j])
        s2a[j] = total(s1[x, yj, :, 0:512], r2a.at[j]).astype(BF16)
        copy_to(s2a.at[j], r3a.at[j - 1], x_send.at[0, 4], x_recv.at[0, 4], (z, at(x, yj, c))).start()
        take(r2b.at[j], x_recv.at[1, j])
        s2b[j] = total(s1[xj, y, :, 512:1024], r2b.at[j]).astype(BF16)
        copy_to(s2b.at[j], r3b.at[j - 1], x_send.at[1, 4], x_recv.at[1, 4], (z, at(xj, y, c))).start()

    firsts = (((0,), (0,)), ((), ()))
    own_pos = jnp.where(iota((16, 16), 0) == iota((16, 16), 1), 1.0, 0.0)
    q_unit, q_hi, q_lo = unit[0:16], u_hi[0:16], u_lo[0:16]

    def column(row):
        return jnp.sum(own_pos * jnp.broadcast_to(row, (16, 16)), axis=1, keepdims=True)

    def scores(start, count, mask):
        rows = slice(start, start + count)
        high, low = u_hi[rows], u_lo[rows]
        logits = 50.0 * (dot(high, q_hi, LAST) + (dot(low, q_hi, LAST) + dot(high, q_lo, LAST)))
        logits = jnp.where(mask > 0.5, logits, 0.0)
        return logits, jnp.where(mask > 0.5, jnp.exp(logits), 0.0)

    def negatives(start, count):
        rows = slice(start, start + count)
        logits, w = scores(start, count, owned[start - 32 : start - 32 + count, 0:16])
        w_hi, w_lo = split(w)
        high, low = u_hi[rows], u_lo[rows]
        along = dot(w_hi, high, firsts) + (dot(w_lo, high, firsts) + dot(w_hi, low, firsts))
        scale = inv[rows, 0:1]
        k_hi, k_lo = split(w * (50.0 * scale))
        pull = dot(k_hi, q_hi) + (dot(k_lo, q_hi) + dot(k_hi, q_lo))
        k2 = jnp.sum(w * logits, axis=1, keepdims=True) * scale
        raw[start - 32 : start - 32 + count] = pull - unit[rows] * k2
        return jnp.sum(w, axis=0, keepdims=True), along

    take(brecv.at[pl.ds(0, GROUP - 1)], b_sem.at[1])
    got = brecv[...].astype(F32)
    xs[32:288, 0:512] = got[:, 0:8].reshape(256, 512).astype(BF16)
    xs[32:288, 512:1024] = got[:, 8:16].reshape(256, 512).astype(BF16)
    project(32, 256)
    pass_on(2)
    pos_logits, pos_w = scores(16, 16, own_pos)
    base_sum, base_along = negatives(32, 256)
    pass_on(1)
    pass_on(3)

    take(r2a.at[0], x_recv.at[0, 0])
    own_left = total(s1[x, y, :, 0:512], r2a.at[0])
    take(r2b.at[0], x_recv.at[1, 0])
    own_right = total(s1[x, y, :, 512:1024], r2b.at[0])
    take(r3a, x_recv.at[0, 4])
    xs[288:320, 0:512] = total(own_left, r3a).astype(BF16)
    take(r3b, x_recv.at[1, 4])
    xs[288:320, 512:1024] = total(own_right, r3b).astype(BF16)
    project(288, 32)
    ext_sum, ext_along = negatives(288, 32)

    share = 1.0 / (base_sum + ext_sum + jnp.sum(pos_w, axis=0, keepdims=True))
    slot_share = jnp.sum(owned[:, 0:16] * share, axis=1, keepdims=True)
    dz[32:320] = (raw[...] * slot_share).astype(BF16)
    pos_slope = column(jnp.sum(pos_w, axis=0, keepdims=True) * share - 1.0)
    pos_unit = unit[16:32]
    du = 50.0 * (column(share) * (base_along + ext_along) + pos_slope * pos_unit)
    dz[0:16] = ((du - q_unit * jnp.sum(q_unit * du, axis=1, keepdims=True)) * inv[0:16, 0:1]).astype(BF16)
    pos_logit = jnp.sum(pos_logits, axis=1, keepdims=True)
    dz[16:32] = (pos_slope * (50.0 * q_unit - pos_unit * pos_logit) * inv[16:32, 0:1]).astype(BF16)

    def h_copy(i):
        zz = lax.rem(z + STEPS[i], SIDE)
        return copy_to(hs.at[1 - c, zz], core_in.at[zz], h_send, h_recv.at[i], partner)

    def grow(i):
        zz = lax.rem(z + STEPS[i], SIDE)
        part = dot(xs[:, pl.ds(pl.multiple_of(zz * 256, 256), 256)], dz[...], firsts).reshape(32, 8, 1024)
        part = jnp.concatenate([part[:, :, 0:512], part[:, :, 512:1024]], axis=1).astype(BF16)
        part = part.reshape(4, 4, 2, 16, 512)
        for core in range(2):
            hs[core, zz] = part[:, :, core]
        h_copy(i).start()

    place = (z, x, y)

    def device(axis, to):
        where = [z, x, y]
        where[axis] = to
        return (where[0], at(where[1], where[2], c))

    def first_from(p, to):
        tile, y0, ys, order = PORTIONS[p]
        index = [slice(None), slice(None), pl.ds(y0, ys)]
        if order[0] == 2:
            index[2] = to
        else:
            index[order[0]] = to
        return (*index, slice(None), pl.ds(tile * 128, 128))

    def gather_core(i):
        zz = lax.rem(z + STEPS[i], SIDE)
        h_copy(i).wait_recv()
        parts[zz] = (hs[c, zz].astype(F32) + core_in[zz].astype(F32)).astype(BF16)
        for p in (3, 4, 0, 1, 2):
            tile, y0, ys, order = PORTIONS[p]
            lanes = pl.ds(tile * 128, 128)
            if order[0] == 0:
                moves = [(zz, parts.at[zz, :, pl.ds(y0, ys), :, lanes], in1[p].at[STEPS[i] - 1])] if STEPS[i] else []
            else:
                moves = []
                for k in (2, 1, 3):
                    to = lax.rem(place[order[0]] + k, SIDE)
                    if order[0] == 1:
                        source = parts.at[zz, to, pl.ds(y0, ys), :, lanes]
                    else:
                        source = parts.at[zz, :, to, :, lanes]
                    moves.append((to, source, in1[p].at[k - 1, zz]))
            for to, source, target in moves:
                copy_to(source, target, r_send.at[0, p], r_recv.at[0, p], device(order[0], to)).start()

    grow(0)
    grow(1)
    gather_core(0)
    grow(2)
    gather_core(1)
    grow(3)
    gather_core(2)
    select(0)
    gather_core(3)
    select(1)
    select(2)
    select(3)
    for peer in others:
        copy_to(shard_best.at[lax.div(peer, 8)], crecv.at[me], t_sem.at[0], t_sem.at[1], (z, peer)).start()
    crecv[me] = shard_best[lax.div(me, 8)]

    out_v[8:40] = dot(dz[0:32], head[...], LAST)

    def pick(p, stage, to):
        axis = PORTIONS[p][3][stage]
        return tuple(to if a == axis else slice(None) for a, _ in extents(p, stage))

    for p in (1, 2, 4, 0, 3):
        axis = PORTIONS[p][3][0]
        take(in1[p], r_recv.at[0, p])
        mid[p][...] = total(parts[first_from(p, place[axis])], in1[p]).astype(BF16)
        axis = PORTIONS[p][3][1]
        for k in (2, 1, 3):
            to = lax.rem(place[axis] + k, SIDE)
            copy_to(
                mid[p].at[pick(p, 1, to)], in2[p].at[k - 1], r_send.at[1, p], r_recv.at[1, p], device(axis, to)
            ).start()
    for p in (1, 2, 4, 0, 3):
        axis = PORTIONS[p][3][1]
        take(in2[p], r_recv.at[1, p])
        _, y0, ys, order = PORTIONS[p]
        sums = total(mid[p][pick(p, 1, place[axis])], in2[p]).astype(BF16)
        if TAIL[p] == 3:
            tail[3, y0 : y0 + ys] = sums
        else:
            tail[p] = sums
        if p == 4:
            continue
        q = TAIL[p]
        axis = order[2]
        for k in (2, 1, 3):
            to = lax.rem(place[axis] + k, SIDE)
            copy_to(
                tail.at[q, to], in3.at[q, k - 1], r_send.at[2, q], r_recv.at[2, q], device(axis, to)
            ).start()
    take(crecv.at[pl.ds(0, GROUP - 1)], t_sem.at[1])
    lane = iota((16, 128), 1)
    packed[...] = jnp.full((8, 16, 128), 2147483647, jnp.int32)
    mine = lax.rem(me, 8)
    for g in range(4):
        merged = jnp.zeros((16, 128), jnp.int32)
        for s in range(8):
            key = crecv[g * 8 + s].astype(jnp.int32)
            key = ((key >> 11) << 16) + (key & 2047) + (g * 8 + s) * 2048
            key = pltpu.roll(key, lax.rem((s - mine + 8) * 16, 128), 1)
            merged = jnp.where((lane >> 4) == s, key, merged)
        packed[g] = merged
    best = [packed[:, i, :] for i in range(16)]
    for d in (64, 32, 16):
        best = merge16(best, [pltpu.roll(b, d, 1) for b in best])
    for d in (6, 7):
        best = merge16(best, [pltpu.roll(b, d, 0) for b in best])
    square[...] = jnp.zeros((128, 128), jnp.int32)
    for i in range(16):
        square[i : i + 1, :] = best[i][0:1, :]
    flat = square[...]
    out_v[40:56, 0:128] = jnp.transpose((flat & 65535).astype(F32))[0:16]
    out_v[40:56, 128:256] = jnp.transpose((flat >> 16).astype(F32))[0:16]
    early = pltpu.make_async_copy(out_v.at[pl.ds(8, 48)], out_hbm.at[pl.ds(8, 48)], small_sem.at[0])
    early.start()

    for q in range(4):
        take(in3.at[q], r_recv.at[2, q])
        out = total(tail[q, place[PORTIONS[q][3][2]]], in3.at[q])
        out_v[0:8, q * 128 : (q + 1) * 128] = out[0:8]
        out_v[0:8, 512 + q * 128 : 512 + (q + 1) * 128] = out[8:16]
    late = pltpu.make_async_copy(out_v.at[pl.ds(0, 8)], out_hbm.at[pl.ds(0, 8)], small_sem.at[1])
    late.start()

    take(out_buf.at[pl.ds(0, GROUP - 1)], p_sem.at[0])
    take(bsend.at[pl.ds(0, GROUP - 1)], b_sem.at[0])
    take(crecv.at[pl.ds(0, GROUP - 1)], t_sem.at[0])
    core_copy.wait_send()
    for j in range(SIDE):
        take(r2a.at[j], x_send.at[0, j])
        take(r2b.at[j], x_send.at[1, j])
    take(r3a, x_send.at[0, 4])
    take(r3b, x_send.at[1, 4])
    take(core_in, h_send)
    for p in range(5):
        take(in1[p], r_send.at[0, p])
        take(in2[p], r_send.at[1, p])
    for q in range(4):
        take(in3.at[q], r_send.at[2, q])
    early.wait()
    late.wait()


def whole(codes, pos, neg, bank_codes, bank_emb, query_emb, positive_emb, head):
    anywhere = pl.BlockSpec(memory_space=pl.ANY)
    dma = pltpu.SemaphoreType.DMA
    block = (16, 128)

    def by_portion(stage, lead):
        return [pltpu.VMEM((*lead, *(n for _, n in extents(p, stage)), *block), BF16) for p in range(5)]

    return pl.pallas_call(
        whole_kernel,
        out_shape=jax.ShapeDtypeStruct((56, 1024), F32),
        in_specs=[anywhere] * 8,
        out_specs=anywhere,
        scratch_shapes=[
            pltpu.VMEM((16, 64), jnp.int32),
            pltpu.VMEM((1, 16), jnp.int32),
            pltpu.VMEM((16, 16), jnp.int32),
            pltpu.VMEM((56, 1024), F32),
            pltpu.VMEM((2048, 1024), BF16),
            pltpu.VMEM((2048, 1024), BF16),
            pltpu.VMEM((1024, 1024), BF16),
            pltpu.VMEM((8, 128), F32),
            pltpu.VMEM((288, 128), F32),
            pltpu.VMEM((32, 16, 128), F32),
            pltpu.VMEM((32, 16, 128), F32),
            pltpu.VMEM((32, 16, 512), BF16),
            pltpu.VMEM((32, 16, 512), BF16),
            pltpu.VMEM((16, 32, 1024), BF16),
            pltpu.VMEM((16, 32, 1024), BF16),
            pltpu.VMEM((16, 32, 1024), BF16),
            pltpu.VMEM((4, 4, 32, 1024), BF16),
            pltpu.VMEM((4, 3, 32, 512), BF16),
            pltpu.VMEM((4, 3, 32, 512), BF16),
            pltpu.VMEM((4, 32, 512), BF16),
            pltpu.VMEM((4, 32, 512), BF16),
            pltpu.VMEM((3, 32, 512), BF16),
            pltpu.VMEM((3, 32, 512), BF16),
            pltpu.VMEM((1024, 512), BF16),
            pltpu.VMEM((2048, 512), F32),
            pltpu.VMEM((8, 512), F32),
            pltpu.VMEM((4, 16, 128), F32),
            pltpu.VMEM((32, 16, 128), F32),
            pltpu.VMEM((8, 16, 128), jnp.int32),
            pltpu.VMEM((128, 128), jnp.int32),
            pltpu.VMEM((320, 1024), BF16),
            pltpu.VMEM((320, 1024), BF16),
            pltpu.VMEM((288, 1024), F32),
            pltpu.VMEM((320, 1024), F32),
            pltpu.VMEM((320, 128), F32),
            pltpu.VMEM((320, 1024), BF16),
            pltpu.VMEM((320, 1024), BF16),
            pltpu.VMEM((2, 4, 4, 4, 16, 512), BF16),
            pltpu.VMEM((4, 4, 4, 16, 512), BF16),
            pltpu.VMEM((4, 4, 4, 16, 512), BF16),
            by_portion(1, (3,)),
            by_portion(1, ()),
            by_portion(2, (3,)),
            pltpu.VMEM((4, 4, *block), BF16),
            pltpu.VMEM((4, 3, *block), BF16),
            dma((3,)),
            dma((5,)),
            dma((2,)),
            dma((2,)),
            dma((2,)),
            dma((2,)),
            dma((2, 5)),
            dma((2, 5)),
            dma,
            dma((4,)),
            dma((3, 5)),
            dma((3, 5)),
        ],
        compiler_params=pltpu.CompilerParams(
            collective_id=0, has_side_effects=True, vmem_limit_bytes=60 * MIB
        ),
        name="whole",
    )(codes, pos, neg, bank_codes, bank_emb, query_emb, positive_emb, head)


OUT = (((16, 16), jnp.int32), ((16, 16), jnp.int32), ((16, 1024), BF16), ((16, 1024), BF16), ((8, 1024), F32))


def emit_kernel(packed_ref, *refs):
    targets, held, sem = refs[0:5], refs[5:9], refs[9]
    held[0][...] = packed_ref[40:56, 0:16].astype(jnp.int32)
    held[1][...] = packed_ref[40:56, 128:144].astype(jnp.int32)
    held[2][...] = packed_ref[8:24].astype(BF16)
    held[3][...] = packed_ref[24:40].astype(BF16)
    sources = (*held, packed_ref.at[pl.ds(0, 8)])
    copies = [pltpu.make_async_copy(a, b, sem.at[i]) for i, (a, b) in enumerate(zip(sources, targets))]
    for copy in copies:
        copy.start()
    for copy in copies:
        copy.wait()


def emit(packed):
    return pl.pallas_call(
        emit_kernel,
        out_shape=tuple(jax.ShapeDtypeStruct(*o) for o in OUT),
        in_specs=[pl.BlockSpec(memory_space=pltpu.VMEM)],
        out_specs=(pl.BlockSpec(memory_space=pl.ANY),) * 5,
        scratch_shapes=[*(pltpu.VMEM(*o) for o in OUT[:4]), pltpu.SemaphoreType.DMA((5,))],
        name="emit",
    )(packed)


def local(
    query_codes, positive_ids, negative_ids, bank_codes, bank_emb, query_emb, positive_emb, head
):
    return emit(
        whole(query_codes, positive_ids.reshape(1, -1), negative_ids, bank_codes, bank_emb, query_emb, positive_emb, head)
    )


def solution(mesh):
    both = ("dp", "index")
    rows = P(both, None)
    return jax.shard_map(
        local,
        mesh=mesh,
        in_specs=(rows, P(both), rows, P("index", None), P("index", None), rows, rows, P()),
        out_specs=(rows,) * 5,
        check_vma=False,
    )
```

```python
import functools

import jax
import jax.numpy as jnp
from jax import lax
from jax.experimental import pallas as pl
from jax.experimental.pallas import tpu as pltpu
from jax.sharding import PartitionSpec as P

F32 = jnp.float32
BF16 = jnp.bfloat16
MESH = pl.DeviceIdType.MESH
MIB = 1 << 20
GROUP = 32
SIDE = 4
BIG = float(1 << 23)
LAST = (((1,), (1,)), ((), ()))


def iota(shape, dim):
    return lax.broadcasted_iota(jnp.int32, shape, dim)


def dot(a, b, dims=(((1,), (0,)), ((), ()))):
    return lax.dot_general(a, b, dims, preferred_element_type=F32)


def copy_to(src, dst, send_sem, recv_sem, device):
    return pltpu.make_async_remote_copy(
        src_ref=src,
        dst_ref=dst,
        send_sem=send_sem,
        recv_sem=recv_sem,
        device_id=device,
        device_id_type=MESH,
    )


def coords():
    z = lax.axis_index("dp")
    me = lax.axis_index("index")
    x = lax.div(me, 8)
    y = lax.rem(lax.div(me, 2), 4)
    c = lax.rem(me, 2)
    return z, me, x, y, c


def at(x, y, c):
    return x * 8 + y * 2 + c


OFFSETS = sorted(
    ((dx, dy, dc) for dx in range(4) for dy in range(4) for dc in range(2) if dx or dy or dc),
    key=lambda o: -(min(o[0], 4 - o[0]) + min(o[1], 4 - o[1])),
)


def peers(x, y, c):
    return [at(lax.rem(x + dx, 4), lax.rem(y + dy, 4), lax.rem(c + dc, 2)) for dx, dy, dc in OFFSETS]


def take(ref, sem):
    pltpu.make_async_copy(ref, ref, sem).wait()


def request_table(pos_row, negatives):
    hi = jnp.floor(negatives * (1.0 / 256.0))
    lo = negatives - 256.0 * hi
    halves = jnp.concatenate([hi, lo], axis=0).astype(BF16)
    spread = jnp.where(iota((16, 256), 0) == (iota((16, 256), 1) & 15), 1.0, 0.0).astype(BF16)
    got = dot(halves, spread)
    ids = 256.0 * got[0:16] + got[16:32]
    ids = jnp.where(iota((16, 256), 0) == (iota((16, 256), 1) >> 4), ids, 0.0)
    id_row = jnp.sum(ids, axis=0, keepdims=True)
    owner_row = jnp.floor(id_row * (1.0 / 2048.0))
    owner_b = jnp.broadcast_to(owner_row, (256, 256))
    owner_t = jnp.transpose(owner_b)
    earlier = iota((256, 256), 0) < iota((256, 256), 1)
    same = jnp.where(owner_b == owner_t, 1.0, 0.0)
    rank = jnp.sum(jnp.where(earlier, same, 0.0), axis=0, keepdims=True)
    slot_row = jnp.where(rank < 7.0, owner_row * 8.0 + rank, 249.0 + rank)
    slot_b = jnp.broadcast_to(slot_row, (288, 256))
    hit = iota((288, 256), 0).astype(F32) == slot_b
    id_col = jnp.sum(jnp.where(hit, jnp.broadcast_to(id_row, (288, 256)) + 1.0, 0.0), axis=1, keepdims=True) - 1.0
    which = jnp.where(iota((256, 128), 1) == (iota((256, 128), 0) >> 4), 1.0, 0.0).astype(BF16)
    owned_by = dot(jnp.where(hit, 1.0, 0.0).astype(BF16), which)
    lane32 = iota((32, 128), 1)
    sub32 = iota((32, 128), 0)
    ext_row = jnp.sum(
        jnp.where(lane32 == sub32 + 96, jnp.broadcast_to(id_col[256:288], (32, 128)), 0.0), axis=0, keepdims=True
    )
    return id_col, owned_by, ext_row


def onehot_rows(rel, count):
    return jnp.where(
        jnp.broadcast_to(rel, (count, 2048)) == iota((count, 2048), 1).astype(F32), 1.0, 0.0
    ).astype(BF16)


def batcher(n):
    pairs = []
    p = 1
    while p < n:
        k = p
        while k >= 1:
            for j in range(k % p, n - k, 2 * k):
                for i in range(min(k, n - j - k)):
                    if (i + j) // (2 * p) == (i + j + k) // (2 * p):
                        pairs.append((i + j, i + j + k))
            k //= 2
        p *= 2
    return pairs


SORT16 = batcher(16)


def exchange(v, i, j):
    v[i], v[j] = jnp.minimum(v[i], v[j]), jnp.maximum(v[i], v[j])


def sort16(v):
    v = list(v)
    for i, j in SORT16:
        exchange(v, i, j)
    return v


def merge16(a, b):
    v = [jnp.minimum(a[i], b[15 - i]) for i in range(16)]
    for d in (8, 4, 2, 1):
        for i in range(16):
            if i & d == 0:
                exchange(v, i, i + d)
    return v


def sign_rows(table):
    hi = jnp.floor(table * (1.0 / 256.0))
    lo = table - 256.0 * hi
    both = jnp.concatenate([hi, lo], axis=1).astype(BF16)
    k = iota((1024, 256), 0)
    lane = iota((1024, 256), 1)
    source = (k >> 4) + jnp.where((k & 8) == 0, 128, 0)
    pick = jnp.where(lane == source, 1.0, 0.0).astype(BF16)
    byte = dot(pick, both, LAST).astype(jnp.int32)
    bit = byte & (1 << (iota((1024, 512), 0) & 7))
    return jnp.where(bit != 0, -1024.0, 1024.0).astype(BF16)


PORTIONS = ((0, 0, 4, (0, 1, 2)), (1, 0, 4, (1, 2, 0)), (2, 0, 4, (2, 0, 1)), (3, 0, 2, (0, 1, 2)), (3, 2, 2, (1, 0, 2)))
TAIL = (0, 1, 2, 3, 3)
STEPS = (2, 1, 3, 0)


def extents(p, stage):
    _, _, ys, order = PORTIONS[p]
    return [(a, ys if a == 2 else SIDE) for a in range(3) if a not in order[:stage]]


def split(v):
    high = v.astype(BF16)
    return high, (v - high.astype(F32)).astype(BF16)


def whole_kernel(
    qcodes_hbm, pos_hbm, neg_hbm, codes_hbm, bank_hbm, query_hbm, positive_hbm, head_hbm,
    out_hbm,
    qcodes, pos_in, neg_in, out_v,
    bank, codes, head, pay, owned, out_buf, in_buf, bsend, brecv, esend, eown, ecore, s1, r2a, r2b, s2a, s2b, r3a, r3b,
    signs, keys, pos, shard_best, crecv, packed, square, xs, dz, raw, unit, inv, u_hi, u_lo, u_qq, u_qqq,
    hs, core_in, parts, in1, mid, in2, tail, in3,
    load_sem, small_sem, p_sem, b_sem, t_sem, c_sem, x_send, x_recv, h_send, h_recv, r_send, r_recv,
):
    z, me, x, y, c = coords()
    others = peers(x, y, c)
    partner = (z, at(x, y, 1 - c))
    load_bank = pltpu.make_async_copy(bank_hbm, bank, load_sem.at[0])
    load_codes = pltpu.make_async_copy(codes_hbm, codes, load_sem.at[1])
    load_head = pltpu.make_async_copy(head_hbm, head, load_sem.at[2])
    small = [
        pltpu.make_async_copy(source, target, small_sem.at[i])
        for i, (source, target) in enumerate(
            (
                (neg_hbm, neg_in),
                (pos_hbm, pos_in),
                (qcodes_hbm, qcodes),
                (query_hbm, xs.at[pl.ds(0, 16)]),
                (positive_hbm, xs.at[pl.ds(16, 16)]),
            )
        )
    ]
    for load in small:
        load.start()
    load_bank.start()
    barrier = pltpu.get_barrier_semaphore()
    for peer in others:
        pl.semaphore_signal(barrier, inc=1, device_id=(z, peer), device_id_type=MESH)
    for k in range(1, SIDE):
        pl.semaphore_signal(barrier, inc=1, device_id=(lax.rem(z + k, SIDE), me), device_id_type=MESH)
    load_codes.start()
    load_head.start()

    for load in small[:3]:
        load.wait()
    pay[...] = jnp.zeros((8, 128), F32)
    pay[:, 64:80] = jnp.broadcast_to(pos_in[...].astype(F32), (8, 16))
    out_buf[:, 8:16, :] = jnp.broadcast_to(
        jnp.concatenate([qcodes[0:8], qcodes[8:16]], axis=1).astype(F32)[None], (32, 8, 128)
    )
    id_col, owned_by, ext_row = request_table(pos_in[...].astype(F32), neg_in[...].astype(F32))
    owned[...] = owned_by
    lane8 = iota((8, 128), 1)
    common = jnp.where(lane8 >= 96, jnp.broadcast_to(ext_row, (8, 128)), pay[...])
    base_cols = jnp.broadcast_to(id_col[0:256], (256, 128)).reshape(32, 8, 128)
    out_buf[:, 0:8, :] = jnp.where(
        iota((32, 8, 128), 2) == 0, base_cols, jnp.broadcast_to(common[None], (32, 8, 128))
    )
    pl.semaphore_wait(barrier, len(others) + SIDE - 1)
    for peer in others:
        copy_to(out_buf.at[peer], in_buf.at[me], p_sem.at[0], p_sem.at[1], (z, peer)).start()
    in_buf[me] = out_buf[me]

    for load in small[3:]:
        load.wait()

    def project(start, count):
        rows = slice(start, start + count)
        zed = dot(xs[rows], head[...])
        scale = 1.0 / jnp.sqrt(jnp.sum(zed * zed, axis=1, keepdims=True) + 1e-6)
        u = zed * scale
        unit[rows] = u
        inv[rows] = jnp.broadcast_to(scale, (count, 128))
        high, low = split(u)
        u_hi[rows] = high
        u_lo[rows] = low

    load_head.wait()
    project(0, 32)
    load_bank.wait()
    take(in_buf.at[pl.ds(0, GROUP - 1)], p_sem.at[1])

    first = (me * 2048).astype(F32)
    asked = in_buf[:, 0:8, :].reshape(256, 128)
    base_rel = jnp.sum(jnp.where(iota((256, 128), 1) == 0, asked, 0.0), axis=1, keepdims=True) - first
    hot = onehot_rows(base_rel, 256)
    for h in range(2):
        part = dot(hot, bank[:, h * 512 : (h + 1) * 512])
        bsend[:, 8 * h : 8 * h + 8, :] = part.reshape(32, 8, 512).astype(BF16)
    for peer in others:
        copy_to(bsend.at[peer], brecv.at[me], b_sem.at[0], b_sem.at[1], (z, peer)).start()
    brecv[me] = bsend[me]

    def extras(core):
        rows = in_buf[:, 0:1, :].reshape(16, 2, 1, 128)
        mine = jnp.where(core == 0, rows[:, 0], rows[:, 1])
        wide = jnp.broadcast_to(mine, (16, 32, 128))
        keep = iota((16, 32, 128), 2) == iota((16, 32, 128), 1) + 96
        rel = jnp.sum(jnp.where(keep, wide, 0.0), axis=2, keepdims=True).reshape(512, 1) - first
        return dot(onehot_rows(rel, 512), bank[...])

    esend[...] = extras(1 - c).reshape(16, 32, 1024).astype(BF16)
    core_copy = copy_to(esend, ecore, c_sem.at[0], c_sem.at[1], partner)
    core_copy.start()
    eown[...] = extras(c).reshape(16, 32, 1024).astype(BF16)
    core_copy.wait_recv()
    s1[...] = (eown[...].astype(F32) + ecore[...].astype(F32)).astype(BF16).reshape(4, 4, 32, 1024)

    left, right = pl.ds(0, 512), pl.ds(512, 512)
    for j in (2, 1, 3, 0):
        xj, yj = lax.rem(x + j, SIDE), lax.rem(y + j, SIDE)
        for k in (2, 1, 3):
            xk, yk = lax.rem(x + k, SIDE), lax.rem(y + k, SIDE)
            copy_to(
                s1.at[xk, yj, :, left], r2a.at[j, k - 1], x_send.at[0, j], x_recv.at[0, j], (z, at(xk, y, c))
            ).start()
            copy_to(
                s1.at[xj, yk, :, right], r2b.at[j, k - 1], x_send.at[1, j], x_recv.at[1, j], (z, at(x, yk, c))
            ).start()

    pairs = in_buf[:, 8:16, :]
    signs[...] = sign_rows(
        jnp.concatenate([pairs, pltpu.roll(pairs.reshape(256, 128), 64, 1).reshape(32, 8, 128)], axis=1).reshape(512, 128)
    )
    lane8 = iota((8, 128), 1)
    for t in range(4):
        row = jnp.zeros((8, 128), F32)
        for i in range(8):
            ids = pltpu.roll(in_buf[8 * t + i, 0:8], (16 * i + 64) % 128, 1)
            row = jnp.where((lane8 >> 4) == i, ids, row)
        pos[:, t * 128 : (t + 1) * 128] = row - first
    load_codes.wait()

    def product(m, carry):
        at_row = pl.multiple_of(m * 512, 512)
        keys[pl.ds(at_row, 512), :] = dot(codes[pl.ds(at_row, 512), :], signs[...])
        return carry

    lax.fori_loop(0, 4, product, 0)
    sub = iota((8, 128), 0)

    def select(t):
        lanes = slice(t * 128, (t + 1) * 128)
        wanted = pos[:, lanes]

        def load16(g):
            out = []
            for i in range(16):
                row = pl.multiple_of(g * 128 + i * 8, 8)
                p = (sub + (g * 128 + i * 8)).astype(F32)
                key = keys[pl.ds(row, 8), lanes] + (p + float(1 << 20))
                out.append(jnp.where(p == wanted, BIG, key))
            return out

        def step(g, best):
            return tuple(merge16(best, sort16(load16(g))))

        best = lax.fori_loop(1, 16, step, tuple(sort16(load16(0))))
        for d in (4, 2, 1):
            best = merge16(best, [pltpu.roll(b, d, 0) for b in best])
        for i in range(16):
            shard_best[t, i : i + 1, :] = best[i][0:1, :]

    def total(own, got):
        t = own.astype(F32)
        for k in range(SIDE - 1):
            t = t + got[k].astype(F32)
        return t

    def pass_on(j):
        xj, yj = lax.rem(x + j, SIDE), lax.rem(y + j, SIDE)
        take(r2a.at[j], x_recv.at[0, j])
        s2a[j] = total(s1[x, yj, :, 0:512], r2a.at[j]).astype(BF16)
        copy_to(s2a.at[j], r3a.at[j - 1], x_send.at[0, 4], x_recv.at[0, 4], (z, at(x, yj, c))).start()
        take(r2b.at[j], x_recv.at[1, j])
        s2b[j] = total(s1[xj, y, :, 512:1024], r2b.at[j]).astype(BF16)
        copy_to(s2b.at[j], r3b.at[j - 1], x_send.at[1, 4], x_recv.at[1, 4], (z, at(xj, y, c))).start()

    firsts = (((0,), (0,)), ((), ()))
    own_pos = jnp.where(iota((16, 16), 0) == iota((16, 16), 1), 1.0, 0.0)
    q_unit, q_hi, q_lo = unit[0:16], u_hi[0:16], u_lo[0:16]

    u_qq[0:16], u_qq[16:32] = q_hi, q_lo
    u_qqq[0:16], u_qqq[16:32], u_qqq[32:48] = q_hi, q_hi, q_lo

    def column(row):
        return jnp.sum(own_pos * jnp.broadcast_to(row, (16, 16)), axis=1, keepdims=True)

    def scores(start, count, mask):
        rows = slice(start, start + count)
        high, low = u_hi[rows], u_lo[rows]
        twice = dot(high, u_qq[...], LAST)
        logits = 50.0 * (twice[:, 0:16] + (dot(low, q_hi, LAST) + twice[:, 16:32]))
        logits = jnp.where(mask > 0.5, logits, 0.0)
        return logits, jnp.where(mask > 0.5, jnp.exp(logits), 0.0)

    def negatives(start, count):
        rows = slice(start, start + count)
        logits, w = scores(start, count, owned[start - 32 : start - 32 + count, 0:16])
        w_hi, w_lo = split(w)
        high, low = u_hi[rows], u_lo[rows]
        along = dot(w_hi, high, firsts) + (dot(w_lo, high, firsts) + dot(w_hi, low, firsts))
        scale = inv[rows, 0:1]
        k_hi, k_lo = split(w * (50.0 * scale))
        pull = dot(jnp.concatenate([k_hi, k_lo, k_hi], axis=1), u_qqq[...])
        k2 = jnp.sum(w * logits, axis=1, keepdims=True) * scale
        raw[start - 32 : start - 32 + count] = pull - unit[rows] * k2
        return jnp.sum(w, axis=0, keepdims=True), along

    select(0)
    select(1)
    take(brecv.at[pl.ds(0, GROUP - 1)], b_sem.at[1])
    got = brecv[...].astype(F32)
    xs[32:288, 0:512] = got[:, 0:8].reshape(256, 512).astype(BF16)
    xs[32:288, 512:1024] = got[:, 8:16].reshape(256, 512).astype(BF16)
    project(32, 256)
    pass_on(2)
    select(2)
    pos_logits, pos_w = scores(16, 16, own_pos)
    base_sum, base_along = negatives(32, 256)
    pass_on(1)
    select(3)
    pass_on(3)

    take(r2a.at[0], x_recv.at[0, 0])
    own_left = total(s1[x, y, :, 0:512], r2a.at[0])
    take(r2b.at[0], x_recv.at[1, 0])
    own_right = total(s1[x, y, :, 512:1024], r2b.at[0])
    take(r3a, x_recv.at[0, 4])
    xs[288:320, 0:512] = total(own_left, r3a).astype(BF16)
    take(r3b, x_recv.at[1, 4])
    xs[288:320, 512:1024] = total(own_right, r3b).astype(BF16)
    for peer in others:
        copy_to(shard_best.at[lax.div(peer, 8)], crecv.at[me], t_sem.at[0], t_sem.at[1], (z, peer)).start()
    crecv[me] = shard_best[lax.div(me, 8)]
    project(288, 32)
    ext_sum, ext_along = negatives(288, 32)

    share = 1.0 / (base_sum + ext_sum + jnp.sum(pos_w, axis=0, keepdims=True))
    slot_share = jnp.sum(owned[:, 0:16] * share, axis=1, keepdims=True)
    dz[32:320] = (raw[...] * slot_share).astype(BF16)
    pos_slope = column(jnp.sum(pos_w, axis=0, keepdims=True) * share - 1.0)
    pos_unit = unit[16:32]
    du = 50.0 * (column(share) * (base_along + ext_along) + pos_slope * pos_unit)
    dz[0:16] = ((du - q_unit * jnp.sum(q_unit * du, axis=1, keepdims=True)) * inv[0:16, 0:1]).astype(BF16)
    pos_logit = jnp.sum(pos_logits, axis=1, keepdims=True)
    dz[16:32] = (pos_slope * (50.0 * q_unit - pos_unit * pos_logit) * inv[16:32, 0:1]).astype(BF16)

    def h_copy(i):
        zz = lax.rem(z + STEPS[i], SIDE)
        return copy_to(hs.at[1 - c, zz], core_in.at[zz], h_send, h_recv.at[i], partner)

    def grow(i):
        zz = lax.rem(z + STEPS[i], SIDE)
        part = dot(xs[:, pl.ds(pl.multiple_of(zz * 256, 256), 256)], dz[...], firsts).reshape(32, 8, 1024)
        part = jnp.concatenate([part[:, :, 0:512], part[:, :, 512:1024]], axis=1).astype(BF16)
        part = part.reshape(4, 4, 2, 16, 512)
        for core in range(2):
            hs[core, zz] = part[:, :, core]
        h_copy(i).start()

    place = (z, x, y)

    def device(axis, to):
        where = [z, x, y]
        where[axis] = to
        return (where[0], at(where[1], where[2], c))

    def first_from(p, to):
        tile, y0, ys, order = PORTIONS[p]
        index = [slice(None), slice(None), pl.ds(y0, ys)]
        if order[0] == 2:
            index[2] = to
        else:
            index[order[0]] = to
        return (*index, slice(None), pl.ds(tile * 128, 128))

    def gather_core(i):
        zz = lax.rem(z + STEPS[i], SIDE)
        h_copy(i).wait_recv()
        parts[zz] = (hs[c, zz].astype(F32) + core_in[zz].astype(F32)).astype(BF16)
        for p in (3, 4, 0, 1, 2):
            tile, y0, ys, order = PORTIONS[p]
            lanes = pl.ds(tile * 128, 128)
            if order[0] == 0:
                moves = [(zz, parts.at[zz, :, pl.ds(y0, ys), :, lanes], in1[p].at[STEPS[i] - 1])] if STEPS[i] else []
            else:
                moves = []
                for k in (2, 1, 3):
                    to = lax.rem(place[order[0]] + k, SIDE)
                    if order[0] == 1:
                        source = parts.at[zz, to, pl.ds(y0, ys), :, lanes]
                    else:
                        source = parts.at[zz, :, to, :, lanes]
                    moves.append((to, source, in1[p].at[k - 1, zz]))
            for to, source, target in moves:
                copy_to(source, target, r_send.at[0, p], r_recv.at[0, p], device(order[0], to)).start()

    grow(0)
    grow(1)
    gather_core(0)
    grow(2)
    gather_core(1)
    grow(3)
    gather_core(2)
    gather_core(3)

    out_v[8:40] = dot(dz[0:32], head[...], LAST)

    def pick(p, stage, to):
        axis = PORTIONS[p][3][stage]
        return tuple(to if a == axis else slice(None) for a, _ in extents(p, stage))

    for p in (1, 2, 4, 0, 3):
        axis = PORTIONS[p][3][0]
        take(in1[p], r_recv.at[0, p])
        mid[p][...] = total(parts[first_from(p, place[axis])], in1[p]).astype(BF16)
        axis = PORTIONS[p][3][1]
        for k in (2, 1, 3):
            to = lax.rem(place[axis] + k, SIDE)
            copy_to(
                mid[p].at[pick(p, 1, to)], in2[p].at[k - 1], r_send.at[1, p], r_recv.at[1, p], device(axis, to)
            ).start()
    for p in (1, 2, 4, 0, 3):
        axis = PORTIONS[p][3][1]
        take(in2[p], r_recv.at[1, p])
        _, y0, ys, order = PORTIONS[p]
        sums = total(mid[p][pick(p, 1, place[axis])], in2[p]).astype(BF16)
        if TAIL[p] == 3:
            tail[3, y0 : y0 + ys] = sums
        else:
            tail[p] = sums
        if p == 4:
            continue
        q = TAIL[p]
        axis = order[2]
        for k in (2, 1, 3):
            to = lax.rem(place[axis] + k, SIDE)
            copy_to(
                tail.at[q, to], in3.at[q, k - 1], r_send.at[2, q], r_recv.at[2, q], device(axis, to)
            ).start()
    take(crecv.at[pl.ds(0, GROUP - 1)], t_sem.at[1])
    lane = iota((16, 128), 1)
    packed[...] = jnp.full((8, 16, 128), 2147483647, jnp.int32)
    mine = lax.rem(me, 8)
    for g in range(4):
        merged = jnp.zeros((16, 128), jnp.int32)
        for s in range(8):
            key = crecv[g * 8 + s].astype(jnp.int32)
            key = ((key >> 11) << 16) + (key & 2047) + (g * 8 + s) * 2048
            key = pltpu.roll(key, lax.rem((s - mine + 8) * 16, 128), 1)
            merged = jnp.where((lane >> 4) == s, key, merged)
        packed[g] = merged
    best = [packed[:, i, :] for i in range(16)]
    for d in (64, 32, 16):
        best = merge16(best, [pltpu.roll(b, d, 1) for b in best])
    for d in (6, 7):
        best = merge16(best, [pltpu.roll(b, d, 0) for b in best])
    square[...] = jnp.zeros((128, 128), jnp.int32)
    for i in range(16):
        square[i : i + 1, :] = best[i][0:1, :]
    flat = square[...]
    out_v[40:56, 0:128] = jnp.transpose((flat & 65535).astype(F32))[0:16]
    out_v[40:56, 128:256] = jnp.transpose((flat >> 16).astype(F32))[0:16]
    early = pltpu.make_async_copy(out_v.at[pl.ds(8, 48)], out_hbm.at[pl.ds(8, 48)], small_sem.at[0])
    early.start()

    for q in range(4):
        take(in3.at[q], r_recv.at[2, q])
        out = total(tail[q, place[PORTIONS[q][3][2]]], in3.at[q])
        out_v[0:8, q * 128 : (q + 1) * 128] = out[0:8]
        out_v[0:8, 512 + q * 128 : 512 + (q + 1) * 128] = out[8:16]
    late = pltpu.make_async_copy(out_v.at[pl.ds(0, 8)], out_hbm.at[pl.ds(0, 8)], small_sem.at[1])
    late.start()

    take(out_buf.at[pl.ds(0, GROUP - 1)], p_sem.at[0])
    take(bsend.at[pl.ds(0, GROUP - 1)], b_sem.at[0])
    take(crecv.at[pl.ds(0, GROUP - 1)], t_sem.at[0])
    core_copy.wait_send()
    for j in range(SIDE):
        take(r2a.at[j], x_send.at[0, j])
        take(r2b.at[j], x_send.at[1, j])
    take(r3a, x_send.at[0, 4])
    take(r3b, x_send.at[1, 4])
    take(core_in, h_send)
    for p in range(5):
        take(in1[p], r_send.at[0, p])
        take(in2[p], r_send.at[1, p])
    for q in range(4):
        take(in3.at[q], r_send.at[2, q])
    early.wait()
    late.wait()


def whole(codes, pos, neg, bank_codes, bank_emb, query_emb, positive_emb, head):
    anywhere = pl.BlockSpec(memory_space=pl.ANY)
    dma = pltpu.SemaphoreType.DMA
    block = (16, 128)

    def by_portion(stage, lead):
        return [pltpu.VMEM((*lead, *(n for _, n in extents(p, stage)), *block), BF16) for p in range(5)]

    return pl.pallas_call(
        whole_kernel,
        out_shape=jax.ShapeDtypeStruct((56, 1024), F32),
        in_specs=[anywhere] * 8,
        out_specs=anywhere,
        scratch_shapes=[
            pltpu.VMEM((16, 64), jnp.int32),
            pltpu.VMEM((1, 16), jnp.int32),
            pltpu.VMEM((16, 16), jnp.int32),
            pltpu.VMEM((56, 1024), F32),
            pltpu.VMEM((2048, 1024), BF16),
            pltpu.VMEM((2048, 1024), BF16),
            pltpu.VMEM((1024, 1024), BF16),
            pltpu.VMEM((8, 128), F32),
            pltpu.VMEM((288, 128), F32),
            pltpu.VMEM((32, 16, 128), F32),
            pltpu.VMEM((32, 16, 128), F32),
            pltpu.VMEM((32, 16, 512), BF16),
            pltpu.VMEM((32, 16, 512), BF16),
            pltpu.VMEM((16, 32, 1024), BF16),
            pltpu.VMEM((16, 32, 1024), BF16),
            pltpu.VMEM((16, 32, 1024), BF16),
            pltpu.VMEM((4, 4, 32, 1024), BF16),
            pltpu.VMEM((4, 3, 32, 512), BF16),
            pltpu.VMEM((4, 3, 32, 512), BF16),
            pltpu.VMEM((4, 32, 512), BF16),
            pltpu.VMEM((4, 32, 512), BF16),
            pltpu.VMEM((3, 32, 512), BF16),
            pltpu.VMEM((3, 32, 512), BF16),
            pltpu.VMEM((1024, 512), BF16),
            pltpu.VMEM((2048, 512), F32),
            pltpu.VMEM((8, 512), F32),
            pltpu.VMEM((4, 16, 128), F32),
            pltpu.VMEM((32, 16, 128), F32),
            pltpu.VMEM((8, 16, 128), jnp.int32),
            pltpu.VMEM((128, 128), jnp.int32),
            pltpu.VMEM((320, 1024), BF16),
            pltpu.VMEM((320, 1024), BF16),
            pltpu.VMEM((288, 1024), F32),
            pltpu.VMEM((320, 1024), F32),
            pltpu.VMEM((320, 128), F32),
            pltpu.VMEM((320, 1024), BF16),
            pltpu.VMEM((320, 1024), BF16),
            pltpu.VMEM((32, 1024), BF16),
            pltpu.VMEM((48, 1024), BF16),
            pltpu.VMEM((2, 4, 4, 4, 16, 512), BF16),
            pltpu.VMEM((4, 4, 4, 16, 512), BF16),
            pltpu.VMEM((4, 4, 4, 16, 512), BF16),
            by_portion(1, (3,)),
            by_portion(1, ()),
            by_portion(2, (3,)),
            pltpu.VMEM((4, 4, *block), BF16),
            pltpu.VMEM((4, 3, *block), BF16),
            dma((3,)),
            dma((5,)),
            dma((2,)),
            dma((2,)),
            dma((2,)),
            dma((2,)),
            dma((2, 5)),
            dma((2, 5)),
            dma,
            dma((4,)),
            dma((3, 5)),
            dma((3, 5)),
        ],
        compiler_params=pltpu.CompilerParams(
            collective_id=0, has_side_effects=True, vmem_limit_bytes=60 * MIB
        ),
        name="whole",
    )(codes, pos, neg, bank_codes, bank_emb, query_emb, positive_emb, head)


OUT = (((16, 16), jnp.int32), ((16, 16), jnp.int32), ((16, 1024), BF16), ((16, 1024), BF16), ((8, 1024), F32))


def emit_kernel(packed_ref, *refs):
    targets, held, sem = refs[0:5], refs[5:9], refs[9]
    held[0][...] = packed_ref[40:56, 0:16].astype(jnp.int32)
    held[1][...] = packed_ref[40:56, 128:144].astype(jnp.int32)
    held[2][...] = packed_ref[8:24].astype(BF16)
    held[3][...] = packed_ref[24:40].astype(BF16)
    sources = (*held, packed_ref.at[pl.ds(0, 8)])
    copies = [pltpu.make_async_copy(a, b, sem.at[i]) for i, (a, b) in enumerate(zip(sources, targets))]
    for copy in copies:
        copy.start()
    for copy in copies:
        copy.wait()


def emit(packed):
    return pl.pallas_call(
        emit_kernel,
        out_shape=tuple(jax.ShapeDtypeStruct(*o) for o in OUT),
        in_specs=[pl.BlockSpec(memory_space=pltpu.VMEM)],
        out_specs=(pl.BlockSpec(memory_space=pl.ANY),) * 5,
        scratch_shapes=[*(pltpu.VMEM(*o) for o in OUT[:4]), pltpu.SemaphoreType.DMA((5,))],
        name="emit",
    )(packed)


def local(
    query_codes, positive_ids, negative_ids, bank_codes, bank_emb, query_emb, positive_emb, head
):
    return emit(
        whole(query_codes, positive_ids.reshape(1, -1), negative_ids, bank_codes, bank_emb, query_emb, positive_emb, head)
    )


def solution(mesh):
    both = ("dp", "index")
    rows = P(both, None)
    return jax.shard_map(
        local,
        mesh=mesh,
        in_specs=(rows, P(both), rows, P("index", None), P("index", None), rows, rows, P()),
        out_specs=(rows,) * 5,
        check_vma=False,
    )
```

```python
import functools

import jax
import jax.numpy as jnp
from jax import lax
from jax.experimental import pallas as pl
from jax.experimental.pallas import tpu as pltpu
from jax.sharding import PartitionSpec as P

F32 = jnp.float32
BF16 = jnp.bfloat16
MESH = pl.DeviceIdType.MESH
MIB = 1 << 20
GROUP = 32
SIDE = 4
BIG = float(1 << 23)
LAST = (((1,), (1,)), ((), ()))


def iota(shape, dim):
    return lax.broadcasted_iota(jnp.int32, shape, dim)


def dot(a, b, dims=(((1,), (0,)), ((), ()))):
    return lax.dot_general(a, b, dims, preferred_element_type=F32)


def copy_to(src, dst, send_sem, recv_sem, device):
    return pltpu.make_async_remote_copy(
        src_ref=src,
        dst_ref=dst,
        send_sem=send_sem,
        recv_sem=recv_sem,
        device_id=device,
        device_id_type=MESH,
    )


def coords():
    z = lax.axis_index("dp")
    me = lax.axis_index("index")
    x = lax.div(me, 8)
    y = lax.rem(lax.div(me, 2), 4)
    c = lax.rem(me, 2)
    return z, me, x, y, c


def at(x, y, c):
    return x * 8 + y * 2 + c


OFFSETS = sorted(
    ((dx, dy, dc) for dx in range(4) for dy in range(4) for dc in range(2) if dx or dy or dc),
    key=lambda o: -(min(o[0], 4 - o[0]) + min(o[1], 4 - o[1])),
)


def peers(x, y, c):
    return [at(lax.rem(x + dx, 4), lax.rem(y + dy, 4), lax.rem(c + dc, 2)) for dx, dy, dc in OFFSETS]


def take(ref, sem):
    pltpu.make_async_copy(ref, ref, sem).wait()


def request_table(pos_row, negatives):
    hi = jnp.floor(negatives * (1.0 / 256.0))
    lo = negatives - 256.0 * hi
    halves = jnp.concatenate([hi, lo], axis=0).astype(BF16)
    spread = jnp.where(iota((16, 256), 0) == (iota((16, 256), 1) & 15), 1.0, 0.0).astype(BF16)
    got = dot(halves, spread)
    ids = 256.0 * got[0:16] + got[16:32]
    ids = jnp.where(iota((16, 256), 0) == (iota((16, 256), 1) >> 4), ids, 0.0)
    id_row = jnp.sum(ids, axis=0, keepdims=True)
    owner_row = jnp.floor(id_row * (1.0 / 2048.0))
    owner_b = jnp.broadcast_to(owner_row, (256, 256))
    owner_t = jnp.transpose(owner_b)
    earlier = iota((256, 256), 0) < iota((256, 256), 1)
    same = jnp.where(owner_b == owner_t, 1.0, 0.0)
    rank = jnp.sum(jnp.where(earlier, same, 0.0), axis=0, keepdims=True)
    slot_row = jnp.where(rank < 7.0, owner_row * 8.0 + rank, 249.0 + rank)
    slot_b = jnp.broadcast_to(slot_row, (288, 256))
    hit = iota((288, 256), 0).astype(F32) == slot_b
    id_col = jnp.sum(jnp.where(hit, jnp.broadcast_to(id_row, (288, 256)) + 1.0, 0.0), axis=1, keepdims=True) - 1.0
    which = jnp.where(iota((256, 128), 1) == (iota((256, 128), 0) >> 4), 1.0, 0.0).astype(BF16)
    owned_by = dot(jnp.where(hit, 1.0, 0.0).astype(BF16), which)
    lane32 = iota((32, 128), 1)
    sub32 = iota((32, 128), 0)
    ext_row = jnp.sum(
        jnp.where(lane32 == sub32 + 96, jnp.broadcast_to(id_col[256:288], (32, 128)), 0.0), axis=0, keepdims=True
    )
    return id_col, owned_by, ext_row


def onehot_rows(rel, count):
    return jnp.where(
        jnp.broadcast_to(rel, (count, 2048)) == iota((count, 2048), 1).astype(F32), 1.0, 0.0
    ).astype(BF16)


def batcher(n):
    pairs = []
    p = 1
    while p < n:
        k = p
        while k >= 1:
            for j in range(k % p, n - k, 2 * k):
                for i in range(min(k, n - j - k)):
                    if (i + j) // (2 * p) == (i + j + k) // (2 * p):
                        pairs.append((i + j, i + j + k))
            k //= 2
        p *= 2
    return pairs


SORT16 = batcher(16)


def exchange(v, i, j):
    v[i], v[j] = jnp.minimum(v[i], v[j]), jnp.maximum(v[i], v[j])


def sort16(v):
    v = list(v)
    for i, j in SORT16:
        exchange(v, i, j)
    return v


def merge16(a, b):
    v = [jnp.minimum(a[i], b[15 - i]) for i in range(16)]
    for d in (8, 4, 2, 1):
        for i in range(16):
            if i & d == 0:
                exchange(v, i, i + d)
    return v


def sign_rows(table):
    hi = jnp.floor(table * (1.0 / 256.0))
    lo = table - 256.0 * hi
    both = jnp.concatenate([hi, lo], axis=1).astype(BF16)
    k = iota((1024, 256), 0)
    lane = iota((1024, 256), 1)
    source = (k >> 4) + jnp.where((k & 8) == 0, 128, 0)
    pick = jnp.where(lane == source, 1.0, 0.0).astype(BF16)
    byte = dot(pick, both, LAST).astype(jnp.int32)
    bit = byte & (1 << (iota((1024, 512), 0) & 7))
    return jnp.where(bit != 0, -1024.0, 1024.0).astype(BF16)


PORTIONS = ((0, 0, 4, (0, 1, 2)), (1, 0, 4, (1, 2, 0)), (2, 0, 4, (2, 0, 1)), (3, 0, 2, (0, 1, 2)), (3, 2, 2, (1, 0, 2)))
TAIL = (0, 1, 2, 3, 3)
STEPS = (2, 1, 3, 0)


def extents(p, stage):
    _, _, ys, order = PORTIONS[p]
    return [(a, ys if a == 2 else SIDE) for a in range(3) if a not in order[:stage]]


def split(v):
    high = v.astype(BF16)
    return high, (v - high.astype(F32)).astype(BF16)


def whole_kernel(
    qcodes_hbm, pos_hbm, neg_hbm, codes_hbm, bank_hbm, query_hbm, positive_hbm, head_hbm,
    out_hbm,
    qcodes, pos_in, neg_in, out_v,
    bank, codes, head, pay, owned, out_buf, in_buf, bsend, brecv, esend, eown, ecore, s1, relay, both, r2a, r2b, s2a, s2b, r3a, r3b,
    signs, keys, pos, shard_best, crecv, packed, square, xs, dz, raw, unit, inv, u_hi, u_lo, u_qq, u_qqq,
    hs, core_in, parts, in1, mid, in2, tail, in3,
    load_sem, small_sem, p_sem, b_sem, t_sem, c_sem, x_send, x_recv, h_send, h_recv, r_send, r_recv,
):
    z, me, x, y, c = coords()
    others = peers(x, y, c)
    partner = (z, at(x, y, 1 - c))
    load_bank = pltpu.make_async_copy(bank_hbm, bank, load_sem.at[0])
    load_codes = pltpu.make_async_copy(codes_hbm, codes, load_sem.at[1])
    load_head = pltpu.make_async_copy(head_hbm, head, load_sem.at[2])
    small = [
        pltpu.make_async_copy(source, target, small_sem.at[i])
        for i, (source, target) in enumerate(
            (
                (neg_hbm, neg_in),
                (pos_hbm, pos_in),
                (qcodes_hbm, qcodes),
                (query_hbm, xs.at[pl.ds(0, 16)]),
                (positive_hbm, xs.at[pl.ds(16, 16)]),
            )
        )
    ]
    for load in small:
        load.start()
    load_bank.start()
    barrier = pltpu.get_barrier_semaphore()
    for peer in others:
        pl.semaphore_signal(barrier, inc=1, device_id=(z, peer), device_id_type=MESH)
    for k in range(1, SIDE):
        pl.semaphore_signal(barrier, inc=1, device_id=(lax.rem(z + k, SIDE), me), device_id_type=MESH)
    load_codes.start()
    load_head.start()

    for load in small[:3]:
        load.wait()
    pay[...] = jnp.zeros((8, 128), F32)
    pay[:, 64:80] = jnp.broadcast_to(pos_in[...].astype(F32), (8, 16))
    out_buf[:, 8:16, :] = jnp.broadcast_to(
        jnp.concatenate([qcodes[0:8], qcodes[8:16]], axis=1).astype(F32)[None], (32, 8, 128)
    )
    id_col, owned_by, ext_row = request_table(pos_in[...].astype(F32), neg_in[...].astype(F32))
    owned[...] = owned_by
    lane8 = iota((8, 128), 1)
    common = jnp.where(lane8 >= 96, jnp.broadcast_to(ext_row, (8, 128)), pay[...])
    base_cols = jnp.broadcast_to(id_col[0:256], (256, 128)).reshape(32, 8, 128)
    out_buf[:, 0:8, :] = jnp.where(
        iota((32, 8, 128), 2) == 0, base_cols, jnp.broadcast_to(common[None], (32, 8, 128))
    )
    pl.semaphore_wait(barrier, len(others) + SIDE - 1)
    for peer in others:
        copy_to(out_buf.at[peer], in_buf.at[me], p_sem.at[0], p_sem.at[1], (z, peer)).start()
    in_buf[me] = out_buf[me]

    for load in small[3:]:
        load.wait()

    def project(start, count):
        rows = slice(start, start + count)
        zed = dot(xs[rows], head[...])
        scale = 1.0 / jnp.sqrt(jnp.sum(zed * zed, axis=1, keepdims=True) + 1e-6)
        u = zed * scale
        unit[rows] = u
        inv[rows] = jnp.broadcast_to(scale, (count, 128))
        high, low = split(u)
        u_hi[rows] = high
        u_lo[rows] = low

    load_head.wait()
    project(0, 32)
    load_bank.wait()
    take(in_buf.at[pl.ds(0, GROUP - 1)], p_sem.at[1])

    first = (me * 2048).astype(F32)
    asked = in_buf[:, 0:8, :].reshape(256, 128)
    base_rel = jnp.sum(jnp.where(iota((256, 128), 1) == 0, asked, 0.0), axis=1, keepdims=True) - first
    hot = onehot_rows(base_rel, 256)
    for h in range(2):
        part = dot(hot, bank[:, h * 512 : (h + 1) * 512])
        bsend[:, 8 * h : 8 * h + 8, :] = part.reshape(32, 8, 512).astype(BF16)
    for peer in others:
        copy_to(bsend.at[peer], brecv.at[me], b_sem.at[0], b_sem.at[1], (z, peer)).start()
    brecv[me] = bsend[me]

    def extras(core):
        rows = in_buf[:, 0:1, :].reshape(16, 2, 1, 128)
        mine = jnp.where(core == 0, rows[:, 0], rows[:, 1])
        wide = jnp.broadcast_to(mine, (16, 32, 128))
        keep = iota((16, 32, 128), 2) == iota((16, 32, 128), 1) + 96
        rel = jnp.sum(jnp.where(keep, wide, 0.0), axis=2, keepdims=True).reshape(512, 1) - first
        return dot(onehot_rows(rel, 512), bank[...])

    esend[...] = extras(1 - c).reshape(16, 32, 1024).astype(BF16)
    core_copy = copy_to(esend, ecore, c_sem.at[0], c_sem.at[1], partner)
    core_copy.start()
    eown[...] = extras(c).reshape(16, 32, 1024).astype(BF16)
    core_copy.wait_recv()
    s1[...] = (eown[...].astype(F32) + ecore[...].astype(F32)).astype(BF16).reshape(4, 4, 32, 1024)

    x1, x2, x3 = (lax.rem(x + k, SIDE) for k in (1, 2, 3))
    y1, y2, y3 = (lax.rem(y + k, SIDE) for k in (1, 2, 3))
    quarter = [pl.ds(256 * i, 256) for i in range(4)]
    next_x, last_x = (z, at(x1, y, c)), (z, at(x3, y, c))
    next_y, last_y = (z, at(x, y1, c)), (z, at(x, y3, c))
    copy_to(s1.at[x2, :, :, quarter[0]], relay.at[0], x_send.at[0, 5], x_recv.at[0, 5], next_x).start()
    copy_to(s1.at[:, y2, :, quarter[2]], relay.at[2], x_send.at[1, 5], x_recv.at[1, 5], next_y).start()
    copy_to(s1.at[x2, :, :, quarter[1]], relay.at[1], x_send.at[0, 6], x_recv.at[0, 6], last_x).start()
    copy_to(s1.at[:, y2, :, quarter[3]], relay.at[3], x_send.at[1, 6], x_recv.at[1, 6], last_y).start()

    def send_two(j, sources):
        for source, got, half, i, to in zip(
            sources[0], (r2a.at[j, 0], r2a.at[j, 1], r2b.at[j, 0], r2b.at[j, 1]), sources[1], (0, 0, 1, 1),
            (next_x, last_x, next_y, last_y),
        ):
            copy_to(source, got.at[:, quarter[half]], x_send.at[i, j], x_recv.at[i, j], to).start()

    for j in (2, 1, 3, 0):
        xj, yj = lax.rem(x + j, SIDE), lax.rem(y + j, SIDE)
        plain = (
            s1.at[x1, yj, :, quarter[1]],
            s1.at[x3, yj, :, quarter[0]],
            s1.at[xj, y1, :, quarter[3]],
            s1.at[xj, y3, :, quarter[2]],
        )
        send_two(j, (plain, (1, 0, 1, 0)))

    def relayed():
        for i, own in enumerate(
            (
                lambda: s1[x1, :, :, 0:256],
                lambda: s1[x3, :, :, 256:512],
                lambda: s1[:, y1, :, 512:768],
                lambda: s1[:, y3, :, 768:1024],
            )
        ):
            take(relay.at[i], x_recv.at[i // 2, 5 + i % 2])
            both[i] = (own().astype(F32) + relay[i].astype(F32)).astype(BF16)
        for j in (2, 1, 3, 0):
            xj, yj = lax.rem(x + j, SIDE), lax.rem(y + j, SIDE)
            send_two(j, ((both.at[0, yj], both.at[1, yj], both.at[2, xj], both.at[3, xj]), (0, 1, 0, 1)))

    pairs = in_buf[:, 8:16, :]
    signs[...] = sign_rows(
        jnp.concatenate([pairs, pltpu.roll(pairs.reshape(256, 128), 64, 1).reshape(32, 8, 128)], axis=1).reshape(512, 128)
    )
    lane8 = iota((8, 128), 1)
    for t in range(4):
        row = jnp.zeros((8, 128), F32)
        for i in range(8):
            ids = pltpu.roll(in_buf[8 * t + i, 0:8], (16 * i + 64) % 128, 1)
            row = jnp.where((lane8 >> 4) == i, ids, row)
        pos[:, t * 128 : (t + 1) * 128] = row - first
    load_codes.wait()

    def product(m, carry):
        at_row = pl.multiple_of(m * 512, 512)
        keys[pl.ds(at_row, 512), :] = dot(codes[pl.ds(at_row, 512), :], signs[...])
        return carry

    lax.fori_loop(0, 4, product, 0)
    relayed()
    sub = iota((8, 128), 0)

    def select(t):
        lanes = slice(t * 128, (t + 1) * 128)
        wanted = pos[:, lanes]

        def load16(g):
            out = []
            for i in range(16):
                row = pl.multiple_of(g * 128 + i * 8, 8)
                p = (sub + (g * 128 + i * 8)).astype(F32)
                key = keys[pl.ds(row, 8), lanes] + (p + float(1 << 20))
                out.append(jnp.where(p == wanted, BIG, key))
            return out

        def step(g, best):
            return tuple(merge16(best, sort16(load16(g))))

        best = lax.fori_loop(1, 16, step, tuple(sort16(load16(0))))
        for d in (4, 2, 1):
            best = merge16(best, [pltpu.roll(b, d, 0) for b in best])
        for i in range(16):
            shard_best[t, i : i + 1, :] = best[i][0:1, :]

    def total(own, got, count=SIDE - 1):
        t = own.astype(F32)
        for k in range(count):
            t = t + got[k].astype(F32)
        return t

    def pass_on(j):
        xj, yj = lax.rem(x + j, SIDE), lax.rem(y + j, SIDE)
        take(r2a.at[j], x_recv.at[0, j])
        s2a[j] = total(s1[x, yj, :, 0:512], r2a.at[j], 2).astype(BF16)
        copy_to(s2a.at[j], r3a.at[j - 1], x_send.at[0, 4], x_recv.at[0, 4], (z, at(x, yj, c))).start()
        take(r2b.at[j], x_recv.at[1, j])
        s2b[j] = total(s1[xj, y, :, 512:1024], r2b.at[j], 2).astype(BF16)
        copy_to(s2b.at[j], r3b.at[j - 1], x_send.at[1, 4], x_recv.at[1, 4], (z, at(xj, y, c))).start()

    firsts = (((0,), (0,)), ((), ()))
    own_pos = jnp.where(iota((16, 16), 0) == iota((16, 16), 1), 1.0, 0.0)
    q_unit, q_hi, q_lo = unit[0:16], u_hi[0:16], u_lo[0:16]

    u_qq[0:16], u_qq[16:32] = q_hi, q_lo
    u_qqq[0:16], u_qqq[16:32], u_qqq[32:48] = q_hi, q_hi, q_lo

    def column(row):
        return jnp.sum(own_pos * jnp.broadcast_to(row, (16, 16)), axis=1, keepdims=True)

    def scores(start, count, mask):
        rows = slice(start, start + count)
        high, low = u_hi[rows], u_lo[rows]
        twice = dot(high, u_qq[...], LAST)
        logits = 50.0 * (twice[:, 0:16] + (dot(low, q_hi, LAST) + twice[:, 16:32]))
        logits = jnp.where(mask > 0.5, logits, 0.0)
        return logits, jnp.where(mask > 0.5, jnp.exp(logits), 0.0)

    def negatives(start, count):
        rows = slice(start, start + count)
        logits, w = scores(start, count, owned[start - 32 : start - 32 + count, 0:16])
        w_hi, w_lo = split(w)
        high, low = u_hi[rows], u_lo[rows]
        along = dot(w_hi, high, firsts) + (dot(w_lo, high, firsts) + dot(w_hi, low, firsts))
        scale = inv[rows, 0:1]
        k_hi, k_lo = split(w * (50.0 * scale))
        pull = dot(jnp.concatenate([k_hi, k_lo, k_hi], axis=1), u_qqq[...])
        k2 = jnp.sum(w * logits, axis=1, keepdims=True) * scale
        raw[start - 32 : start - 32 + count] = pull - unit[rows] * k2
        return jnp.sum(w, axis=0, keepdims=True), along

    select(0)
    select(1)
    take(brecv.at[pl.ds(0, GROUP - 1)], b_sem.at[1])
    got = brecv[...].astype(F32)
    xs[32:288, 0:512] = got[:, 0:8].reshape(256, 512).astype(BF16)
    xs[32:288, 512:1024] = got[:, 8:16].reshape(256, 512).astype(BF16)
    project(32, 256)
    pass_on(2)
    select(2)
    pos_logits, pos_w = scores(16, 16, own_pos)
    base_sum, base_along = negatives(32, 256)
    pass_on(1)
    select(3)
    pass_on(3)

    take(r2a.at[0], x_recv.at[0, 0])
    own_left = total(s1[x, y, :, 0:512], r2a.at[0], 2)
    take(r2b.at[0], x_recv.at[1, 0])
    own_right = total(s1[x, y, :, 512:1024], r2b.at[0], 2)
    take(r3a, x_recv.at[0, 4])
    xs[288:320, 0:512] = total(own_left, r3a).astype(BF16)
    take(r3b, x_recv.at[1, 4])
    xs[288:320, 512:1024] = total(own_right, r3b).astype(BF16)
    for peer in others:
        copy_to(shard_best.at[lax.div(peer, 8)], crecv.at[me], t_sem.at[0], t_sem.at[1], (z, peer)).start()
    crecv[me] = shard_best[lax.div(me, 8)]
    project(288, 32)
    ext_sum, ext_along = negatives(288, 32)

    share = 1.0 / (base_sum + ext_sum + jnp.sum(pos_w, axis=0, keepdims=True))
    slot_share = jnp.sum(owned[:, 0:16] * share, axis=1, keepdims=True)
    dz[32:320] = (raw[...] * slot_share).astype(BF16)
    pos_slope = column(jnp.sum(pos_w, axis=0, keepdims=True) * share - 1.0)
    pos_unit = unit[16:32]
    du = 50.0 * (column(share) * (base_along + ext_along) + pos_slope * pos_unit)
    dz[0:16] = ((du - q_unit * jnp.sum(q_unit * du, axis=1, keepdims=True)) * inv[0:16, 0:1]).astype(BF16)
    pos_logit = jnp.sum(pos_logits, axis=1, keepdims=True)
    dz[16:32] = (pos_slope * (50.0 * q_unit - pos_unit * pos_logit) * inv[16:32, 0:1]).astype(BF16)

    def h_copy(i):
        zz = lax.rem(z + STEPS[i], SIDE)
        return copy_to(hs.at[1 - c, zz], core_in.at[zz], h_send, h_recv.at[i], partner)

    def grow(i):
        zz = lax.rem(z + STEPS[i], SIDE)
        part = dot(xs[:, pl.ds(pl.multiple_of(zz * 256, 256), 256)], dz[...], firsts).reshape(32, 8, 1024)
        part = jnp.concatenate([part[:, :, 0:512], part[:, :, 512:1024]], axis=1).astype(BF16)
        part = part.reshape(4, 4, 2, 16, 512)
        for core in range(2):
            hs[core, zz] = part[:, :, core]
        h_copy(i).start()

    place = (z, x, y)

    def device(axis, to):
        where = [z, x, y]
        where[axis] = to
        return (where[0], at(where[1], where[2], c))

    def first_from(p, to):
        tile, y0, ys, order = PORTIONS[p]
        index = [slice(None), slice(None), pl.ds(y0, ys)]
        if order[0] == 2:
            index[2] = to
        else:
            index[order[0]] = to
        return (*index, slice(None), pl.ds(tile * 128, 128))

    def gather_core(i):
        zz = lax.rem(z + STEPS[i], SIDE)
        h_copy(i).wait_recv()
        parts[zz] = (hs[c, zz].astype(F32) + core_in[zz].astype(F32)).astype(BF16)
        for p in (3, 4, 0, 1, 2):
            tile, y0, ys, order = PORTIONS[p]
            lanes = pl.ds(tile * 128, 128)
            if order[0] == 0:
                moves = [(zz, parts.at[zz, :, pl.ds(y0, ys), :, lanes], in1[p].at[STEPS[i] - 1])] if STEPS[i] else []
            else:
                moves = []
                for k in (2, 1, 3):
                    to = lax.rem(place[order[0]] + k, SIDE)
                    if order[0] == 1:
                        source = parts.at[zz, to, pl.ds(y0, ys), :, lanes]
                    else:
                        source = parts.at[zz, :, to, :, lanes]
                    moves.append((to, source, in1[p].at[k - 1, zz]))
            for to, source, target in moves:
                copy_to(source, target, r_send.at[0, p], r_recv.at[0, p], device(order[0], to)).start()

    grow(0)
    grow(1)
    gather_core(0)
    grow(2)
    gather_core(1)
    grow(3)
    gather_core(2)
    gather_core(3)

    out_v[8:40] = dot(dz[0:32], head[...], LAST)

    def pick(p, stage, to):
        axis = PORTIONS[p][3][stage]
        return tuple(to if a == axis else slice(None) for a, _ in extents(p, stage))

    for p in (1, 2, 4, 0, 3):
        axis = PORTIONS[p][3][0]
        take(in1[p], r_recv.at[0, p])
        mid[p][...] = total(parts[first_from(p, place[axis])], in1[p]).astype(BF16)
        axis = PORTIONS[p][3][1]
        for k in (2, 1, 3):
            to = lax.rem(place[axis] + k, SIDE)
            copy_to(
                mid[p].at[pick(p, 1, to)], in2[p].at[k - 1], r_send.at[1, p], r_recv.at[1, p], device(axis, to)
            ).start()
    for p in (1, 2, 4, 0, 3):
        axis = PORTIONS[p][3][1]
        take(in2[p], r_recv.at[1, p])
        _, y0, ys, order = PORTIONS[p]
        sums = total(mid[p][pick(p, 1, place[axis])], in2[p]).astype(BF16)
        if TAIL[p] == 3:
            tail[3, y0 : y0 + ys] = sums
        else:
            tail[p] = sums
        if p == 4:
            continue
        q = TAIL[p]
        axis = order[2]
        for k in (2, 1, 3):
            to = lax.rem(place[axis] + k, SIDE)
            copy_to(
                tail.at[q, to], in3.at[q, k - 1], r_send.at[2, q], r_recv.at[2, q], device(axis, to)
            ).start()
    take(crecv.at[pl.ds(0, GROUP - 1)], t_sem.at[1])
    lane = iota((16, 128), 1)
    packed[...] = jnp.full((8, 16, 128), 2147483647, jnp.int32)
    mine = lax.rem(me, 8)
    for g in range(4):
        merged = jnp.zeros((16, 128), jnp.int32)
        for s in range(8):
            key = crecv[g * 8 + s].astype(jnp.int32)
            key = ((key >> 11) << 16) + (key & 2047) + (g * 8 + s) * 2048
            key = pltpu.roll(key, lax.rem((s - mine + 8) * 16, 128), 1)
            merged = jnp.where((lane >> 4) == s, key, merged)
        packed[g] = merged
    best = [packed[:, i, :] for i in range(16)]
    for d in (64, 32, 16):
        best = merge16(best, [pltpu.roll(b, d, 1) for b in best])
    for d in (6, 7):
        best = merge16(best, [pltpu.roll(b, d, 0) for b in best])
    square[...] = jnp.zeros((128, 128), jnp.int32)
    for i in range(16):
        square[i : i + 1, :] = best[i][0:1, :]
    flat = square[...]
    out_v[40:56, 0:128] = jnp.transpose((flat & 65535).astype(F32))[0:16]
    out_v[40:56, 128:256] = jnp.transpose((flat >> 16).astype(F32))[0:16]
    early = pltpu.make_async_copy(out_v.at[pl.ds(8, 48)], out_hbm.at[pl.ds(8, 48)], small_sem.at[0])
    early.start()

    for q in range(4):
        take(in3.at[q], r_recv.at[2, q])
        out = total(tail[q, place[PORTIONS[q][3][2]]], in3.at[q])
        out_v[0:8, q * 128 : (q + 1) * 128] = out[0:8]
        out_v[0:8, 512 + q * 128 : 512 + (q + 1) * 128] = out[8:16]
    late = pltpu.make_async_copy(out_v.at[pl.ds(0, 8)], out_hbm.at[pl.ds(0, 8)], small_sem.at[1])
    late.start()

    take(out_buf.at[pl.ds(0, GROUP - 1)], p_sem.at[0])
    take(bsend.at[pl.ds(0, GROUP - 1)], b_sem.at[0])
    take(crecv.at[pl.ds(0, GROUP - 1)], t_sem.at[0])
    core_copy.wait_send()
    for j in range(SIDE):
        take(r2a.at[j], x_send.at[0, j])
        take(r2b.at[j], x_send.at[1, j])
    for i in range(4):
        take(relay.at[i], x_send.at[i // 2, 5 + i % 2])
    take(r3a, x_send.at[0, 4])
    take(r3b, x_send.at[1, 4])
    take(core_in, h_send)
    for p in range(5):
        take(in1[p], r_send.at[0, p])
        take(in2[p], r_send.at[1, p])
    for q in range(4):
        take(in3.at[q], r_send.at[2, q])
    early.wait()
    late.wait()


def whole(codes, pos, neg, bank_codes, bank_emb, query_emb, positive_emb, head):
    anywhere = pl.BlockSpec(memory_space=pl.ANY)
    dma = pltpu.SemaphoreType.DMA
    block = (16, 128)

    def by_portion(stage, lead):
        return [pltpu.VMEM((*lead, *(n for _, n in extents(p, stage)), *block), BF16) for p in range(5)]

    return pl.pallas_call(
        whole_kernel,
        out_shape=jax.ShapeDtypeStruct((56, 1024), F32),
        in_specs=[anywhere] * 8,
        out_specs=anywhere,
        scratch_shapes=[
            pltpu.VMEM((16, 64), jnp.int32),
            pltpu.VMEM((1, 16), jnp.int32),
            pltpu.VMEM((16, 16), jnp.int32),
            pltpu.VMEM((56, 1024), F32),
            pltpu.VMEM((2048, 1024), BF16),
            pltpu.VMEM((2048, 1024), BF16),
            pltpu.VMEM((1024, 1024), BF16),
            pltpu.VMEM((8, 128), F32),
            pltpu.VMEM((288, 128), F32),
            pltpu.VMEM((32, 16, 128), F32),
            pltpu.VMEM((32, 16, 128), F32),
            pltpu.VMEM((32, 16, 512), BF16),
            pltpu.VMEM((32, 16, 512), BF16),
            pltpu.VMEM((16, 32, 1024), BF16),
            pltpu.VMEM((16, 32, 1024), BF16),
            pltpu.VMEM((16, 32, 1024), BF16),
            pltpu.VMEM((4, 4, 32, 1024), BF16),
            pltpu.VMEM((4, 4, 32, 256), BF16),
            pltpu.VMEM((4, 4, 32, 256), BF16),
            pltpu.VMEM((4, 2, 32, 512), BF16),
            pltpu.VMEM((4, 2, 32, 512), BF16),
            pltpu.VMEM((4, 32, 512), BF16),
            pltpu.VMEM((4, 32, 512), BF16),
            pltpu.VMEM((3, 32, 512), BF16),
            pltpu.VMEM((3, 32, 512), BF16),
            pltpu.VMEM((1024, 512), BF16),
            pltpu.VMEM((2048, 512), F32),
            pltpu.VMEM((8, 512), F32),
            pltpu.VMEM((4, 16, 128), F32),
            pltpu.VMEM((32, 16, 128), F32),
            pltpu.VMEM((8, 16, 128), jnp.int32),
            pltpu.VMEM((128, 128), jnp.int32),
            pltpu.VMEM((320, 1024), BF16),
            pltpu.VMEM((320, 1024), BF16),
            pltpu.VMEM((288, 1024), F32),
            pltpu.VMEM((320, 1024), F32),
            pltpu.VMEM((320, 128), F32),
            pltpu.VMEM((320, 1024), BF16),
            pltpu.VMEM((320, 1024), BF16),
            pltpu.VMEM((32, 1024), BF16),
            pltpu.VMEM((48, 1024), BF16),
            pltpu.VMEM((2, 4, 4, 4, 16, 512), BF16),
            pltpu.VMEM((4, 4, 4, 16, 512), BF16),
            pltpu.VMEM((4, 4, 4, 16, 512), BF16),
            by_portion(1, (3,)),
            by_portion(1, ()),
            by_portion(2, (3,)),
            pltpu.VMEM((4, 4, *block), BF16),
            pltpu.VMEM((4, 3, *block), BF16),
            dma((3,)),
            dma((5,)),
            dma((2,)),
            dma((2,)),
            dma((2,)),
            dma((2,)),
            dma((2, 7)),
            dma((2, 7)),
            dma,
            dma((4,)),
            dma((3, 5)),
            dma((3, 5)),
        ],
        compiler_params=pltpu.CompilerParams(
            collective_id=0, has_side_effects=True, vmem_limit_bytes=60 * MIB
        ),
        name="whole",
    )(codes, pos, neg, bank_codes, bank_emb, query_emb, positive_emb, head)


OUT = (((16, 16), jnp.int32), ((16, 16), jnp.int32), ((16, 1024), BF16), ((16, 1024), BF16), ((8, 1024), F32))


def emit_kernel(packed_ref, *refs):
    targets, held, sem = refs[0:5], refs[5:9], refs[9]
    held[0][...] = packed_ref[40:56, 0:16].astype(jnp.int32)
    held[1][...] = packed_ref[40:56, 128:144].astype(jnp.int32)
    held[2][...] = packed_ref[8:24].astype(BF16)
    held[3][...] = packed_ref[24:40].astype(BF16)
    sources = (*held, packed_ref.at[pl.ds(0, 8)])
    copies = [pltpu.make_async_copy(a, b, sem.at[i]) for i, (a, b) in enumerate(zip(sources, targets))]
    for copy in copies:
        copy.start()
    for copy in copies:
        copy.wait()


def emit(packed):
    return pl.pallas_call(
        emit_kernel,
        out_shape=tuple(jax.ShapeDtypeStruct(*o) for o in OUT),
        in_specs=[pl.BlockSpec(memory_space=pltpu.VMEM)],
        out_specs=(pl.BlockSpec(memory_space=pl.ANY),) * 5,
        scratch_shapes=[*(pltpu.VMEM(*o) for o in OUT[:4]), pltpu.SemaphoreType.DMA((5,))],
        name="emit",
    )(packed)


def local(
    query_codes, positive_ids, negative_ids, bank_codes, bank_emb, query_emb, positive_emb, head
):
    return emit(
        whole(query_codes, positive_ids.reshape(1, -1), negative_ids, bank_codes, bank_emb, query_emb, positive_emb, head)
    )


def solution(mesh):
    both = ("dp", "index")
    rows = P(both, None)
    return jax.shard_map(
        local,
        mesh=mesh,
        in_specs=(rows, P(both), rows, P("index", None), P("index", None), rows, rows, P()),
        out_specs=(rows,) * 5,
        check_vma=False,
    )
```

```python
import functools

import jax
import jax.numpy as jnp
from jax import lax
from jax.experimental import pallas as pl
from jax.experimental.pallas import tpu as pltpu
from jax.sharding import PartitionSpec as P

F32 = jnp.float32
BF16 = jnp.bfloat16
MESH = pl.DeviceIdType.MESH
MIB = 1 << 20
GROUP = 32
SIDE = 4
BIG = float(1 << 23)
LAST = (((1,), (1,)), ((), ()))


def iota(shape, dim):
    return lax.broadcasted_iota(jnp.int32, shape, dim)


def dot(a, b, dims=(((1,), (0,)), ((), ()))):
    return lax.dot_general(a, b, dims, preferred_element_type=F32)


def copy_to(src, dst, send_sem, recv_sem, device):
    return pltpu.make_async_remote_copy(
        src_ref=src,
        dst_ref=dst,
        send_sem=send_sem,
        recv_sem=recv_sem,
        device_id=device,
        device_id_type=MESH,
    )


def coords():
    z = lax.axis_index("dp")
    me = lax.axis_index("index")
    x = lax.div(me, 8)
    y = lax.rem(lax.div(me, 2), 4)
    c = lax.rem(me, 2)
    return z, me, x, y, c


def at(x, y, c):
    return x * 8 + y * 2 + c


OFFSETS = sorted(
    ((dx, dy, dc) for dx in range(4) for dy in range(4) for dc in range(2) if dx or dy or dc),
    key=lambda o: -(min(o[0], 4 - o[0]) + min(o[1], 4 - o[1])),
)


def peers(x, y, c):
    return [at(lax.rem(x + dx, 4), lax.rem(y + dy, 4), lax.rem(c + dc, 2)) for dx, dy, dc in OFFSETS]


def take(ref, sem):
    pltpu.make_async_copy(ref, ref, sem).wait()


def request_table(pos_row, negatives):
    hi = jnp.floor(negatives * (1.0 / 256.0))
    lo = negatives - 256.0 * hi
    halves = jnp.concatenate([hi, lo], axis=0).astype(BF16)
    spread = jnp.where(iota((16, 256), 0) == (iota((16, 256), 1) & 15), 1.0, 0.0).astype(BF16)
    got = dot(halves, spread)
    ids = 256.0 * got[0:16] + got[16:32]
    ids = jnp.where(iota((16, 256), 0) == (iota((16, 256), 1) >> 4), ids, 0.0)
    id_row = jnp.sum(ids, axis=0, keepdims=True)
    owner_row = jnp.floor(id_row * (1.0 / 2048.0))
    owner_b = jnp.broadcast_to(owner_row, (256, 256))
    owner_t = jnp.transpose(owner_b)
    earlier = iota((256, 256), 0) < iota((256, 256), 1)
    same = jnp.where(owner_b == owner_t, 1.0, 0.0)
    rank = jnp.sum(jnp.where(earlier, same, 0.0), axis=0, keepdims=True)
    slot_row = jnp.where(rank < 7.0, owner_row * 8.0 + rank, 249.0 + rank)
    slot_b = jnp.broadcast_to(slot_row, (288, 256))
    hit = iota((288, 256), 0).astype(F32) == slot_b
    id_col = jnp.sum(jnp.where(hit, jnp.broadcast_to(id_row, (288, 256)) + 1.0, 0.0), axis=1, keepdims=True) - 1.0
    which = jnp.where(iota((256, 128), 1) == (iota((256, 128), 0) >> 4), 1.0, 0.0).astype(BF16)
    owned_by = dot(jnp.where(hit, 1.0, 0.0).astype(BF16), which)
    lane32 = iota((32, 128), 1)
    sub32 = iota((32, 128), 0)
    ext_row = jnp.sum(
        jnp.where(lane32 == sub32 + 96, jnp.broadcast_to(id_col[256:288], (32, 128)), 0.0), axis=0, keepdims=True
    )
    return id_col, owned_by, ext_row


def onehot_rows(rel, count):
    return jnp.where(
        jnp.broadcast_to(rel, (count, 2048)) == iota((count, 2048), 1).astype(F32), 1.0, 0.0
    ).astype(BF16)


def batcher(n):
    pairs = []
    p = 1
    while p < n:
        k = p
        while k >= 1:
            for j in range(k % p, n - k, 2 * k):
                for i in range(min(k, n - j - k)):
                    if (i + j) // (2 * p) == (i + j + k) // (2 * p):
                        pairs.append((i + j, i + j + k))
            k //= 2
        p *= 2
    return pairs


SORT16 = batcher(16)


def exchange(v, i, j):
    v[i], v[j] = jnp.minimum(v[i], v[j]), jnp.maximum(v[i], v[j])


def sort16(v):
    v = list(v)
    for i, j in SORT16:
        exchange(v, i, j)
    return v


def merge16(a, b):
    v = [jnp.minimum(a[i], b[15 - i]) for i in range(16)]
    for d in (8, 4, 2, 1):
        for i in range(16):
            if i & d == 0:
                exchange(v, i, i + d)
    return v


def sign_rows(table):
    hi = jnp.floor(table * (1.0 / 256.0))
    lo = table - 256.0 * hi
    both = jnp.concatenate([hi, lo], axis=1).astype(BF16)
    k = iota((1024, 256), 0)
    lane = iota((1024, 256), 1)
    source = (k >> 4) + jnp.where((k & 8) == 0, 128, 0)
    pick = jnp.where(lane == source, 1.0, 0.0).astype(BF16)
    byte = dot(pick, both, LAST).astype(jnp.int32)
    bit = byte & (1 << (iota((1024, 512), 0) & 7))
    return jnp.where(bit != 0, -1024.0, 1024.0).astype(BF16)


PORTIONS = ((0, 0, 4, (0, 1, 2)), (1, 0, 4, (1, 2, 0)), (2, 0, 4, (2, 0, 1)), (3, 0, 2, (0, 1, 2)), (3, 2, 2, (1, 0, 2)))
TAIL = (0, 1, 2, 3, 3)
STEPS = (2, 1, 3, 0)


def extents(p, stage):
    _, _, ys, order = PORTIONS[p]
    return [(a, ys if a == 2 else SIDE) for a in range(3) if a not in order[:stage]]


def split(v):
    high = v.astype(BF16)
    return high, (v - high.astype(F32)).astype(BF16)


def whole_kernel(
    qcodes_hbm, pos_hbm, neg_hbm, codes_hbm, bank_hbm, query_hbm, positive_hbm, head_hbm,
    out_hbm,
    qcodes, pos_in, neg_in, out_v,
    bank, codes, head, pay, owned, out_buf, in_buf, bsend, brecv, esend, eown, ecore, s1, r2a, r2b, s2a, s2b, r3a, r3b,
    signs, keys, pos, shard_best, crecv, packed, square, xs, dz, raw, unit, inv, u_hi, u_lo, u_qq, u_qqq,
    hs, core_in, parts, in1, mid, in2, tail, in3,
    load_sem, small_sem, p_sem, b_sem, t_sem, c_sem, x_send, x_recv, h_send, h_recv, r_send, r_recv,
):
    z, me, x, y, c = coords()
    others = peers(x, y, c)
    partner = (z, at(x, y, 1 - c))
    load_bank = pltpu.make_async_copy(bank_hbm, bank, load_sem.at[0])
    load_codes = pltpu.make_async_copy(codes_hbm, codes, load_sem.at[1])
    load_head = pltpu.make_async_copy(head_hbm, head, load_sem.at[2])
    small = [
        pltpu.make_async_copy(source, target, small_sem.at[i])
        for i, (source, target) in enumerate(
            (
                (neg_hbm, neg_in),
                (pos_hbm, pos_in),
                (qcodes_hbm, qcodes),
                (query_hbm, xs.at[pl.ds(0, 16)]),
                (positive_hbm, xs.at[pl.ds(16, 16)]),
            )
        )
    ]
    for load in small:
        load.start()
    load_bank.start()
    barrier = pltpu.get_barrier_semaphore()
    for peer in others:
        pl.semaphore_signal(barrier, inc=1, device_id=(z, peer), device_id_type=MESH)
    for k in range(1, SIDE):
        pl.semaphore_signal(barrier, inc=1, device_id=(lax.rem(z + k, SIDE), me), device_id_type=MESH)
    load_codes.start()
    load_head.start()

    for load in small[:3]:
        load.wait()
    pay[...] = jnp.zeros((8, 128), F32)
    pay[:, 64:80] = jnp.broadcast_to(pos_in[...].astype(F32), (8, 16))
    out_buf[:, 8:16, :] = jnp.broadcast_to(
        jnp.concatenate([qcodes[0:8], qcodes[8:16]], axis=1).astype(F32)[None], (32, 8, 128)
    )
    id_col, owned_by, ext_row = request_table(pos_in[...].astype(F32), neg_in[...].astype(F32))
    owned[...] = owned_by
    lane8 = iota((8, 128), 1)
    common = jnp.where(lane8 >= 96, jnp.broadcast_to(ext_row, (8, 128)), pay[...])
    base_cols = jnp.broadcast_to(id_col[0:256], (256, 128)).reshape(32, 8, 128)
    out_buf[:, 0:8, :] = jnp.where(
        iota((32, 8, 128), 2) == 0, base_cols, jnp.broadcast_to(common[None], (32, 8, 128))
    )
    pl.semaphore_wait(barrier, len(others) + SIDE - 1)
    for peer in others:
        copy_to(out_buf.at[peer], in_buf.at[me], p_sem.at[0], p_sem.at[1], (z, peer)).start()
    in_buf[me] = out_buf[me]

    for load in small[3:]:
        load.wait()

    def project(start, count):
        rows = slice(start, start + count)
        zed = dot(xs[rows], head[...])
        scale = 1.0 / jnp.sqrt(jnp.sum(zed * zed, axis=1, keepdims=True) + 1e-6)
        u = zed * scale
        unit[rows] = u
        inv[rows] = jnp.broadcast_to(scale, (count, 128))
        high, low = split(u)
        u_hi[rows] = high
        u_lo[rows] = low

    load_head.wait()
    project(0, 32)
    load_bank.wait()
    take(in_buf.at[pl.ds(0, GROUP - 1)], p_sem.at[1])

    first = (me * 2048).astype(F32)
    asked = in_buf[:, 0:8, :].reshape(256, 128)
    base_rel = jnp.sum(jnp.where(iota((256, 128), 1) == 0, asked, 0.0), axis=1, keepdims=True) - first
    hot = onehot_rows(base_rel, 256)
    for h in range(2):
        part = dot(hot, bank[:, h * 512 : (h + 1) * 512])
        bsend[:, 8 * h : 8 * h + 8, :] = part.reshape(32, 8, 512).astype(BF16)
    for peer in others:
        copy_to(bsend.at[peer], brecv.at[me], b_sem.at[0], b_sem.at[1], (z, peer)).start()
    brecv[me] = bsend[me]

    def extras(core):
        rows = in_buf[:, 0:1, :].reshape(16, 2, 1, 128)
        mine = jnp.where(core == 0, rows[:, 0], rows[:, 1])
        wide = jnp.broadcast_to(mine, (16, 32, 128))
        keep = iota((16, 32, 128), 2) == iota((16, 32, 128), 1) + 96
        rel = jnp.sum(jnp.where(keep, wide, 0.0), axis=2, keepdims=True).reshape(512, 1) - first
        return dot(onehot_rows(rel, 512), bank[...])

    esend[...] = extras(1 - c).reshape(16, 32, 1024).astype(BF16)
    core_copy = copy_to(esend, ecore, c_sem.at[0], c_sem.at[1], partner)
    core_copy.start()
    eown[...] = extras(c).reshape(16, 32, 1024).astype(BF16)
    core_copy.wait_recv()
    s1[...] = (eown[...].astype(F32) + ecore[...].astype(F32)).astype(BF16).reshape(4, 4, 32, 1024)

    left, right = pl.ds(0, 512), pl.ds(512, 512)
    for j in (2, 1, 3, 0):
        xj, yj = lax.rem(x + j, SIDE), lax.rem(y + j, SIDE)
        for k in (2, 1, 3):
            xk, yk = lax.rem(x + k, SIDE), lax.rem(y + k, SIDE)
            copy_to(
                s1.at[xk, yj, :, left], r2a.at[j, k - 1], x_send.at[0, j], x_recv.at[0, j], (z, at(xk, y, c))
            ).start()
            copy_to(
                s1.at[xj, yk, :, right], r2b.at[j, k - 1], x_send.at[1, j], x_recv.at[1, j], (z, at(x, yk, c))
            ).start()

    pairs = in_buf[:, 8:16, :]
    signs[...] = sign_rows(
        jnp.concatenate([pairs, pltpu.roll(pairs.reshape(256, 128), 64, 1).reshape(32, 8, 128)], axis=1).reshape(512, 128)
    )
    lane8 = iota((8, 128), 1)
    for t in range(4):
        row = jnp.zeros((8, 128), F32)
        for i in range(8):
            ids = pltpu.roll(in_buf[8 * t + i, 0:8], (16 * i + 64) % 128, 1)
            row = jnp.where((lane8 >> 4) == i, ids, row)
        pos[:, t * 128 : (t + 1) * 128] = row - first
    load_codes.wait()

    def product(m, carry):
        at_row = pl.multiple_of(m * 512, 512)
        keys[pl.ds(at_row, 512), :] = dot(codes[pl.ds(at_row, 512), :], signs[...])
        return carry

    lax.fori_loop(0, 4, product, 0)
    sub = iota((8, 128), 0)

    def select(t):
        lanes = slice(t * 128, (t + 1) * 128)
        wanted = pos[:, lanes]

        def load16(g):
            out = []
            for i in range(16):
                row = pl.multiple_of(g * 128 + i * 8, 8)
                p = (sub + (g * 128 + i * 8)).astype(F32)
                key = keys[pl.ds(row, 8), lanes] + (p + float(1 << 20))
                out.append(jnp.where(p == wanted, BIG, key))
            return out

        def step(g, best):
            return tuple(merge16(best, sort16(load16(g))))

        best = lax.fori_loop(1, 16, step, tuple(sort16(load16(0))))
        for d in (4, 2, 1):
            best = merge16(best, [pltpu.roll(b, d, 0) for b in best])
        low, high = best[0], best[8]
        for i in range(1, 8):
            low = jnp.where(sub == i, best[i], low)
            high = jnp.where(sub == i, best[8 + i], high)
        high = pltpu.roll(high, 64, 1)
        left_half = iota((8, 128), 1) < 64
        shard_best[t, 0] = jnp.where(left_half, low, high)
        shard_best[t, 1] = jnp.where(left_half, high, low)

    def total(own, got):
        t = own.astype(F32)
        for k in range(SIDE - 1):
            t = t + got[k].astype(F32)
        return t

    def pass_on(j):
        xj, yj = lax.rem(x + j, SIDE), lax.rem(y + j, SIDE)
        take(r2a.at[j], x_recv.at[0, j])
        s2a[j] = total(s1[x, yj, :, 0:512], r2a.at[j]).astype(BF16)
        copy_to(s2a.at[j], r3a.at[j - 1], x_send.at[0, 4], x_recv.at[0, 4], (z, at(x, yj, c))).start()
        take(r2b.at[j], x_recv.at[1, j])
        s2b[j] = total(s1[xj, y, :, 512:1024], r2b.at[j]).astype(BF16)
        copy_to(s2b.at[j], r3b.at[j - 1], x_send.at[1, 4], x_recv.at[1, 4], (z, at(xj, y, c))).start()

    firsts = (((0,), (0,)), ((), ()))
    own_pos = jnp.where(iota((16, 16), 0) == iota((16, 16), 1), 1.0, 0.0)
    q_unit, q_hi, q_lo = unit[0:16], u_hi[0:16], u_lo[0:16]

    u_qq[0:16], u_qq[16:32] = q_hi, q_lo
    u_qqq[0:16], u_qqq[16:32], u_qqq[32:48] = q_hi, q_hi, q_lo

    def column(row):
        return jnp.sum(own_pos * jnp.broadcast_to(row, (16, 16)), axis=1, keepdims=True)

    def scores(start, count, mask):
        rows = slice(start, start + count)
        high, low = u_hi[rows], u_lo[rows]
        twice = dot(high, u_qq[...], LAST)
        logits = 50.0 * (twice[:, 0:16] + (dot(low, q_hi, LAST) + twice[:, 16:32]))
        logits = jnp.where(mask > 0.5, logits, 0.0)
        return logits, jnp.where(mask > 0.5, jnp.exp(logits), 0.0)

    def negatives(start, count):
        rows = slice(start, start + count)
        logits, w = scores(start, count, owned[start - 32 : start - 32 + count, 0:16])
        w_hi, w_lo = split(w)
        high, low = u_hi[rows], u_lo[rows]
        along = dot(w_hi, high, firsts) + (dot(w_lo, high, firsts) + dot(w_hi, low, firsts))
        scale = inv[rows, 0:1]
        k_hi, k_lo = split(w * (50.0 * scale))
        pull = dot(jnp.concatenate([k_hi, k_lo, k_hi], axis=1), u_qqq[...])
        k2 = jnp.sum(w * logits, axis=1, keepdims=True) * scale
        raw[start - 32 : start - 32 + count] = pull - unit[rows] * k2
        return jnp.sum(w, axis=0, keepdims=True), along

    take(brecv.at[pl.ds(0, GROUP - 1)], b_sem.at[1])
    got = brecv[...].astype(F32)
    xs[32:288, 0:512] = got[:, 0:8].reshape(256, 512).astype(BF16)
    xs[32:288, 512:1024] = got[:, 8:16].reshape(256, 512).astype(BF16)
    project(32, 256)
    pass_on(2)
    pos_logits, pos_w = scores(16, 16, own_pos)
    base_sum, base_along = negatives(32, 256)
    pass_on(1)
    pass_on(3)

    take(r2a.at[0], x_recv.at[0, 0])
    own_left = total(s1[x, y, :, 0:512], r2a.at[0])
    take(r2b.at[0], x_recv.at[1, 0])
    own_right = total(s1[x, y, :, 512:1024], r2b.at[0])
    take(r3a, x_recv.at[0, 4])
    xs[288:320, 0:512] = total(own_left, r3a).astype(BF16)
    take(r3b, x_recv.at[1, 4])
    xs[288:320, 512:1024] = total(own_right, r3b).astype(BF16)
    project(288, 32)
    ext_sum, ext_along = negatives(288, 32)

    share = 1.0 / (base_sum + ext_sum + jnp.sum(pos_w, axis=0, keepdims=True))
    slot_share = jnp.sum(owned[:, 0:16] * share, axis=1, keepdims=True)
    dz[32:320] = (raw[...] * slot_share).astype(BF16)
    pos_slope = column(jnp.sum(pos_w, axis=0, keepdims=True) * share - 1.0)
    pos_unit = unit[16:32]
    du = 50.0 * (column(share) * (base_along + ext_along) + pos_slope * pos_unit)
    dz[0:16] = ((du - q_unit * jnp.sum(q_unit * du, axis=1, keepdims=True)) * inv[0:16, 0:1]).astype(BF16)
    pos_logit = jnp.sum(pos_logits, axis=1, keepdims=True)
    dz[16:32] = (pos_slope * (50.0 * q_unit - pos_unit * pos_logit) * inv[16:32, 0:1]).astype(BF16)

    def h_copy(i):
        zz = lax.rem(z + STEPS[i], SIDE)
        return copy_to(hs.at[1 - c, zz], core_in.at[zz], h_send, h_recv.at[i], partner)

    def grow(i):
        zz = lax.rem(z + STEPS[i], SIDE)
        part = dot(xs[:, pl.ds(pl.multiple_of(zz * 256, 256), 256)], dz[...], firsts).reshape(32, 8, 1024)
        part = jnp.concatenate([part[:, :, 0:512], part[:, :, 512:1024]], axis=1).astype(BF16)
        part = part.reshape(4, 4, 2, 16, 512)
        for core in range(2):
            hs[core, zz] = part[:, :, core]
        h_copy(i).start()

    place = (z, x, y)

    def device(axis, to):
        where = [z, x, y]
        where[axis] = to
        return (where[0], at(where[1], where[2], c))

    def first_from(p, to):
        tile, y0, ys, order = PORTIONS[p]
        index = [slice(None), slice(None), pl.ds(y0, ys)]
        if order[0] == 2:
            index[2] = to
        else:
            index[order[0]] = to
        return (*index, slice(None), pl.ds(tile * 128, 128))

    def gather_core(i):
        zz = lax.rem(z + STEPS[i], SIDE)
        h_copy(i).wait_recv()
        parts[zz] = (hs[c, zz].astype(F32) + core_in[zz].astype(F32)).astype(BF16)
        for p in (3, 4, 0, 1, 2):
            tile, y0, ys, order = PORTIONS[p]
            lanes = pl.ds(tile * 128, 128)
            if order[0] == 0:
                moves = [(zz, parts.at[zz, :, pl.ds(y0, ys), :, lanes], in1[p].at[STEPS[i] - 1])] if STEPS[i] else []
            else:
                moves = []
                for k in (2, 1, 3):
                    to = lax.rem(place[order[0]] + k, SIDE)
                    if order[0] == 1:
                        source = parts.at[zz, to, pl.ds(y0, ys), :, lanes]
                    else:
                        source = parts.at[zz, :, to, :, lanes]
                    moves.append((to, source, in1[p].at[k - 1, zz]))
            for to, source, target in moves:
                copy_to(source, target, r_send.at[0, p], r_recv.at[0, p], device(order[0], to)).start()

    grow(0)
    grow(1)
    gather_core(0)
    grow(2)
    gather_core(1)
    grow(3)
    gather_core(2)
    select(0)
    gather_core(3)
    select(1)
    select(2)
    select(3)

    out_v[8:40] = dot(dz[0:32], head[...], LAST)

    def pick(p, stage, to):
        axis = PORTIONS[p][3][stage]
        return tuple(to if a == axis else slice(None) for a, _ in extents(p, stage))

    for p in (1, 2, 4, 0, 3):
        axis = PORTIONS[p][3][0]
        take(in1[p], r_recv.at[0, p])
        mid[p][...] = total(parts[first_from(p, place[axis])], in1[p]).astype(BF16)
        axis = PORTIONS[p][3][1]
        for k in (2, 1, 3):
            to = lax.rem(place[axis] + k, SIDE)
            copy_to(
                mid[p].at[pick(p, 1, to)], in2[p].at[k - 1], r_send.at[1, p], r_recv.at[1, p], device(axis, to)
            ).start()
    def half_of(device):
        return lax.div(device, 8), lax.div(lax.rem(device, 8), 4)

    for peer in others:
        copy_to(shard_best.at[half_of(peer)], crecv.at[me], t_sem.at[0], t_sem.at[1], (z, peer)).start()
    crecv[me] = shard_best[half_of(me)]

    for p in (1, 2, 4, 0, 3):
        axis = PORTIONS[p][3][1]
        take(in2[p], r_recv.at[1, p])
        _, y0, ys, order = PORTIONS[p]
        sums = total(mid[p][pick(p, 1, place[axis])], in2[p]).astype(BF16)
        if TAIL[p] == 3:
            tail[3, y0 : y0 + ys] = sums
        else:
            tail[p] = sums
        if p == 4:
            continue
        q = TAIL[p]
        axis = order[2]
        for k in (2, 1, 3):
            to = lax.rem(place[axis] + k, SIDE)
            copy_to(
                tail.at[q, to], in3.at[q, k - 1], r_send.at[2, q], r_recv.at[2, q], device(axis, to)
            ).start()
    take(crecv.at[pl.ds(0, GROUP - 1)], t_sem.at[1])
    lane = iota((16, 128), 1)
    packed[...] = jnp.full((8, 16, 128), 2147483647, jnp.int32)
    mine = lax.rem(me, 8)
    for g in range(4):
        merged = jnp.zeros((16, 128), jnp.int32)
        for s in range(8):
            got = crecv[g * 8 + s]
            key = jnp.concatenate([got, pltpu.roll(got, 64, 1)], axis=0).astype(jnp.int32)
            key = ((key >> 11) << 16) + (key & 2047) + (g * 8 + s) * 2048
            key = pltpu.roll(key, lax.rem((s - mine + 8) * 16, 128), 1)
            merged = jnp.where((lane >> 4) == s, key, merged)
        packed[g] = merged
    best = [packed[:, i, :] for i in range(16)]
    for d in (64, 32, 16):
        best = merge16(best, [pltpu.roll(b, d, 1) for b in best])
    for d in (6, 7):
        best = merge16(best, [pltpu.roll(b, d, 0) for b in best])
    square[...] = jnp.zeros((128, 128), jnp.int32)
    for i in range(16):
        square[i : i + 1, :] = best[i][0:1, :]
    flat = square[...]
    out_v[40:56, 0:128] = jnp.transpose((flat & 65535).astype(F32))[0:16]
    out_v[40:56, 128:256] = jnp.transpose((flat >> 16).astype(F32))[0:16]
    early = pltpu.make_async_copy(out_v.at[pl.ds(8, 48)], out_hbm.at[pl.ds(8, 48)], small_sem.at[0])
    early.start()

    for q in range(4):
        take(in3.at[q], r_recv.at[2, q])
        out = total(tail[q, place[PORTIONS[q][3][2]]], in3.at[q])
        out_v[0:8, q * 128 : (q + 1) * 128] = out[0:8]
        out_v[0:8, 512 + q * 128 : 512 + (q + 1) * 128] = out[8:16]
    late = pltpu.make_async_copy(out_v.at[pl.ds(0, 8)], out_hbm.at[pl.ds(0, 8)], small_sem.at[1])
    late.start()

    take(out_buf.at[pl.ds(0, GROUP - 1)], p_sem.at[0])
    take(bsend.at[pl.ds(0, GROUP - 1)], b_sem.at[0])
    take(crecv.at[pl.ds(0, GROUP - 1)], t_sem.at[0])
    core_copy.wait_send()
    for j in range(SIDE):
        take(r2a.at[j], x_send.at[0, j])
        take(r2b.at[j], x_send.at[1, j])
    take(r3a, x_send.at[0, 4])
    take(r3b, x_send.at[1, 4])
    take(core_in, h_send)
    for p in range(5):
        take(in1[p], r_send.at[0, p])
        take(in2[p], r_send.at[1, p])
    for q in range(4):
        take(in3.at[q], r_send.at[2, q])
    early.wait()
    late.wait()


def whole(codes, pos, neg, bank_codes, bank_emb, query_emb, positive_emb, head):
    anywhere = pl.BlockSpec(memory_space=pl.ANY)
    dma = pltpu.SemaphoreType.DMA
    block = (16, 128)

    def by_portion(stage, lead):
        return [pltpu.VMEM((*lead, *(n for _, n in extents(p, stage)), *block), BF16) for p in range(5)]

    return pl.pallas_call(
        whole_kernel,
        out_shape=jax.ShapeDtypeStruct((56, 1024), F32),
        in_specs=[anywhere] * 8,
        out_specs=anywhere,
        scratch_shapes=[
            pltpu.VMEM((16, 64), jnp.int32),
            pltpu.VMEM((1, 16), jnp.int32),
            pltpu.VMEM((16, 16), jnp.int32),
            pltpu.VMEM((56, 1024), F32),
            pltpu.VMEM((2048, 1024), BF16),
            pltpu.VMEM((2048, 1024), BF16),
            pltpu.VMEM((1024, 1024), BF16),
            pltpu.VMEM((8, 128), F32),
            pltpu.VMEM((288, 128), F32),
            pltpu.VMEM((32, 16, 128), F32),
            pltpu.VMEM((32, 16, 128), F32),
            pltpu.VMEM((32, 16, 512), BF16),
            pltpu.VMEM((32, 16, 512), BF16),
            pltpu.VMEM((16, 32, 1024), BF16),
            pltpu.VMEM((16, 32, 1024), BF16),
            pltpu.VMEM((16, 32, 1024), BF16),
            pltpu.VMEM((4, 4, 32, 1024), BF16),
            pltpu.VMEM((4, 3, 32, 512), BF16),
            pltpu.VMEM((4, 3, 32, 512), BF16),
            pltpu.VMEM((4, 32, 512), BF16),
            pltpu.VMEM((4, 32, 512), BF16),
            pltpu.VMEM((3, 32, 512), BF16),
            pltpu.VMEM((3, 32, 512), BF16),
            pltpu.VMEM((1024, 512), BF16),
            pltpu.VMEM((2048, 512), F32),
            pltpu.VMEM((8, 512), F32),
            pltpu.VMEM((4, 2, 8, 128), F32),
            pltpu.VMEM((32, 8, 128), F32),
            pltpu.VMEM((8, 16, 128), jnp.int32),
            pltpu.VMEM((128, 128), jnp.int32),
            pltpu.VMEM((320, 1024), BF16),
            pltpu.VMEM((320, 1024), BF16),
            pltpu.VMEM((288, 1024), F32),
            pltpu.VMEM((320, 1024), F32),
            pltpu.VMEM((320, 128), F32),
            pltpu.VMEM((320, 1024), BF16),
            pltpu.VMEM((320, 1024), BF16),
            pltpu.VMEM((32, 1024), BF16),
            pltpu.VMEM((48, 1024), BF16),
            pltpu.VMEM((2, 4, 4, 4, 16, 512), BF16),
            pltpu.VMEM((4, 4, 4, 16, 512), BF16),
            pltpu.VMEM((4, 4, 4, 16, 512), BF16),
            by_portion(1, (3,)),
            by_portion(1, ()),
            by_portion(2, (3,)),
            pltpu.VMEM((4, 4, *block), BF16),
            pltpu.VMEM((4, 3, *block), BF16),
            dma((3,)),
            dma((5,)),
            dma((2,)),
            dma((2,)),
            dma((2,)),
            dma((2,)),
            dma((2, 5)),
            dma((2, 5)),
            dma,
            dma((4,)),
            dma((3, 5)),
            dma((3, 5)),
        ],
        compiler_params=pltpu.CompilerParams(
            collective_id=0, has_side_effects=True, vmem_limit_bytes=60 * MIB
        ),
        name="whole",
    )(codes, pos, neg, bank_codes, bank_emb, query_emb, positive_emb, head)


OUT = (((16, 16), jnp.int32), ((16, 16), jnp.int32), ((16, 1024), BF16), ((16, 1024), BF16), ((8, 1024), F32))


def emit_kernel(packed_ref, *refs):
    targets, held, sem = refs[0:5], refs[5:9], refs[9]
    held[0][...] = packed_ref[40:56, 0:16].astype(jnp.int32)
    held[1][...] = packed_ref[40:56, 128:144].astype(jnp.int32)
    held[2][...] = packed_ref[8:24].astype(BF16)
    held[3][...] = packed_ref[24:40].astype(BF16)
    sources = (*held, packed_ref.at[pl.ds(0, 8)])
    copies = [pltpu.make_async_copy(a, b, sem.at[i]) for i, (a, b) in enumerate(zip(sources, targets))]
    for copy in copies:
        copy.start()
    for copy in copies:
        copy.wait()


def emit(packed):
    return pl.pallas_call(
        emit_kernel,
        out_shape=tuple(jax.ShapeDtypeStruct(*o) for o in OUT),
        in_specs=[pl.BlockSpec(memory_space=pltpu.VMEM)],
        out_specs=(pl.BlockSpec(memory_space=pl.ANY),) * 5,
        scratch_shapes=[*(pltpu.VMEM(*o) for o in OUT[:4]), pltpu.SemaphoreType.DMA((5,))],
        name="emit",
    )(packed)


def local(
    query_codes, positive_ids, negative_ids, bank_codes, bank_emb, query_emb, positive_emb, head
):
    return emit(
        whole(query_codes, positive_ids.reshape(1, -1), negative_ids, bank_codes, bank_emb, query_emb, positive_emb, head)
    )


def solution(mesh):
    both = ("dp", "index")
    rows = P(both, None)
    return jax.shard_map(
        local,
        mesh=mesh,
        in_specs=(rows, P(both), rows, P("index", None), P("index", None), rows, rows, P()),
        out_specs=(rows,) * 5,
        check_vma=False,
    )
```

```python
import functools

import jax
import jax.numpy as jnp
from jax import lax
from jax.experimental import pallas as pl
from jax.experimental.pallas import tpu as pltpu
from jax.sharding import PartitionSpec as P

F32 = jnp.float32
BF16 = jnp.bfloat16
MESH = pl.DeviceIdType.MESH
MIB = 1 << 20
GROUP = 32
SIDE = 4
BIG = float(1 << 23)
LAST = (((1,), (1,)), ((), ()))


def iota(shape, dim):
    return lax.broadcasted_iota(jnp.int32, shape, dim)


def dot(a, b, dims=(((1,), (0,)), ((), ()))):
    return lax.dot_general(a, b, dims, preferred_element_type=F32)


def copy_to(src, dst, send_sem, recv_sem, device):
    return pltpu.make_async_remote_copy(
        src_ref=src,
        dst_ref=dst,
        send_sem=send_sem,
        recv_sem=recv_sem,
        device_id=device,
        device_id_type=MESH,
    )


def coords():
    z = lax.axis_index("dp")
    me = lax.axis_index("index")
    x = lax.div(me, 8)
    y = lax.rem(lax.div(me, 2), 4)
    c = lax.rem(me, 2)
    return z, me, x, y, c


def at(x, y, c):
    return x * 8 + y * 2 + c


OFFSETS = sorted(
    ((dx, dy, dc) for dx in range(4) for dy in range(4) for dc in range(2) if dx or dy or dc),
    key=lambda o: -(min(o[0], 4 - o[0]) + min(o[1], 4 - o[1])),
)


def peers(x, y, c):
    return [at(lax.rem(x + dx, 4), lax.rem(y + dy, 4), lax.rem(c + dc, 2)) for dx, dy, dc in OFFSETS]


def take(ref, sem):
    pltpu.make_async_copy(ref, ref, sem).wait()


def request_table(pos_row, negatives):
    hi = jnp.floor(negatives * (1.0 / 256.0))
    lo = negatives - 256.0 * hi
    halves = jnp.concatenate([hi, lo], axis=0).astype(BF16)
    spread = jnp.where(iota((16, 256), 0) == (iota((16, 256), 1) & 15), 1.0, 0.0).astype(BF16)
    got = dot(halves, spread)
    ids = 256.0 * got[0:16] + got[16:32]
    ids = jnp.where(iota((16, 256), 0) == (iota((16, 256), 1) >> 4), ids, 0.0)
    id_row = jnp.sum(ids, axis=0, keepdims=True)
    owner_row = jnp.floor(id_row * (1.0 / 2048.0))
    owner_b = jnp.broadcast_to(owner_row, (256, 256))
    owner_t = jnp.transpose(owner_b)
    earlier = iota((256, 256), 0) < iota((256, 256), 1)
    same = jnp.where(owner_b == owner_t, 1.0, 0.0)
    rank = jnp.sum(jnp.where(earlier, same, 0.0), axis=0, keepdims=True)
    slot_row = jnp.where(rank < 7.0, owner_row * 8.0 + rank, 249.0 + rank)
    slot_b = jnp.broadcast_to(slot_row, (288, 256))
    hit = iota((288, 256), 0).astype(F32) == slot_b
    id_col = jnp.sum(jnp.where(hit, jnp.broadcast_to(id_row, (288, 256)) + 1.0, 0.0), axis=1, keepdims=True) - 1.0
    which = jnp.where(iota((256, 128), 1) == (iota((256, 128), 0) >> 4), 1.0, 0.0).astype(BF16)
    owned_by = dot(jnp.where(hit, 1.0, 0.0).astype(BF16), which)
    lane32 = iota((32, 128), 1)
    sub32 = iota((32, 128), 0)
    ext_row = jnp.sum(
        jnp.where(lane32 == sub32 + 96, jnp.broadcast_to(id_col[256:288], (32, 128)), 0.0), axis=0, keepdims=True
    )
    return id_col, owned_by, ext_row


def onehot_rows(rel, count):
    return jnp.where(
        jnp.broadcast_to(rel, (count, 2048)) == iota((count, 2048), 1).astype(F32), 1.0, 0.0
    ).astype(BF16)


def batcher(n):
    pairs = []
    p = 1
    while p < n:
        k = p
        while k >= 1:
            for j in range(k % p, n - k, 2 * k):
                for i in range(min(k, n - j - k)):
                    if (i + j) // (2 * p) == (i + j + k) // (2 * p):
                        pairs.append((i + j, i + j + k))
            k //= 2
        p *= 2
    return pairs


SORT16 = batcher(16)


def exchange(v, i, j):
    v[i], v[j] = jnp.minimum(v[i], v[j]), jnp.maximum(v[i], v[j])


def sort16(v):
    v = list(v)
    for i, j in SORT16:
        exchange(v, i, j)
    return v


def merge16(a, b):
    v = [jnp.minimum(a[i], b[15 - i]) for i in range(16)]
    for d in (8, 4, 2, 1):
        for i in range(16):
            if i & d == 0:
                exchange(v, i, i + d)
    return v


def sign_rows(table):
    hi = jnp.floor(table * (1.0 / 256.0))
    lo = table - 256.0 * hi
    both = jnp.concatenate([hi, lo], axis=1).astype(BF16)
    k = iota((1024, 256), 0)
    lane = iota((1024, 256), 1)
    source = (k >> 4) + jnp.where((k & 8) == 0, 128, 0)
    pick = jnp.where(lane == source, 1.0, 0.0).astype(BF16)
    byte = dot(pick, both, LAST).astype(jnp.int32)
    bit = byte & (1 << (iota((1024, 512), 0) & 7))
    return jnp.where(bit != 0, -1024.0, 1024.0).astype(BF16)


PORTIONS = ((0, 0, 4, (0, 1, 2)), (1, 0, 4, (1, 2, 0)), (2, 0, 4, (2, 0, 1)), (3, 0, 2, (0, 1, 2)), (3, 2, 2, (1, 0, 2)))
TAIL = (0, 1, 2, 3, 3)
STEPS = (2, 1, 3, 0)


def extents(p, stage):
    _, _, ys, order = PORTIONS[p]
    return [(a, ys if a == 2 else SIDE) for a in range(3) if a not in order[:stage]]


def split(v):
    high = v.astype(BF16)
    return high, (v - high.astype(F32)).astype(BF16)


def whole_kernel(
    qcodes_hbm, pos_hbm, neg_hbm, codes_hbm, bank_hbm, query_hbm, positive_hbm, head_hbm,
    out_hbm,
    qcodes, pos_in, neg_in, out_v,
    bank, codes, head, pay, owned, out_buf, in_buf, bsend, brecv, esend, eown, ecore, s1, r2a, r2b, s2a, s2b, r3a, r3b,
    signs, keys, pos, shard_best, crecv, packed, square, xs, dz, raw, unit, inv, u_hi, u_lo, u_qq, u_qqq,
    hs, core_in, parts, in1, mid, in2, tail, in3,
    load_sem, small_sem, p_sem, b_sem, t_sem, c_sem, x_send, x_recv, h_send, h_recv, r_send, r_recv,
):
    z, me, x, y, c = coords()
    others = peers(x, y, c)
    partner = (z, at(x, y, 1 - c))
    load_bank = pltpu.make_async_copy(bank_hbm, bank, load_sem.at[0])
    load_codes = pltpu.make_async_copy(codes_hbm, codes, load_sem.at[1])
    load_head = pltpu.make_async_copy(head_hbm, head, load_sem.at[2])
    small = [
        pltpu.make_async_copy(source, target, small_sem.at[i])
        for i, (source, target) in enumerate(
            (
                (neg_hbm, neg_in),
                (pos_hbm, pos_in),
                (qcodes_hbm, qcodes),
                (query_hbm, xs.at[pl.ds(0, 16)]),
                (positive_hbm, xs.at[pl.ds(16, 16)]),
            )
        )
    ]
    for load in small:
        load.start()
    load_bank.start()
    barrier = pltpu.get_barrier_semaphore()
    for peer in others:
        pl.semaphore_signal(barrier, inc=1, device_id=(z, peer), device_id_type=MESH)
    for k in range(1, SIDE):
        pl.semaphore_signal(barrier, inc=1, device_id=(lax.rem(z + k, SIDE), me), device_id_type=MESH)
    load_codes.start()
    load_head.start()

    for load in small[:3]:
        load.wait()
    pay[...] = jnp.zeros((8, 128), F32)
    pay[:, 64:80] = jnp.broadcast_to(pos_in[...].astype(F32), (8, 16))
    out_buf[:, 8:16, :] = jnp.broadcast_to(
        jnp.concatenate([qcodes[0:8], qcodes[8:16]], axis=1).astype(F32)[None], (32, 8, 128)
    )
    id_col, owned_by, ext_row = request_table(pos_in[...].astype(F32), neg_in[...].astype(F32))
    owned[...] = owned_by
    lane8 = iota((8, 128), 1)
    common = jnp.where(lane8 >= 96, jnp.broadcast_to(ext_row, (8, 128)), pay[...])
    base_cols = jnp.broadcast_to(id_col[0:256], (256, 128)).reshape(32, 8, 128)
    out_buf[:, 0:8, :] = jnp.where(
        iota((32, 8, 128), 2) == 0, base_cols, jnp.broadcast_to(common[None], (32, 8, 128))
    )
    pl.semaphore_wait(barrier, len(others) + SIDE - 1)
    for peer in others:
        copy_to(out_buf.at[peer], in_buf.at[me], p_sem.at[0], p_sem.at[1], (z, peer)).start()
    in_buf[me] = out_buf[me]

    for load in small[3:]:
        load.wait()

    def project(start, count):
        rows = slice(start, start + count)
        zed = dot(xs[rows], head[...])
        scale = 1.0 / jnp.sqrt(jnp.sum(zed * zed, axis=1, keepdims=True) + 1e-6)
        u = zed * scale
        unit[rows] = u
        inv[rows] = jnp.broadcast_to(scale, (count, 128))
        high, low = split(u)
        u_hi[rows] = high
        u_lo[rows] = low

    load_head.wait()
    project(0, 32)
    load_bank.wait()
    take(in_buf.at[pl.ds(0, GROUP - 1)], p_sem.at[1])

    first = (me * 2048).astype(F32)
    asked = in_buf[:, 0:8, :].reshape(256, 128)
    base_rel = jnp.sum(jnp.where(iota((256, 128), 1) == 0, asked, 0.0), axis=1, keepdims=True) - first
    hot = onehot_rows(base_rel, 256)
    for h in range(2):
        part = dot(hot, bank[:, h * 512 : (h + 1) * 512])
        bsend[:, 8 * h : 8 * h + 8, :] = part.reshape(32, 8, 512).astype(BF16)
    for peer in others:
        copy_to(bsend.at[peer], brecv.at[me], b_sem.at[0], b_sem.at[1], (z, peer)).start()
    brecv[me] = bsend[me]

    def extras(core):
        rows = in_buf[:, 0:1, :].reshape(16, 2, 1, 128)
        mine = jnp.where(core == 0, rows[:, 0], rows[:, 1])
        wide = jnp.broadcast_to(mine, (16, 32, 128))
        keep = iota((16, 32, 128), 2) == iota((16, 32, 128), 1) + 96
        rel = jnp.sum(jnp.where(keep, wide, 0.0), axis=2, keepdims=True).reshape(512, 1) - first
        return dot(onehot_rows(rel, 512), bank[...])

    esend[...] = extras(1 - c).reshape(16, 32, 1024).astype(BF16)
    core_copy = copy_to(esend, ecore, c_sem.at[0], c_sem.at[1], partner)
    core_copy.start()
    eown[...] = extras(c).reshape(16, 32, 1024).astype(BF16)
    core_copy.wait_recv()
    s1[...] = (eown[...].astype(F32) + ecore[...].astype(F32)).astype(BF16).reshape(4, 4, 32, 1024)

    left, right = pl.ds(0, 512), pl.ds(512, 512)
    for j in (2, 1, 3, 0):
        xj, yj = lax.rem(x + j, SIDE), lax.rem(y + j, SIDE)
        for k in (2, 1, 3):
            xk, yk = lax.rem(x + k, SIDE), lax.rem(y + k, SIDE)
            copy_to(
                s1.at[xk, yj, :, left], r2a.at[j, k - 1], x_send.at[0, j], x_recv.at[0, j], (z, at(xk, y, c))
            ).start()
            copy_to(
                s1.at[xj, yk, :, right], r2b.at[j, k - 1], x_send.at[1, j], x_recv.at[1, j], (z, at(x, yk, c))
            ).start()

    pairs = in_buf[:, 8:16, :]
    signs[...] = sign_rows(
        jnp.concatenate([pairs, pltpu.roll(pairs.reshape(256, 128), 64, 1).reshape(32, 8, 128)], axis=1).reshape(512, 128)
    )
    lane8 = iota((8, 128), 1)
    for t in range(4):
        row = jnp.zeros((8, 128), F32)
        for i in range(8):
            ids = pltpu.roll(in_buf[8 * t + i, 0:8], (16 * i + 64) % 128, 1)
            row = jnp.where((lane8 >> 4) == i, ids, row)
        pos[:, t * 128 : (t + 1) * 128] = row - first
    load_codes.wait()

    def product(m, carry):
        at_row = pl.multiple_of(m * 512, 512)
        keys[pl.ds(at_row, 512), :] = dot(codes[pl.ds(at_row, 512), :], signs[...])
        return carry

    lax.fori_loop(0, 4, product, 0)
    sub = iota((8, 128), 0)

    def select(t):
        lanes = slice(t * 128, (t + 1) * 128)
        wanted = pos[:, lanes]

        def load16(g):
            out = []
            for i in range(16):
                row = pl.multiple_of(g * 128 + i * 8, 8)
                p = (sub + (g * 128 + i * 8)).astype(F32)
                key = keys[pl.ds(row, 8), lanes] + (p + float(1 << 20))
                out.append(jnp.where(p == wanted, BIG, key))
            return out

        def step(g, best):
            return tuple(merge16(best, sort16(load16(g))))

        best = lax.fori_loop(1, 16, step, tuple(sort16(load16(0))))
        for d in (4, 2, 1):
            best = merge16(best, [pltpu.roll(b, d, 0) for b in best])
        low, high = best[0], best[8]
        for i in range(1, 8):
            low = jnp.where(sub == i, best[i], low)
            high = jnp.where(sub == i, best[8 + i], high)
        high = pltpu.roll(high, 64, 1)
        left_half = iota((8, 128), 1) < 64
        shard_best[t, 0] = jnp.where(left_half, low, high)
        shard_best[t, 1] = jnp.where(left_half, high, low)

    def total(own, got):
        t = own.astype(F32)
        for k in range(SIDE - 1):
            t = t + got[k].astype(F32)
        return t

    def pass_on(j):
        xj, yj = lax.rem(x + j, SIDE), lax.rem(y + j, SIDE)
        take(r2a.at[j], x_recv.at[0, j])
        s2a[j] = total(s1[x, yj, :, 0:512], r2a.at[j]).astype(BF16)
        copy_to(s2a.at[j], r3a.at[j - 1], x_send.at[0, 4], x_recv.at[0, 4], (z, at(x, yj, c))).start()
        take(r2b.at[j], x_recv.at[1, j])
        s2b[j] = total(s1[xj, y, :, 512:1024], r2b.at[j]).astype(BF16)
        copy_to(s2b.at[j], r3b.at[j - 1], x_send.at[1, 4], x_recv.at[1, 4], (z, at(xj, y, c))).start()

    firsts = (((0,), (0,)), ((), ()))
    own_pos = jnp.where(iota((16, 16), 0) == iota((16, 16), 1), 1.0, 0.0)
    q_unit, q_hi, q_lo = unit[0:16], u_hi[0:16], u_lo[0:16]

    u_qq[0:16], u_qq[16:32] = q_hi, q_lo
    u_qqq[0:16], u_qqq[16:32], u_qqq[32:48] = q_hi, q_hi, q_lo

    def column(row):
        return jnp.sum(own_pos * jnp.broadcast_to(row, (16, 16)), axis=1, keepdims=True)

    def scores(start, count, mask):
        rows = slice(start, start + count)
        high, low = u_hi[rows], u_lo[rows]
        twice = dot(high, u_qq[...], LAST)
        logits = 50.0 * (twice[:, 0:16] + (dot(low, q_hi, LAST) + twice[:, 16:32]))
        logits = jnp.where(mask > 0.5, logits, 0.0)
        return logits, jnp.where(mask > 0.5, jnp.exp(logits), 0.0)

    def negatives(start, count):
        rows = slice(start, start + count)
        logits, w = scores(start, count, owned[start - 32 : start - 32 + count, 0:16])
        w_hi, w_lo = split(w)
        high, low = u_hi[rows], u_lo[rows]
        along = dot(w_hi, high, firsts) + (dot(w_lo, high, firsts) + dot(w_hi, low, firsts))
        scale = inv[rows, 0:1]
        k_hi, k_lo = split(w * (50.0 * scale))
        pull = dot(jnp.concatenate([k_hi, k_lo, k_hi], axis=1), u_qqq[...])
        k2 = jnp.sum(w * logits, axis=1, keepdims=True) * scale
        raw[start - 32 : start - 32 + count] = pull - unit[rows] * k2
        return jnp.sum(w, axis=0, keepdims=True), along

    select(0)
    select(1)
    take(brecv.at[pl.ds(0, GROUP - 1)], b_sem.at[1])
    got = brecv[...].astype(F32)
    xs[32:288, 0:512] = got[:, 0:8].reshape(256, 512).astype(BF16)
    xs[32:288, 512:1024] = got[:, 8:16].reshape(256, 512).astype(BF16)
    project(32, 256)
    pass_on(2)
    select(2)
    pos_logits, pos_w = scores(16, 16, own_pos)
    base_sum, base_along = negatives(32, 256)
    pass_on(1)
    select(3)
    pass_on(3)

    take(r2a.at[0], x_recv.at[0, 0])
    own_left = total(s1[x, y, :, 0:512], r2a.at[0])
    take(r2b.at[0], x_recv.at[1, 0])
    own_right = total(s1[x, y, :, 512:1024], r2b.at[0])
    take(r3a, x_recv.at[0, 4])
    xs[288:320, 0:512] = total(own_left, r3a).astype(BF16)
    take(r3b, x_recv.at[1, 4])
    xs[288:320, 512:1024] = total(own_right, r3b).astype(BF16)
    def half_of(device):
        return lax.div(device, 8), lax.div(lax.rem(device, 8), 4)

    for peer in others:
        copy_to(shard_best.at[half_of(peer)], crecv.at[me], t_sem.at[0], t_sem.at[1], (z, peer)).start()
    crecv[me] = shard_best[half_of(me)]
    project(288, 32)
    ext_sum, ext_along = negatives(288, 32)

    share = 1.0 / (base_sum + ext_sum + jnp.sum(pos_w, axis=0, keepdims=True))
    slot_share = jnp.sum(owned[:, 0:16] * share, axis=1, keepdims=True)
    dz[32:320] = (raw[...] * slot_share).astype(BF16)
    pos_slope = column(jnp.sum(pos_w, axis=0, keepdims=True) * share - 1.0)
    pos_unit = unit[16:32]
    du = 50.0 * (column(share) * (base_along + ext_along) + pos_slope * pos_unit)
    dz[0:16] = ((du - q_unit * jnp.sum(q_unit * du, axis=1, keepdims=True)) * inv[0:16, 0:1]).astype(BF16)
    pos_logit = jnp.sum(pos_logits, axis=1, keepdims=True)
    dz[16:32] = (pos_slope * (50.0 * q_unit - pos_unit * pos_logit) * inv[16:32, 0:1]).astype(BF16)

    def h_copy(i):
        zz = lax.rem(z + STEPS[i], SIDE)
        return copy_to(hs.at[1 - c, zz], core_in.at[zz], h_send, h_recv.at[i], partner)

    def grow(i):
        zz = lax.rem(z + STEPS[i], SIDE)
        part = dot(xs[:, pl.ds(pl.multiple_of(zz * 256, 256), 256)], dz[...], firsts).reshape(32, 8, 1024)
        part = jnp.concatenate([part[:, :, 0:512], part[:, :, 512:1024]], axis=1).astype(BF16)
        part = part.reshape(4, 4, 2, 16, 512)
        for core in range(2):
            hs[core, zz] = part[:, :, core]
        h_copy(i).start()

    place = (z, x, y)

    def device(axis, to):
        where = [z, x, y]
        where[axis] = to
        return (where[0], at(where[1], where[2], c))

    def first_from(p, to):
        tile, y0, ys, order = PORTIONS[p]
        index = [slice(None), slice(None), pl.ds(y0, ys)]
        if order[0] == 2:
            index[2] = to
        else:
            index[order[0]] = to
        return (*index, slice(None), pl.ds(tile * 128, 128))

    def gather_core(i):
        zz = lax.rem(z + STEPS[i], SIDE)
        h_copy(i).wait_recv()
        parts[zz] = (hs[c, zz].astype(F32) + core_in[zz].astype(F32)).astype(BF16)
        for p in (3, 4, 0, 1, 2):
            tile, y0, ys, order = PORTIONS[p]
            lanes = pl.ds(tile * 128, 128)
            if order[0] == 0:
                moves = [(zz, parts.at[zz, :, pl.ds(y0, ys), :, lanes], in1[p].at[STEPS[i] - 1])] if STEPS[i] else []
            else:
                moves = []
                for k in (2, 1, 3):
                    to = lax.rem(place[order[0]] + k, SIDE)
                    if order[0] == 1:
                        source = parts.at[zz, to, pl.ds(y0, ys), :, lanes]
                    else:
                        source = parts.at[zz, :, to, :, lanes]
                    moves.append((to, source, in1[p].at[k - 1, zz]))
            for to, source, target in moves:
                copy_to(source, target, r_send.at[0, p], r_recv.at[0, p], device(order[0], to)).start()

    grow(0)
    grow(1)
    gather_core(0)
    grow(2)
    gather_core(1)
    grow(3)
    gather_core(2)
    gather_core(3)

    out_v[8:40] = dot(dz[0:32], head[...], LAST)

    take(crecv.at[pl.ds(0, GROUP - 1)], t_sem.at[1])
    lane = iota((16, 128), 1)
    packed[...] = jnp.full((8, 16, 128), 2147483647, jnp.int32)
    mine = lax.rem(me, 8)
    for g in range(4):
        merged = jnp.zeros((16, 128), jnp.int32)
        for s in range(8):
            got = crecv[g * 8 + s]
            key = jnp.concatenate([got, pltpu.roll(got, 64, 1)], axis=0).astype(jnp.int32)
            key = ((key >> 11) << 16) + (key & 2047) + (g * 8 + s) * 2048
            key = pltpu.roll(key, lax.rem((s - mine + 8) * 16, 128), 1)
            merged = jnp.where((lane >> 4) == s, key, merged)
        packed[g] = merged
    best = [packed[:, i, :] for i in range(16)]
    for d in (64, 32, 16):
        best = merge16(best, [pltpu.roll(b, d, 1) for b in best])
    for d in (6, 7):
        best = merge16(best, [pltpu.roll(b, d, 0) for b in best])
    square[...] = jnp.zeros((128, 128), jnp.int32)
    for i in range(16):
        square[i : i + 1, :] = best[i][0:1, :]
    flat = square[...]
    out_v[40:56, 0:128] = jnp.transpose((flat & 65535).astype(F32))[0:16]
    out_v[40:56, 128:256] = jnp.transpose((flat >> 16).astype(F32))[0:16]
    early = pltpu.make_async_copy(out_v.at[pl.ds(8, 48)], out_hbm.at[pl.ds(8, 48)], small_sem.at[0])
    early.start()

    def pick(p, stage, to):
        axis = PORTIONS[p][3][stage]
        return tuple(to if a == axis else slice(None) for a, _ in extents(p, stage))

    for p in (1, 2, 4, 0, 3):
        axis = PORTIONS[p][3][0]
        take(in1[p], r_recv.at[0, p])
        mid[p][...] = total(parts[first_from(p, place[axis])], in1[p]).astype(BF16)
        axis = PORTIONS[p][3][1]
        for k in (2, 1, 3):
            to = lax.rem(place[axis] + k, SIDE)
            copy_to(
                mid[p].at[pick(p, 1, to)], in2[p].at[k - 1], r_send.at[1, p], r_recv.at[1, p], device(axis, to)
            ).start()
    for p in (1, 2, 4, 0, 3):
        axis = PORTIONS[p][3][1]
        take(in2[p], r_recv.at[1, p])
        _, y0, ys, order = PORTIONS[p]
        sums = total(mid[p][pick(p, 1, place[axis])], in2[p]).astype(BF16)
        if TAIL[p] == 3:
            tail[3, y0 : y0 + ys] = sums
        else:
            tail[p] = sums
        if p == 4:
            continue
        q = TAIL[p]
        axis = order[2]
        for k in (2, 1, 3):
            to = lax.rem(place[axis] + k, SIDE)
            copy_to(
                tail.at[q, to], in3.at[q, k - 1], r_send.at[2, q], r_recv.at[2, q], device(axis, to)
            ).start()
    for q in range(4):
        take(in3.at[q], r_recv.at[2, q])
        out = total(tail[q, place[PORTIONS[q][3][2]]], in3.at[q])
        out_v[0:8, q * 128 : (q + 1) * 128] = out[0:8]
        out_v[0:8, 512 + q * 128 : 512 + (q + 1) * 128] = out[8:16]
    late = pltpu.make_async_copy(out_v.at[pl.ds(0, 8)], out_hbm.at[pl.ds(0, 8)], small_sem.at[1])
    late.start()

    take(out_buf.at[pl.ds(0, GROUP - 1)], p_sem.at[0])
    take(bsend.at[pl.ds(0, GROUP - 1)], b_sem.at[0])
    take(crecv.at[pl.ds(0, GROUP - 1)], t_sem.at[0])
    core_copy.wait_send()
    for j in range(SIDE):
        take(r2a.at[j], x_send.at[0, j])
        take(r2b.at[j], x_send.at[1, j])
    take(r3a, x_send.at[0, 4])
    take(r3b, x_send.at[1, 4])
    take(core_in, h_send)
    for p in range(5):
        take(in1[p], r_send.at[0, p])
        take(in2[p], r_send.at[1, p])
    for q in range(4):
        take(in3.at[q], r_send.at[2, q])
    early.wait()
    late.wait()


def whole(codes, pos, neg, bank_codes, bank_emb, query_emb, positive_emb, head):
    anywhere = pl.BlockSpec(memory_space=pl.ANY)
    dma = pltpu.SemaphoreType.DMA
    block = (16, 128)

    def by_portion(stage, lead):
        return [pltpu.VMEM((*lead, *(n for _, n in extents(p, stage)), *block), BF16) for p in range(5)]

    return pl.pallas_call(
        whole_kernel,
        out_shape=jax.ShapeDtypeStruct((56, 1024), F32),
        in_specs=[anywhere] * 8,
        out_specs=anywhere,
        scratch_shapes=[
            pltpu.VMEM((16, 64), jnp.int32),
            pltpu.VMEM((1, 16), jnp.int32),
            pltpu.VMEM((16, 16), jnp.int32),
            pltpu.VMEM((56, 1024), F32),
            pltpu.VMEM((2048, 1024), BF16),
            pltpu.VMEM((2048, 1024), BF16),
            pltpu.VMEM((1024, 1024), BF16),
            pltpu.VMEM((8, 128), F32),
            pltpu.VMEM((288, 128), F32),
            pltpu.VMEM((32, 16, 128), F32),
            pltpu.VMEM((32, 16, 128), F32),
            pltpu.VMEM((32, 16, 512), BF16),
            pltpu.VMEM((32, 16, 512), BF16),
            pltpu.VMEM((16, 32, 1024), BF16),
            pltpu.VMEM((16, 32, 1024), BF16),
            pltpu.VMEM((16, 32, 1024), BF16),
            pltpu.VMEM((4, 4, 32, 1024), BF16),
            pltpu.VMEM((4, 3, 32, 512), BF16),
            pltpu.VMEM((4, 3, 32, 512), BF16),
            pltpu.VMEM((4, 32, 512), BF16),
            pltpu.VMEM((4, 32, 512), BF16),
            pltpu.VMEM((3, 32, 512), BF16),
            pltpu.VMEM((3, 32, 512), BF16),
            pltpu.VMEM((1024, 512), BF16),
            pltpu.VMEM((2048, 512), F32),
            pltpu.VMEM((8, 512), F32),
            pltpu.VMEM((4, 2, 8, 128), F32),
            pltpu.VMEM((32, 8, 128), F32),
            pltpu.VMEM((8, 16, 128), jnp.int32),
            pltpu.VMEM((128, 128), jnp.int32),
            pltpu.VMEM((320, 1024), BF16),
            pltpu.VMEM((320, 1024), BF16),
            pltpu.VMEM((288, 1024), F32),
            pltpu.VMEM((320, 1024), F32),
            pltpu.VMEM((320, 128), F32),
            pltpu.VMEM((320, 1024), BF16),
            pltpu.VMEM((320, 1024), BF16),
            pltpu.VMEM((32, 1024), BF16),
            pltpu.VMEM((48, 1024), BF16),
            pltpu.VMEM((2, 4, 4, 4, 16, 512), BF16),
            pltpu.VMEM((4, 4, 4, 16, 512), BF16),
            pltpu.VMEM((4, 4, 4, 16, 512), BF16),
            by_portion(1, (3,)),
            by_portion(1, ()),
            by_portion(2, (3,)),
            pltpu.VMEM((4, 4, *block), BF16),
            pltpu.VMEM((4, 3, *block), BF16),
            dma((3,)),
            dma((5,)),
            dma((2,)),
            dma((2,)),
            dma((2,)),
            dma((2,)),
            dma((2, 5)),
            dma((2, 5)),
            dma,
            dma((4,)),
            dma((3, 5)),
            dma((3, 5)),
        ],
        compiler_params=pltpu.CompilerParams(
            collective_id=0, has_side_effects=True, vmem_limit_bytes=60 * MIB
        ),
        name="whole",
    )(codes, pos, neg, bank_codes, bank_emb, query_emb, positive_emb, head)


OUT = (((16, 16), jnp.int32), ((16, 16), jnp.int32), ((16, 1024), BF16), ((16, 1024), BF16), ((8, 1024), F32))


def emit_kernel(packed_ref, *refs):
    targets, held, sem = refs[0:5], refs[5:9], refs[9]
    held[0][...] = packed_ref[40:56, 0:16].astype(jnp.int32)
    held[1][...] = packed_ref[40:56, 128:144].astype(jnp.int32)
    held[2][...] = packed_ref[8:24].astype(BF16)
    held[3][...] = packed_ref[24:40].astype(BF16)
    sources = (*held, packed_ref.at[pl.ds(0, 8)])
    copies = [pltpu.make_async_copy(a, b, sem.at[i]) for i, (a, b) in enumerate(zip(sources, targets))]
    for copy in copies:
        copy.start()
    for copy in copies:
        copy.wait()


def emit(packed):
    return pl.pallas_call(
        emit_kernel,
        out_shape=tuple(jax.ShapeDtypeStruct(*o) for o in OUT),
        in_specs=[pl.BlockSpec(memory_space=pltpu.VMEM)],
        out_specs=(pl.BlockSpec(memory_space=pl.ANY),) * 5,
        scratch_shapes=[*(pltpu.VMEM(*o) for o in OUT[:4]), pltpu.SemaphoreType.DMA((5,))],
        name="emit",
    )(packed)


def local(
    query_codes, positive_ids, negative_ids, bank_codes, bank_emb, query_emb, positive_emb, head
):
    return emit(
        whole(query_codes, positive_ids.reshape(1, -1), negative_ids, bank_codes, bank_emb, query_emb, positive_emb, head)
    )


def solution(mesh):
    both = ("dp", "index")
    rows = P(both, None)
    return jax.shard_map(
        local,
        mesh=mesh,
        in_specs=(rows, P(both), rows, P("index", None), P("index", None), rows, rows, P()),
        out_specs=(rows,) * 5,
        check_vma=False,
    )
```
